32 devices in a mesh: seq: 4 (over y, x), table: 8 (over z, core).
Axes of the slice: x: 2, y: 2, z: 4, core: 2. Of those that a mesh axis runs over, the one named last changes fastest.
Arguments:
- events_x: bfloat16 [8, 512, 512], P('table', 'seq'), may hold values from -6 to 6
- proj: bfloat16 [512, 1536], replicated, may hold values from -0.25 to 0.25
- out_grad: bfloat16 [8, 512, 512], P('table', 'seq'), may hold values from -6 to 6
- block_mask: int32 [4, 4], replicated, may hold values 0 or 1
- item_ids: int32 [8, 512], P('table', 'seq'), may hold values from 0 to 4095, as said below
- owner_of: int32 [4096], replicated, may hold values from 0 to 7, as said below
- local_of: int32 [4096], replicated, may hold values from 0 to 511, as said below
- table: bfloat16 [4096, 512], P('table'), may hold values from -3 to 3
- moment: float32 [4096, 512], P('table'), may hold values from -2 to 2
- second: float32 [4096], P('table'), may hold values from 0.05 to 2
Outputs:
- new_table: bfloat16 [4096, 512], P('table')
- new_moment: float32 [4096, 512], P('table')
- new_second: float32 [4096], P('table')
- event_rows: bfloat16 [8, 512, 512], P('table', 'seq')
The draws below stay inside these ranges and needn't reach their ends.
Inputs may be any that keep to these rules, and one draw needn't show every extreme that they name: `item_ids`: among the 128 events of one device (one history, one seq index), at most 32 have items of one owner (owner_of); in every draw, for each seq index, some owner gets exactly 32 from the device of every history. owner_of[r] * 512 + local_of[r] takes every value of 0 to 4095 once over the items r. `local_of`: see owner_of.
All inputs are finite; a program needn't handle non-finite values.
Results may differ from the reference program's by a relative error of at most 0.0075.
Values may be sent and summed in bfloat16 or wider, within the bound.
A program may use at most 64 MiB of HBM per device.

```python
import math
import jax
import jax.numpy as jnp
from jax import lax

D = 512
HEADS = 8
HEAD = 64
TOK_DEV = 128
ROWS = 512
SEQ = 512
BLOCKS = 4
BATCH = 8
ITEMS = 4096
CAP = 32


def slab_layout(key):
    return jax.random.permutation(jax.random.fold_in(key, 11), ITEMS).astype(jnp.int32)


def slab_places(key):
    layout = slab_layout(key)
    return jnp.zeros((ITEMS,), jnp.int32).at[layout].set(jnp.arange(ITEMS, dtype=jnp.int32))


def draw_owner_of(key, part):
    return slab_places(key) // ROWS


def draw_local_of(key, part):
    return slab_places(key) % ROWS


def draw_item_ids(key, part):
    layout = slab_layout(key)
    hottest = jax.random.randint(jax.random.fold_in(key, 5), (BLOCKS,), 0, BATCH).astype(jnp.int32)
    block_hot = jnp.tile(hottest, BATCH)
    block_keys = jax.vmap(lambda number: jax.random.fold_in(jax.random.fold_in(key, 17), number))(jnp.arange(BATCH * BLOCKS))

    def one_block(block_key, hot_owner):
        others = (hot_owner + 1 + jnp.arange((BATCH - 1) * CAP, dtype=jnp.int32) // CAP) % BATCH
        mixed = jax.random.permutation(jax.random.fold_in(block_key, 1), others)[:TOK_DEV - CAP]
        owners = jnp.concatenate([jnp.full((CAP,), hot_owner, jnp.int32), mixed.astype(jnp.int32)])
        owners = jax.random.permutation(jax.random.fold_in(block_key, 2), owners)
        first_pick = jax.random.randint(jax.random.fold_in(block_key, 3), (TOK_DEV,), 0, ROWS)
        second_pick = jax.random.randint(jax.random.fold_in(block_key, 4), (TOK_DEV,), 0, ROWS)
        local_row = first_pick * second_pick // ROWS
        return layout[owners * ROWS + local_row]
    events = jax.vmap(one_block)(block_keys, block_hot)
    return events.reshape(BATCH, SEQ).astype(jnp.int32)


def with_ends(array, rng, low, high):
    extent = array.shape
    index_at = [jax.random.randint(jax.random.fold_in(rng, axis), (), 0, extent[axis]) for axis in range(len(extent))]
    array = array.at[tuple(index_at)].set(low)
    longest = extent.index(max(extent))
    index_at[longest] = (index_at[longest] + 1) % extent[longest]
    return array.at[tuple(index_at)].set(high)


def levels(rng, shape, pieces, smallest, high):
    factor_of, own = 1.0, jax.random.fold_in(rng, 6)
    for dim, parts in pieces:
        steps = jnp.exp(jax.random.uniform(jax.random.fold_in(own, dim), (parts,), jnp.float32, smallest / len(pieces), high / len(pieces)))
        factor_of = factor_of * jnp.repeat(steps, shape[dim] // parts).reshape([-1 if axis == dim else 1 for axis in range(len(shape))])
    return factor_of


def noise(own_key, dims, width, bound, pieces=(), kind=jnp.bfloat16):
    result = jax.random.normal(own_key, dims, jnp.float32) * width
    if len(pieces) > 0:
        result = levels(own_key, dims, pieces, -0.22, 0.18) * result
    return jnp.clip(result, min=-bound, max=bound).astype(kind)


def setup_inputs(seed: int = 0) -> dict:
    key_list = jax.random.split(jax.random.key(seed), 11)
    return {
        "events_x": noise(key_list[0], (BATCH, SEQ, D), 1.0, 6.0, ((0, 8), (1, 4))),
        "proj": noise(key_list[1], (D, 3 * D), D ** -0.5, 0.25),
        "out_grad": noise(key_list[2], (BATCH, SEQ, D), 1.0, 6.0, ((0, 8), (1, 4))),
        "block_mask": with_ends((jax.random.randint(key_list[3], (BLOCKS, BLOCKS), 0, 4) < 3).astype(jnp.int32), jax.random.fold_in(key_list[3], 1), 0, 1),
        "item_ids": draw_item_ids(jax.random.fold_in(key_list[10], 71), 0),
        "owner_of": draw_owner_of(jax.random.fold_in(key_list[10], 71), 0),
        "local_of": draw_local_of(jax.random.fold_in(key_list[10], 71), 0),
        "table": noise(key_list[7], (ITEMS, D), 0.5, 3.0, ((0, 8),)),
        "moment": noise(key_list[8], (ITEMS, D), 0.3, 2.0, ((0, 8),), jnp.float32),
        "second": jnp.clip(jnp.exp(math.log(2.0) - 3.6888794 * jax.random.uniform(key_list[9], (ITEMS,), jnp.float32) ** levels(key_list[9], (ITEMS,), ((0, 8),), -0.2, 0.2)), 0.05, 2.0),
    }


first_decay = 0.9
second_decay = 0.99
step_rate = 0.05
epsilon = 1e-08

def split_heads(matrix):
    return matrix.reshape(SEQ, HEADS, HEAD).transpose(1, 0, 2)

def merge_heads(matrix):
    return matrix.transpose(1, 0, 2).reshape(SEQ, D)

def history_grad(inputs, cotangent, proj, allowed):
    projected = jnp.dot(inputs, proj, preferred_element_type=jnp.float32).astype(jnp.bfloat16)
    query_mat = split_heads(projected[:, :D])
    key_mat = split_heads(projected[:, D:2 * D])
    value_mat = split_heads(projected[:, 2 * D:])
    grad_mat = split_heads(cotangent)
    history_scale = 1.0 / math.sqrt(SEQ)
    temper = 1.0 / math.sqrt(HEAD)

    def per_head(head_parts):
        query_head, key_head, value_head, grad_head = head_parts
        scores = jnp.dot(query_head, key_head.T, preferred_element_type=jnp.float32) * temper
        gates = jax.nn.sigmoid(scores)
        weights = (scores * gates * history_scale * allowed).astype(jnp.bfloat16)
        slopes = gates * (1.0 + scores * (1.0 - gates))
        attn_grad = jnp.dot(grad_head, value_head.T, preferred_element_type=jnp.float32)
        score_grad = (attn_grad * slopes * (history_scale * temper) * allowed).astype(jnp.bfloat16)
        query_grad = jnp.dot(score_grad, key_head, preferred_element_type=jnp.float32)
        key_grad = jnp.dot(score_grad.T, query_head, preferred_element_type=jnp.float32)
        value_grad = jnp.dot(weights.T, grad_head, preferred_element_type=jnp.float32)
        return (query_grad, key_grad, value_grad)
    query_grad, key_grad, value_grad = lax.map(per_head, (query_mat, key_mat, value_mat, grad_mat))
    stacked = jnp.concatenate([merge_heads(query_grad), merge_heads(key_grad), merge_heads(value_grad)], axis=1).astype(jnp.bfloat16)
    return lax.dot_general(stacked, proj, (((1,), (1,)), ((), ())), preferred_element_type=jnp.float32).astype(jnp.bfloat16)

def reference(events_x, proj, out_grad, block_mask, item_ids, owner_of, local_of, table, moment, second):
    block_ids = jnp.arange(BLOCKS)
    visible = (block_mask == 1) | (block_ids[:, None] == block_ids[None, :])
    positions = jnp.arange(SEQ)
    pos_block = positions // TOK_DEV
    allowed = (visible[pos_block][:, pos_block] & (positions[None, :] <= positions[:, None])).astype(jnp.float32)

    def per_history(history_pair):
        return history_grad(history_pair[0], history_pair[1], proj, allowed)
    input_grad = lax.map(per_history, (events_x, out_grad))
    place = (owner_of[item_ids] * ROWS + local_of[item_ids]).astype(jnp.int32).reshape(-1)
    item_grad = jax.ops.segment_sum(input_grad.reshape(-1, D).astype(jnp.float32), place, num_segments=ITEMS)
    new_moment = first_decay * moment + (1.0 - first_decay) * item_grad
    new_second = second_decay * second + (1.0 - second_decay) * lax.optimization_barrier(jnp.mean(item_grad * item_grad, axis=1))
    new_table = (table.astype(jnp.float32) - step_rate * new_moment / (jnp.sqrt(new_second) + epsilon)[:, None]).astype(jnp.bfloat16)
    event_rows = new_table[place].reshape(BATCH, SEQ, D)
    return (new_table, new_moment, new_second, event_rows)
```

```python
import functools
import math

import jax
import jax.numpy as jnp
from jax import lax
from jax.experimental import pallas as pl
from jax.experimental.pallas import tpu as pltpu
from jax.sharding import PartitionSpec as P

HEADS = 8
LANES = 128

first_decay = 0.9
second_decay = 0.99
step_rate = 0.05
epsilon = 1e-08

F32 = jnp.float32
BF16 = jnp.bfloat16
MESH = pl.DeviceIdType.MESH


def iota(shape, axis):
    return lax.broadcasted_iota(jnp.int32, shape, axis)


def dot(a, b):
    return jnp.dot(a, b, preferred_element_type=F32)


def dot_nt(a, b):
    return lax.dot_general(a, b, (((1,), (1,)), ((), ())), preferred_element_type=F32)


def dot_tn(a, b):
    return lax.dot_general(a, b, (((0,), (0,)), ((), ())), preferred_element_type=F32)


def kernel(
    seq_count, owner_count, capacity,
    x_ref, proj_hbm, do_ref, mask_ref, ids_ref, owner_ref, local_ref, table_hbm, moment_hbm, second_ref,
    ntab_hbm, nmom_hbm, nsec_ref, event_ref,
    x_all, do_all, proj_ref, table_ref, moment_ref, ntab_ref, nmom_ref,
    own_ref, other_ref, dq_ref, dk_ref, dv_ref, sendsel_ref,
    idx_send, idx_got, idx_all, send_buf, got, grad_ref, reply_buf, returned,
    load_sem, store_sem, x_send, x_recv, do_send, do_recv, idx_ssem, idx_rsem, idxf_ssem, idxf_rsem,
    row_ssem, row_rsem, fwd_ssem, fwd_rsem, rep_ssem, rep_rsem,
):
    pos = lax.axis_index("seq")
    me = lax.axis_index("table")
    tokens, features = x_ref.shape
    head_size = features // HEADS
    slab_rows = table_ref.shape[0]
    width = owner_count * capacity
    history_scale = 1.0 / math.sqrt(tokens * seq_count)
    temper = 1.0 / math.sqrt(head_size)
    turn = 1 - 2 * (pos % 2)

    def seq_peer(r):
        return lax.rem(pos + turn * r + seq_count, seq_count)

    def table_peer(r):
        return lax.rem(me + r, owner_count)

    def rows_of(owner):
        return pl.ds(pl.multiple_of(owner * capacity, capacity), capacity)

    def to_seq(src, dst, ssem, rsem, peer):
        return pltpu.make_async_remote_copy(
            src_ref=src, dst_ref=dst, send_sem=ssem, recv_sem=rsem,
            device_id=(peer, me), device_id_type=MESH,
        )

    def to_table(src, dst, ssem, rsem, peer):
        return pltpu.make_async_remote_copy(
            src_ref=src, dst_ref=dst, send_sem=ssem, recv_sem=rsem,
            device_id=(pos, peer), device_id_type=MESH,
        )

    def each(first, last, step):
        lax.fori_loop(first, last, lambda r, c: (step(r), c)[1], 0)

    loads = [
        pltpu.make_async_copy(proj_hbm, proj_ref, load_sem.at[0]),
        pltpu.make_async_copy(table_hbm, table_ref, load_sem.at[1]),
        pltpu.make_async_copy(moment_hbm, moment_ref, load_sem.at[2]),
    ]
    for load in loads:
        load.start()

    barrier = pltpu.get_barrier_semaphore()

    def greet_seq(r):
        pl.semaphore_signal(barrier, inc=1, device_id=(seq_peer(r), me), device_id_type=MESH)

    def greet_table(r):
        pl.semaphore_signal(barrier, inc=1, device_id=(pos, table_peer(r)), device_id_type=MESH)

    each(1, seq_count, greet_seq)
    each(1, owner_count, greet_table)
    pl.semaphore_wait(barrier, seq_count + owner_count - 2)

    def x_copy(peer):
        return to_seq(x_ref, x_all.at[pos], x_send.at[peer], x_recv.at[pos], peer)

    def do_copy(peer):
        return to_seq(do_ref, do_all.at[pos], do_send.at[peer], do_recv.at[pos], peer)

    def send_block(r):
        peer = seq_peer(r)
        x_copy(peer).start()

        @pl.when(peer < pos)
        def _():
            do_copy(peer).start()

    each(1, seq_count, send_block)

    eye = iota((LANES, LANES), 0) == iota((LANES, LANES), 1)

    def to_col(row):
        return jnp.sum(jnp.where(eye, row, 0.0), axis=1, keepdims=True)

    def to_row(col):
        return jnp.sum(jnp.where(eye, col, 0.0), axis=0, keepdims=True)

    ids = ids_ref[...]
    high_col = to_col((ids // LANES).astype(F32))
    low_col = to_col((ids % LANES).astype(F32))
    id_rows = owner_ref.shape[0]
    local_ids = local_ref[...]
    parts = jnp.concatenate(
        [
            owner_ref[...].astype(F32).astype(BF16),
            (local_ids % 256).astype(F32).astype(BF16),
            (local_ids // 256).astype(F32).astype(BF16),
        ],
        axis=1,
    )
    pick = jnp.where(iota((tokens, id_rows), 1).astype(F32) == high_col, 1.0, 0.0).astype(BF16)
    found = dot(pick, parts)
    in_row = iota((tokens, LANES), 1).astype(F32) == low_col

    def column(part):
        piece = found[:, part * LANES : (part + 1) * LANES]
        return jnp.sum(jnp.where(in_row, piece, 0.0), axis=1, keepdims=True)

    owner_col = column(0)
    local_col = column(1) + 256.0 * column(2)
    owner_row = to_row(owner_col)
    before = (owner_col == owner_row) & (iota((tokens, tokens), 0) < iota((tokens, tokens), 1))
    slot_row = jnp.sum(jnp.where(before, 1.0, 0.0), axis=0, keepdims=True)
    slot_col = to_col(slot_row)
    target_row = owner_row * capacity + slot_row
    sendsel_ref[...] = jnp.where(
        iota((width, tokens), 0).astype(F32) == target_row, 1.0, 0.0
    ).astype(BF16)
    lane_col = slot_col + (me * capacity).astype(F32)
    marks = jnp.where(iota((tokens, width), 1).astype(F32) == lane_col, local_col + 1.0, 0.0)

    def make_index(owner):
        line = jnp.sum(
            jnp.where(owner_col == owner.astype(F32), marks, 0.0), axis=0, keepdims=True
        )
        idx_send[owner] = jnp.broadcast_to(line, (8, width))

    each(0, owner_count, make_index)

    def idx_copy(peer):
        return to_table(
            idx_send.at[peer], idx_got.at[me], idx_ssem.at[peer], idx_rsem.at[me], peer
        )

    each(1, owner_count, lambda r: idx_copy(table_peer(r)).start())
    idx_got[me] = idx_send[me]

    x_all[pos] = x_ref[...]
    do_all[pos] = do_ref[...]
    loads[0].wait()
    own_ref[...] = dot(x_ref[...], proj_ref[...]).astype(BF16)
    dq_ref[...] = jnp.zeros_like(dq_ref)
    dk_ref[...] = jnp.zeros_like(dk_ref)
    dv_ref[...] = jnp.zeros_like(dv_ref)

    lane = iota((1, LANES), 1)
    group = LANES // head_size
    span = group * tokens
    head_masks = [
        jnp.where(lane // head_size == g, 1.0, 0.0).astype(BF16) for g in range(group)
    ]

    def spread(block):
        return jnp.concatenate([block * m for m in head_masks], axis=0)

    def terms(scores_dot, grad_dot, allowed):
        scores = scores_dot * temper
        gates = 0.5 * jnp.tanh(0.5 * scores) + 0.5
        scaled = gates * allowed
        weights = (scores * scaled).astype(BF16)
        slopes = scaled * (1.0 + scores * (1.0 - gates))
        score_grad = (grad_dot * slopes * temper).astype(BF16)
        return weights, score_grad

    row_ids = iota((tokens, span), 0)
    lane_ids = iota((tokens, span), 1) % tokens

    def visible(query_block, key_block):
        seen = mask_ref[query_block, key_block] == 1
        return jnp.where(seen | (query_block == key_block), history_scale, 0.0)

    def block_step(r):
        block = seq_peer(r)

        @pl.when(r > 0)
        def _():
            to_seq(
                x_all.at[block], x_all.at[block], x_send.at[block], x_recv.at[block], block
            ).wait_recv()

        @pl.when(block <= pos)
        def _():
            @pl.when(block < pos)
            def _():
                other_ref[...] = dot(x_all[block], proj_ref[:, features:]).astype(BF16)

            @pl.when(block == pos)
            def _():
                other_ref[...] = own_ref[:, features:]

            allowed = jnp.where(
                lane_ids <= row_ids + (pos - block) * tokens, visible(pos, block), 0.0
            )
            for c in range(features // LANES):
                cols = slice(c * LANES, (c + 1) * LANES)
                keys = spread(other_ref[:, cols])
                values = spread(other_ref[:, features + c * LANES : features + (c + 1) * LANES])
                _, score_grad = terms(
                    dot_nt(own_ref[:, cols], keys), dot_nt(do_ref[:, cols], values), allowed
                )
                dq_ref[:, cols] += dot(score_grad, keys)

        @pl.when(block >= pos)
        def _():
            @pl.when(block > pos)
            def _():
                to_seq(
                    do_all.at[block], do_all.at[block], do_send.at[block], do_recv.at[block], block
                ).wait_recv()
                other_ref[:, :features] = dot(x_all[block], proj_ref[:, :features]).astype(BF16)

            @pl.when(block == pos)
            def _():
                other_ref[:, :features] = own_ref[:, :features]

            allowed = jnp.where(
                row_ids <= lane_ids + (block - pos) * tokens, visible(block, pos), 0.0
            )
            for c in range(features // LANES):
                cols = slice(c * LANES, (c + 1) * LANES)
                queries = spread(other_ref[:, cols])
                grads = spread(do_all[block, :, cols])
                weights, score_grad = terms(
                    dot_nt(own_ref[:, features + c * LANES : features + (c + 1) * LANES], queries),
                    dot_nt(
                        own_ref[:, 2 * features + c * LANES : 2 * features + (c + 1) * LANES], grads
                    ),
                    allowed,
                )
                dk_ref[:, cols] += dot(score_grad, queries)
                dv_ref[:, cols] += dot(weights, grads)

    each(0, seq_count, block_step)

    def take_index(r):
        peer = table_peer(r)
        to_table(
            idx_got.at[peer], idx_got.at[peer], idx_ssem.at[peer], idx_rsem.at[peer], peer
        ).wait_recv()

    each(1, owner_count, take_index)
    idx_all[pos] = jnp.sum(idx_got[...], axis=0)

    def idxf_copy(peer):
        return to_seq(idx_all.at[pos], idx_all.at[pos], idxf_ssem.at[peer], idxf_rsem.at[pos], peer)

    each(1, seq_count, lambda r: idxf_copy(seq_peer(r)).start())

    stacked = jnp.concatenate(
        [dq_ref[...].astype(BF16), dk_ref[...].astype(BF16), dv_ref[...].astype(BF16)], axis=1
    )
    input_grad = dot_nt(stacked, proj_ref[...]).astype(BF16)
    send_buf[...] = dot(sendsel_ref[...], input_grad).astype(BF16)

    def row_copy(peer):
        return to_table(
            send_buf.at[rows_of(peer)], got.at[pos, rows_of(me)],
            row_ssem.at[peer], row_rsem.at[me], peer,
        )

    each(1, owner_count, lambda r: row_copy(table_peer(r)).start())
    got[pos, rows_of(me)] = send_buf[rows_of(me)]

    def forward(source):
        def one(r):
            peer = seq_peer(r)
            to_seq(
                got.at[pos, rows_of(source)], got.at[pos, rows_of(source)],
                fwd_ssem.at[peer], fwd_rsem.at[pos], peer,
            ).start()

        each(1, seq_count, one)

    forward(me)

    def relay(r):
        source = lax.rem(me - r + owner_count, owner_count)
        part = got.at[pos, rows_of(source)]
        to_table(part, part, row_ssem.at[source], row_rsem.at[source], source).wait_recv()
        forward(source)

    each(1, owner_count, relay)

    slab_ids = iota((slab_rows, width), 0).astype(F32) + 1.0

    def select(block):
        return jnp.where(slab_ids == idx_all[block][0:1, :], 1.0, 0.0).astype(BF16)

    grad_ref[...] = dot(select(pos), got[pos])

    def add_block(r):
        block = seq_peer(r)
        to_seq(
            idx_all.at[block], idx_all.at[block], idxf_ssem.at[block], idxf_rsem.at[block], block
        ).wait_recv()
        to_seq(
            got.at[block], got.at[block], fwd_ssem.at[block], fwd_rsem.at[block], block
        ).wait_recv()
        grad_ref[...] += dot(select(block), got[block])

    each(1, seq_count, add_block)

    loads[1].wait()
    loads[2].wait()
    for c in range(slab_rows // LANES):
        rows = slice(c * LANES, (c + 1) * LANES)
        grad = grad_ref[rows, :]
        new_moment = first_decay * moment_ref[rows, :] + (1.0 - first_decay) * grad
        mean_square = jnp.sum(grad * grad, axis=1, keepdims=True) * (1.0 / features)
        new_second = second_decay * to_col(second_ref[c : c + 1, :]) + (
            1.0 - second_decay
        ) * mean_square
        nsec_ref[c : c + 1, :] = to_row(new_second)
        nmom_ref[rows, :] = new_moment
        factor = step_rate / (jnp.sqrt(new_second) + epsilon)
        ntab_ref[rows, :] = (table_ref[rows, :].astype(F32) - new_moment * factor).astype(BF16)

    reply_buf[...] = dot_tn(select(pos), ntab_ref[...]).astype(BF16)

    def reply_copy(peer):
        return to_table(
            reply_buf.at[rows_of(peer)], returned.at[rows_of(me)],
            rep_ssem.at[peer], rep_rsem.at[me], peer,
        )

    each(1, owner_count, lambda r: reply_copy(table_peer(r)).start())
    stores = [
        pltpu.make_async_copy(nmom_ref, nmom_hbm, store_sem.at[0]),
        pltpu.make_async_copy(ntab_ref, ntab_hbm, store_sem.at[1]),
    ]
    for store in stores:
        store.start()
    returned[rows_of(me)] = reply_buf[rows_of(me)]

    def end_seq(r):
        peer = seq_peer(r)
        x_copy(peer).wait_send()

        @pl.when(peer < pos)
        def _():
            do_copy(peer).wait_send()

        idxf_copy(peer).wait_send()
        to_seq(got.at[pos], got.at[pos], fwd_ssem.at[peer], fwd_rsem.at[pos], peer).wait_send()

    each(1, seq_count, end_seq)

    def end_table(r):
        peer = table_peer(r)
        idx_copy(peer).wait_send()
        row_copy(peer).wait_send()
        part = returned.at[rows_of(peer)]
        to_table(part, part, rep_ssem.at[peer], rep_rsem.at[peer], peer).wait_recv()

    each(1, owner_count, end_table)
    event_ref[...] = dot_tn(sendsel_ref[...], returned[...]).astype(BF16)
    each(1, owner_count, lambda r: reply_copy(table_peer(r)).wait_send())
    for store in stores:
        store.wait()


def body(events_x, proj, out_grad, block_mask, item_ids, owner_of, local_of, table, moment, second):
    tokens, features = events_x.shape[1:]
    seq_count = lax.axis_size("seq")
    owner_count = lax.axis_size("table")
    slab_rows = table.shape[0]
    capacity = max(2 * tokens // owner_count, 16)
    width = owner_count * capacity
    vmem = pl.BlockSpec(memory_space=pltpu.VMEM)
    smem = pl.BlockSpec(memory_space=pltpu.SMEM)
    hbm = pl.BlockSpec(memory_space=pl.ANY)
    dma = pltpu.SemaphoreType.DMA
    new_table, new_moment, new_second, event_rows = pl.pallas_call(
        functools.partial(kernel, seq_count, owner_count, capacity),
        out_shape=(
            jax.ShapeDtypeStruct((slab_rows, features), BF16),
            jax.ShapeDtypeStruct((slab_rows, features), F32),
            jax.ShapeDtypeStruct((slab_rows // LANES, LANES), F32),
            jax.ShapeDtypeStruct((tokens, features), BF16),
        ),
        in_specs=[vmem, hbm, vmem, smem, vmem, vmem, vmem, hbm, hbm, vmem],
        out_specs=(hbm, hbm, vmem, vmem),
        scratch_shapes=[
            pltpu.VMEM((seq_count, tokens, features), BF16),
            pltpu.VMEM((seq_count, tokens, features), BF16),
            pltpu.VMEM(proj.shape, BF16),
            pltpu.VMEM((slab_rows, features), BF16),
            pltpu.VMEM((slab_rows, features), F32),
            pltpu.VMEM((slab_rows, features), BF16),
            pltpu.VMEM((slab_rows, features), F32),
            pltpu.VMEM((tokens, 3 * features), BF16),
            pltpu.VMEM((tokens, 2 * features), BF16),
            pltpu.VMEM((tokens, features), F32),
            pltpu.VMEM((tokens, features), F32),
            pltpu.VMEM((tokens, features), F32),
            pltpu.VMEM((width, tokens), BF16),
            pltpu.VMEM((owner_count, 8, width), F32),
            pltpu.VMEM((owner_count, 8, width), F32),
            pltpu.VMEM((seq_count, 8, width), F32),
            pltpu.VMEM((width, features), BF16),
            pltpu.VMEM((seq_count, width, features), BF16),
            pltpu.VMEM((slab_rows, features), F32),
            pltpu.VMEM((width, features), BF16),
            pltpu.VMEM((width, features), BF16),
            dma((3,)),
            dma((2,)),
            dma((seq_count,)),
            dma((seq_count,)),
            dma((seq_count,)),
            dma((seq_count,)),
            dma((owner_count,)),
            dma((owner_count,)),
            dma((seq_count,)),
            dma((seq_count,)),
            dma((owner_count,)),
            dma((owner_count,)),
            dma((seq_count,)),
            dma((seq_count,)),
            dma((owner_count,)),
            dma((owner_count,)),
        ],
        compiler_params=pltpu.CompilerParams(
            collective_id=0, has_side_effects=True, vmem_limit_bytes=48 * 1024 * 1024
        ),
    )(
        events_x[0],
        proj,
        out_grad[0],
        block_mask,
        item_ids,
        owner_of.reshape(-1, LANES),
        local_of.reshape(-1, LANES),
        table,
        moment,
        second.reshape(-1, LANES),
    )
    return (new_table, new_moment, new_second.reshape(-1), event_rows[None])


def solution(mesh):
    return jax.shard_map(
        body,
        mesh=mesh,
        in_specs=(
            P("table", "seq", None),
            P(),
            P("table", "seq", None),
            P(),
            P("table", "seq"),
            P(),
            P(),
            P("table", None),
            P("table", None),
            P("table"),
        ),
        out_specs=(P("table", None), P("table", None), P("table"), P("table", "seq", None)),
        check_vma=False,
    )
```

```python
import functools
import math

import jax
import jax.numpy as jnp
from jax import lax
from jax.experimental import pallas as pl
from jax.experimental.pallas import tpu as pltpu
from jax.sharding import PartitionSpec as P

HEADS = 8
LANES = 128
VMEM_BYTES = 63 * 1024 * 1024

first_decay = 0.9
second_decay = 0.99
step_rate = 0.05
epsilon = 1e-08

F32 = jnp.float32
BF16 = jnp.bfloat16
MESH = pl.DeviceIdType.MESH


def iota(shape, axis):
    return lax.broadcasted_iota(jnp.int32, shape, axis)


def dot(a, b):
    return jnp.dot(a, b, preferred_element_type=F32)


def dot_nt(a, b):
    return lax.dot_general(a, b, (((1,), (1,)), ((), ())), preferred_element_type=F32)


def dot_tn(a, b):
    return lax.dot_general(a, b, (((0,), (0,)), ((), ())), preferred_element_type=F32)


def kernel(
    seq_count, owner_count, capacity,
    x_hbm, proj_hbm, do_hbm, mask_ref, ids_hbm, owner_hbm, local_hbm, table_hbm, moment_hbm, second_hbm,
    ntab_hbm, nmom_hbm, nsec_hbm, event_hbm,
    x_ref, do_ref, ids_ref, owner_ref, local_ref, second_ref, nsec_ref, event_ref,
    x_all, do_all, proj_ref, table_ref, moment_ref, ntab_ref, nmom_ref,
    own_ref, other_ref, dq_ref, dk_ref, dv_ref, sendsel_ref,
    idx_send, idx_got, idx_all, send_buf, got, grad_ref, reply_buf, returned,
    load_sem, store_sem, x_send, x_recv, do_send, do_recv, idx_ssem, idx_rsem, idxf_ssem, idxf_rsem,
    row_ssem, row_rsem, fwd_ssem, fwd_rsem, rep_ssem, rep_rsem,
):
    pos = lax.axis_index("seq")
    me = lax.axis_index("table")
    tokens, features = x_ref.shape
    head_size = features // HEADS
    slab_rows = table_ref.shape[0]
    width = owner_count * capacity
    history_scale = 1.0 / math.sqrt(tokens * seq_count)
    temper = 1.0 / math.sqrt(head_size)
    turn = 1 - 2 * (pos % 2)

    def seq_peer(r):
        return lax.rem(pos + turn * r + seq_count, seq_count)

    def table_peer(r):
        return lax.rem(me + r, owner_count)

    def rows_of(owner):
        return pl.ds(pl.multiple_of(owner * capacity, capacity), capacity)

    def to_seq(src, dst, ssem, rsem, peer):
        return pltpu.make_async_remote_copy(
            src_ref=src, dst_ref=dst, send_sem=ssem, recv_sem=rsem,
            device_id=(peer, me), device_id_type=MESH,
        )

    def to_table(src, dst, ssem, rsem, peer):
        return pltpu.make_async_remote_copy(
            src_ref=src, dst_ref=dst, send_sem=ssem, recv_sem=rsem,
            device_id=(pos, peer), device_id_type=MESH,
        )

    def each(first, last, step):
        lax.fori_loop(first, last, lambda r, c: (step(r), c)[1], 0)

    loads = [
        pltpu.make_async_copy(source, target, load_sem.at[number])
        for number, (source, target) in enumerate(
            [
                (ids_hbm, ids_ref),
                (owner_hbm, owner_ref),
                (local_hbm, local_ref),
                (x_hbm, x_ref),
                (do_hbm, do_ref),
                (proj_hbm, proj_ref),
                (table_hbm, table_ref),
                (moment_hbm, moment_ref),
                (second_hbm, second_ref),
            ]
        )
    ]
    for load in loads:
        load.start()

    barrier = pltpu.get_barrier_semaphore()

    def greet_seq(r):
        pl.semaphore_signal(barrier, inc=1, device_id=(seq_peer(r), me), device_id_type=MESH)

    def greet_table(r):
        pl.semaphore_signal(barrier, inc=1, device_id=(pos, table_peer(r)), device_id_type=MESH)

    each(1, seq_count, greet_seq)
    each(1, owner_count, greet_table)
    pl.semaphore_wait(barrier, seq_count + owner_count - 2)

    def x_copy(peer):
        return to_seq(x_hbm, x_all.at[pos], x_send.at[peer], x_recv.at[pos], peer)

    def do_copy(peer):
        return to_seq(do_hbm, do_all.at[pos], do_send.at[peer], do_recv.at[pos], peer)

    def send_block(r):
        peer = seq_peer(r)
        x_copy(peer).start()

        @pl.when(peer < pos)
        def _():
            do_copy(peer).start()

    each(1, seq_count, send_block)

    eye = iota((LANES, LANES), 0) == iota((LANES, LANES), 1)

    def to_col(row):
        return jnp.sum(jnp.where(eye, row, 0.0), axis=1, keepdims=True)

    def to_row(col):
        return jnp.sum(jnp.where(eye, col, 0.0), axis=0, keepdims=True)

    for load in loads[:3]:
        load.wait()
    ids = ids_ref[...]
    high_col = to_col((ids // LANES).astype(F32))
    low_col = to_col((ids % LANES).astype(F32))
    id_rows = owner_ref.shape[0]
    local_ids = local_ref[...]
    parts = jnp.concatenate(
        [
            owner_ref[...].astype(F32).astype(BF16),
            (local_ids % 256).astype(F32).astype(BF16),
            (local_ids // 256).astype(F32).astype(BF16),
        ],
        axis=1,
    )
    pick = jnp.where(iota((tokens, id_rows), 1).astype(F32) == high_col, 1.0, 0.0).astype(BF16)
    found = dot(pick, parts)
    in_row = iota((tokens, LANES), 1).astype(F32) == low_col

    def column(part):
        piece = found[:, part * LANES : (part + 1) * LANES]
        return jnp.sum(jnp.where(in_row, piece, 0.0), axis=1, keepdims=True)

    owner_col = column(0)
    local_col = column(1) + 256.0 * column(2)
    owner_row = to_row(owner_col)
    before = (owner_col == owner_row) & (iota((tokens, tokens), 0) < iota((tokens, tokens), 1))
    slot_row = jnp.sum(jnp.where(before, 1.0, 0.0), axis=0, keepdims=True)
    slot_col = to_col(slot_row)
    target_row = owner_row * capacity + slot_row
    sendsel_ref[...] = jnp.where(
        iota((width, tokens), 0).astype(F32) == target_row, 1.0, 0.0
    ).astype(BF16)
    lane_col = slot_col + (me * capacity).astype(F32)
    marks = jnp.where(iota((tokens, width), 1).astype(F32) == lane_col, local_col + 1.0, 0.0)

    def make_index(owner):
        line = jnp.sum(
            jnp.where(owner_col == owner.astype(F32), marks, 0.0), axis=0, keepdims=True
        )
        idx_send[owner] = jnp.broadcast_to(line, (8, width))

    each(0, owner_count, make_index)

    def idx_copy(peer):
        return to_table(
            idx_send.at[peer], idx_got.at[me], idx_ssem.at[peer], idx_rsem.at[me], peer
        )

    each(1, owner_count, lambda r: idx_copy(table_peer(r)).start())
    idx_got[me] = idx_send[me]

    for load in loads[3:6]:
        load.wait()
    x_all[pos] = x_ref[...]
    do_all[pos] = do_ref[...]
    own_ref[...] = dot(x_ref[...], proj_ref[...]).astype(BF16)
    dq_ref[...] = jnp.zeros_like(dq_ref)
    dk_ref[...] = jnp.zeros_like(dk_ref)
    dv_ref[...] = jnp.zeros_like(dv_ref)

    lane = iota((1, LANES), 1)
    group = LANES // head_size
    span = group * tokens
    head_masks = [
        jnp.where(lane // head_size == g, 1.0, 0.0).astype(BF16) for g in range(group)
    ]

    def spread(block):
        return jnp.concatenate([block * m for m in head_masks], axis=0)

    def terms(scores_dot, grad_dot, allowed):
        scores = scores_dot * temper
        gates = 0.5 * jnp.tanh(0.5 * scores) + 0.5
        scaled = gates * allowed
        weights = (scores * scaled).astype(BF16)
        slopes = scaled * (1.0 + scores * (1.0 - gates))
        score_grad = (grad_dot * slopes * temper).astype(BF16)
        return weights, score_grad

    row_ids = iota((tokens, span), 0)
    lane_ids = iota((tokens, span), 1) % tokens

    def visible(query_block, key_block):
        seen = mask_ref[query_block, key_block] == 1
        return jnp.where(seen | (query_block == key_block), history_scale, 0.0)

    def block_step(r):
        block = seq_peer(r)

        @pl.when(r > 0)
        def _():
            to_seq(
                x_all.at[block], x_all.at[block], x_send.at[block], x_recv.at[block], block
            ).wait_recv()

        @pl.when(block <= pos)
        def _():
            @pl.when(block < pos)
            def _():
                other_ref[...] = dot(x_all[block], proj_ref[:, features:]).astype(BF16)

            @pl.when(block == pos)
            def _():
                other_ref[...] = own_ref[:, features:]

            allowed = jnp.where(
                lane_ids <= row_ids + (pos - block) * tokens, visible(pos, block), 0.0
            )
            for c in range(features // LANES):
                cols = slice(c * LANES, (c + 1) * LANES)
                keys = spread(other_ref[:, cols])
                values = spread(other_ref[:, features + c * LANES : features + (c + 1) * LANES])
                _, score_grad = terms(
                    dot_nt(own_ref[:, cols], keys), dot_nt(do_ref[:, cols], values), allowed
                )
                dq_ref[:, cols] += dot(score_grad, keys)

        @pl.when(block >= pos)
        def _():
            @pl.when(block > pos)
            def _():
                to_seq(
                    do_all.at[block], do_all.at[block], do_send.at[block], do_recv.at[block], block
                ).wait_recv()
                other_ref[:, :features] = dot(x_all[block], proj_ref[:, :features]).astype(BF16)

            @pl.when(block == pos)
            def _():
                other_ref[:, :features] = own_ref[:, :features]

            allowed = jnp.where(
                row_ids <= lane_ids + (block - pos) * tokens, visible(block, pos), 0.0
            )
            for c in range(features // LANES):
                cols = slice(c * LANES, (c + 1) * LANES)
                queries = spread(other_ref[:, cols])
                grads = spread(do_all[block, :, cols])
                weights, score_grad = terms(
                    dot_nt(own_ref[:, features + c * LANES : features + (c + 1) * LANES], queries),
                    dot_nt(
                        own_ref[:, 2 * features + c * LANES : 2 * features + (c + 1) * LANES], grads
                    ),
                    allowed,
                )
                dk_ref[:, cols] += dot(score_grad, queries)
                dv_ref[:, cols] += dot(weights, grads)

    each(0, seq_count, block_step)

    def take_index(r):
        peer = table_peer(r)
        to_table(
            idx_got.at[peer], idx_got.at[peer], idx_ssem.at[peer], idx_rsem.at[peer], peer
        ).wait_recv()

    each(1, owner_count, take_index)
    idx_all[pos] = jnp.sum(idx_got[...], axis=0)

    def idxf_copy(peer):
        return to_seq(idx_all.at[pos], idx_all.at[pos], idxf_ssem.at[peer], idxf_rsem.at[pos], peer)

    each(1, seq_count, lambda r: idxf_copy(seq_peer(r)).start())

    stacked = jnp.concatenate(
        [dq_ref[...].astype(BF16), dk_ref[...].astype(BF16), dv_ref[...].astype(BF16)], axis=1
    )
    input_grad = dot_nt(stacked, proj_ref[...]).astype(BF16)
    send_buf[...] = dot(sendsel_ref[...], input_grad).astype(BF16)

    def row_copy(peer):
        return to_table(
            send_buf.at[rows_of(peer)], got.at[pos, rows_of(me)],
            row_ssem.at[peer], row_rsem.at[me], peer,
        )

    each(1, owner_count, lambda r: row_copy(table_peer(r)).start())
    got[pos, rows_of(me)] = send_buf[rows_of(me)]

    def forward(source):
        def one(r):
            peer = seq_peer(r)
            to_seq(
                got.at[pos, rows_of(source)], got.at[pos, rows_of(source)],
                fwd_ssem.at[peer], fwd_rsem.at[pos], peer,
            ).start()

        each(1, seq_count, one)

    forward(me)

    def relay(r):
        source = lax.rem(me - r + owner_count, owner_count)
        part = got.at[pos, rows_of(source)]
        to_table(part, part, row_ssem.at[source], row_rsem.at[source], source).wait_recv()
        forward(source)

    each(1, owner_count, relay)

    slab_ids = iota((slab_rows, width), 0).astype(F32) + 1.0

    def select(block):
        return jnp.where(slab_ids == idx_all[block][0:1, :], 1.0, 0.0).astype(BF16)

    grad_ref[...] = dot(select(pos), got[pos])

    def add_block(r):
        block = seq_peer(r)
        to_seq(
            idx_all.at[block], idx_all.at[block], idxf_ssem.at[block], idxf_rsem.at[block], block
        ).wait_recv()
        to_seq(
            got.at[block], got.at[block], fwd_ssem.at[block], fwd_rsem.at[block], block
        ).wait_recv()
        grad_ref[...] += dot(select(block), got[block])

    each(1, seq_count, add_block)

    for load in loads[6:]:
        load.wait()
    for c in range(slab_rows // LANES):
        rows = slice(c * LANES, (c + 1) * LANES)
        grad = grad_ref[rows, :]
        new_moment = first_decay * moment_ref[rows, :] + (1.0 - first_decay) * grad
        mean_square = jnp.sum(grad * grad, axis=1, keepdims=True) * (1.0 / features)
        new_second = second_decay * to_col(second_ref[c : c + 1, :]) + (
            1.0 - second_decay
        ) * mean_square
        nsec_ref[c : c + 1, :] = to_row(new_second)
        nmom_ref[rows, :] = new_moment
        factor = step_rate / (jnp.sqrt(new_second) + epsilon)
        ntab_ref[rows, :] = (table_ref[rows, :].astype(F32) - new_moment * factor).astype(BF16)

    reply_buf[...] = dot_tn(select(pos), ntab_ref[...]).astype(BF16)

    def reply_copy(peer):
        return to_table(
            reply_buf.at[rows_of(peer)], returned.at[rows_of(me)],
            rep_ssem.at[peer], rep_rsem.at[me], peer,
        )

    each(1, owner_count, lambda r: reply_copy(table_peer(r)).start())
    stores = [
        pltpu.make_async_copy(nmom_ref, nmom_hbm, store_sem.at[0]),
        pltpu.make_async_copy(ntab_ref, ntab_hbm, store_sem.at[1]),
        pltpu.make_async_copy(nsec_ref, nsec_hbm, store_sem.at[2]),
    ]
    for store in stores:
        store.start()
    returned[rows_of(me)] = reply_buf[rows_of(me)]

    def end_seq(r):
        peer = seq_peer(r)
        x_copy(peer).wait_send()

        @pl.when(peer < pos)
        def _():
            do_copy(peer).wait_send()

        idxf_copy(peer).wait_send()
        to_seq(got.at[pos], got.at[pos], fwd_ssem.at[peer], fwd_rsem.at[pos], peer).wait_send()

    each(1, seq_count, end_seq)

    def end_table(r):
        peer = table_peer(r)
        idx_copy(peer).wait_send()
        row_copy(peer).wait_send()
        part = returned.at[rows_of(peer)]
        to_table(part, part, rep_ssem.at[peer], rep_rsem.at[peer], peer).wait_recv()

    each(1, owner_count, end_table)
    event_ref[...] = dot_tn(sendsel_ref[...], returned[...]).astype(BF16)
    last = pltpu.make_async_copy(event_ref, event_hbm, store_sem.at[3])
    last.start()
    each(1, owner_count, lambda r: reply_copy(table_peer(r)).wait_send())
    for store in stores:
        store.wait()
    last.wait()


def pass_on(*refs):
    sems = refs[-1]
    half = len(refs) // 2
    copies = []
    for source, target in zip(refs[:half], refs[half:-1]):
        rows = source.shape[0]
        pieces = rows // LANES if rows > LANES else 1
        size = rows // pieces
        for piece in range(pieces):
            part = pl.ds(piece * size, size)
            copies.append(
                pltpu.make_async_copy(source.at[part], target.at[part], sems.at[len(copies)])
            )
    for copy in copies:
        copy.start()
    for copy in copies:
        copy.wait()


def body(events_x, proj, out_grad, block_mask, item_ids, owner_of, local_of, table, moment, second):
    tokens, features = events_x.shape[1:]
    seq_count = lax.axis_size("seq")
    owner_count = lax.axis_size("table")
    slab_rows = table.shape[0]
    capacity = max(2 * tokens // owner_count, 16)
    width = owner_count * capacity
    smem = pl.BlockSpec(memory_space=pltpu.SMEM)
    hbm = pl.BlockSpec(memory_space=pl.ANY)
    dma = pltpu.SemaphoreType.DMA
    results = pl.pallas_call(
        functools.partial(kernel, seq_count, owner_count, capacity),
        out_shape=(
            jax.ShapeDtypeStruct((slab_rows, features), BF16),
            jax.ShapeDtypeStruct((slab_rows, features), F32),
            jax.ShapeDtypeStruct((slab_rows // LANES, LANES), F32),
            jax.ShapeDtypeStruct((tokens, features), BF16),
        ),
        in_specs=[hbm, hbm, hbm, smem] + [hbm] * 6,
        out_specs=(hbm,) * 4,
        scratch_shapes=[
            pltpu.VMEM((tokens, features), BF16),
            pltpu.VMEM((tokens, features), BF16),
            pltpu.VMEM((1, tokens), jnp.int32),
            pltpu.VMEM((owner_of.shape[0] // LANES, LANES), jnp.int32),
            pltpu.VMEM((owner_of.shape[0] // LANES, LANES), jnp.int32),
            pltpu.VMEM((slab_rows // LANES, LANES), F32),
            pltpu.VMEM((slab_rows // LANES, LANES), F32),
            pltpu.VMEM((tokens, features), BF16),
            pltpu.VMEM((seq_count, tokens, features), BF16),
            pltpu.VMEM((seq_count, tokens, features), BF16),
            pltpu.VMEM(proj.shape, BF16),
            pltpu.VMEM((slab_rows, features), BF16),
            pltpu.VMEM((slab_rows, features), F32),
            pltpu.VMEM((slab_rows, features), BF16),
            pltpu.VMEM((slab_rows, features), F32),
            pltpu.VMEM((tokens, 3 * features), BF16),
            pltpu.VMEM((tokens, 2 * features), BF16),
            pltpu.VMEM((tokens, features), F32),
            pltpu.VMEM((tokens, features), F32),
            pltpu.VMEM((tokens, features), F32),
            pltpu.VMEM((width, tokens), BF16),
            pltpu.VMEM((owner_count, 8, width), F32),
            pltpu.VMEM((owner_count, 8, width), F32),
            pltpu.VMEM((seq_count, 8, width), F32),
            pltpu.VMEM((width, features), BF16),
            pltpu.VMEM((seq_count, width, features), BF16),
            pltpu.VMEM((slab_rows, features), F32),
            pltpu.VMEM((width, features), BF16),
            pltpu.VMEM((width, features), BF16),
            dma((9,)),
            dma((4,)),
            dma((seq_count,)),
            dma((seq_count,)),
            dma((seq_count,)),
            dma((seq_count,)),
            dma((owner_count,)),
            dma((owner_count,)),
            dma((seq_count,)),
            dma((seq_count,)),
            dma((owner_count,)),
            dma((owner_count,)),
            dma((seq_count,)),
            dma((seq_count,)),
            dma((owner_count,)),
            dma((owner_count,)),
        ],
        compiler_params=pltpu.CompilerParams(
            collective_id=0, has_side_effects=True, vmem_limit_bytes=VMEM_BYTES
        ),
    )(
        events_x[0],
        proj,
        out_grad[0],
        block_mask,
        item_ids,
        owner_of.reshape(-1, LANES),
        local_of.reshape(-1, LANES),
        table,
        moment,
        second.reshape(-1, LANES),
    )
    new_table, new_moment, new_second, event_rows = pl.pallas_call(
        pass_on,
        out_shape=tuple(jax.ShapeDtypeStruct(r.shape, r.dtype) for r in results),
        in_specs=[hbm] * 4,
        out_specs=(hbm,) * 4,
        scratch_shapes=[dma((2 * (slab_rows // LANES) + 2,))],
        compiler_params=pltpu.CompilerParams(vmem_limit_bytes=VMEM_BYTES),
    )(*results)
    return (new_table, new_moment, new_second.reshape(-1), event_rows[None])


def solution(mesh):
    return jax.shard_map(
        body,
        mesh=mesh,
        in_specs=(
            P("table", "seq", None),
            P(),
            P("table", "seq", None),
            P(),
            P("table", "seq"),
            P(),
            P(),
            P("table", None),
            P("table", None),
            P("table"),
        ),
        out_specs=(P("table", None), P("table", None), P("table"), P("table", "seq", None)),
        check_vma=False,
    )
```

```python
import functools
import math

import jax
import jax.numpy as jnp
from jax import lax
from jax.experimental import pallas as pl
from jax.experimental.pallas import tpu as pltpu
from jax.sharding import PartitionSpec as P

HEADS = 8
LANES = 128
VMEM_BYTES = 63 * 1024 * 1024

first_decay = 0.9
second_decay = 0.99
step_rate = 0.05
epsilon = 1e-08

F32 = jnp.float32
BF16 = jnp.bfloat16
MESH = pl.DeviceIdType.MESH


def iota(shape, axis):
    return lax.broadcasted_iota(jnp.int32, shape, axis)


def dot(a, b):
    return jnp.dot(a, b, preferred_element_type=F32)


def dot_nt(a, b):
    return lax.dot_general(a, b, (((1,), (1,)), ((), ())), preferred_element_type=F32)


def dot_tn(a, b):
    return lax.dot_general(a, b, (((0,), (0,)), ((), ())), preferred_element_type=F32)


def kernel(
    seq_count, owner_count, capacity,
    x_hbm, proj_hbm, do_hbm, mask_ref, ids_hbm, owner_hbm, local_hbm, table_hbm, moment_hbm, second_hbm,
    ntab_hbm, nmom_hbm, nsec_hbm, event_hbm,
    x_ref, do_ref, ids_ref, owner_ref, local_ref, second_ref, nsec_ref, event_ref,
    x_all, do_all, proj_ref, table_ref, moment_ref, ntab_ref, nmom_ref,
    own_ref, other_ref, dq_ref, dk_ref, dv_ref, sendsel_ref,
    idx_send, idx_got, idx_all, send_buf, got, grad_ref, reply_buf, returned,
    load_sem, store_sem, x_send, x_recv, do_send, do_recv, idx_ssem, idx_rsem, idxf_ssem, idxf_rsem,
    row_ssem, row_rsem, fwd_ssem, fwd_rsem, rep_ssem, rep_rsem, rel_ssem, xr_send, dor_send,
):
    pos = lax.axis_index("seq")
    me = lax.axis_index("table")
    tokens, features = x_ref.shape
    head_size = features // HEADS
    slab_rows = table_ref.shape[0]
    width = owner_count * capacity
    history_scale = 1.0 / math.sqrt(tokens * seq_count)
    temper = 1.0 / math.sqrt(head_size)
    turn = 1 - 2 * (pos % 2)
    side = math.isqrt(seq_count)
    my_row, my_col = pos // side, pos % side

    def row_peer(i):
        return my_row * side + lax.rem(my_col + i, side)

    def col_peer(i):
        return lax.rem(my_row + i, side) * side + my_col

    def seq_peer(r):
        return lax.rem(pos + turn * r + seq_count, seq_count)

    def table_peer(r):
        peer, bit = 0, 1
        while bit < owner_count:
            mine, other = (me // bit) % 2, (r // bit) % 2
            peer = peer + bit * (mine + other - 2 * mine * other)
            bit *= 2
        return peer

    def rows_of(owner):
        return pl.ds(pl.multiple_of(owner * capacity, capacity), capacity)

    def to_seq(src, dst, ssem, rsem, peer):
        return pltpu.make_async_remote_copy(
            src_ref=src, dst_ref=dst, send_sem=ssem, recv_sem=rsem,
            device_id=(peer, me), device_id_type=MESH,
        )

    def to_table(src, dst, ssem, rsem, peer):
        return pltpu.make_async_remote_copy(
            src_ref=src, dst_ref=dst, send_sem=ssem, recv_sem=rsem,
            device_id=(pos, peer), device_id_type=MESH,
        )

    def each(first, last, step):
        lax.fori_loop(first, last, lambda r, c: (step(r), c)[1], 0)

    loads = [
        pltpu.make_async_copy(source, target, load_sem.at[number])
        for number, (source, target) in enumerate(
            [
                (ids_hbm, ids_ref),
                (owner_hbm, owner_ref),
                (local_hbm, local_ref),
                (x_hbm, x_ref),
                (do_hbm, do_ref),
                (proj_hbm, proj_ref),
                (table_hbm, table_ref),
                (moment_hbm, moment_ref),
                (second_hbm, second_ref),
            ]
        )
    ]
    for load in loads:
        load.start()

    barrier = pltpu.get_barrier_semaphore()

    def greet_seq(r):
        pl.semaphore_signal(barrier, inc=1, device_id=(seq_peer(r), me), device_id_type=MESH)

    def greet_table(r):
        pl.semaphore_signal(barrier, inc=1, device_id=(pos, table_peer(r)), device_id_type=MESH)

    each(1, seq_count, greet_seq)
    each(1, owner_count, greet_table)
    pl.semaphore_wait(barrier, seq_count + owner_count - 2)

    def x_copy(peer):
        return to_seq(x_ref, x_all.at[pos], x_send.at[peer], x_recv.at[pos], peer)

    def do_copy(peer):
        return to_seq(do_ref, do_all.at[pos], do_send.at[peer], do_recv.at[pos], peer)

    for load in loads[3:5]:
        load.wait()

    def send_x(i):
        x_copy(row_peer(i)).start()
        x_copy(col_peer(i)).start()

    def each_do(act):
        def one(i):
            for peer in (row_peer(i), col_peer(i)):
                @pl.when(peer < pos)
                def _():
                    act(do_copy(peer))

        each(1, side, one)

    each(1, side, send_x)
    each_do(lambda copy: copy.start())

    def x_relay(block, peer):
        return to_seq(
            x_all.at[block], x_all.at[block], xr_send.at[block], x_recv.at[block], peer
        )

    def do_relay(block, peer):
        return to_seq(
            do_all.at[block], do_all.at[block], dor_send.at[block], do_recv.at[block], peer
        )

    def relay_x(i):
        for block, to_peer, first in ((row_peer(i), col_peer, 0), (col_peer(i), row_peer, 1)):
            x_relay(block, block).wait_recv()

            @pl.when((block // side + block % side) % 2 == first)
            def _():
                each(1, side, lambda k: x_relay(block, to_peer(k)).start())

    def relay_do(i):
        block = col_peer(i)

        @pl.when(block > pos)
        def _():
            do_relay(block, block).wait_recv()
            each(1, side, lambda k: do_relay(block, row_peer(k)).start())

    def end_relays(i):
        for block, to_peer, first in ((row_peer(i), col_peer, 0), (col_peer(i), row_peer, 1)):
            @pl.when((block // side + block % side) % 2 == first)
            def _():
                each(1, side, lambda k: x_relay(block, to_peer(k)).wait_send())

        below = col_peer(i)

        @pl.when(below > pos)
        def _():
            each(1, side, lambda k: do_relay(below, row_peer(k)).wait_send())

    eye = iota((LANES, LANES), 0) == iota((LANES, LANES), 1)

    def to_col(row):
        return jnp.sum(jnp.where(eye, row, 0.0), axis=1, keepdims=True)

    def to_row(col):
        return jnp.sum(jnp.where(eye, col, 0.0), axis=0, keepdims=True)

    for load in loads[:3]:
        load.wait()
    ids = ids_ref[...]
    high_col = to_col((ids // LANES).astype(F32))
    low_col = to_col((ids % LANES).astype(F32))
    id_rows = owner_ref.shape[0]
    local_ids = local_ref[...]
    parts = jnp.concatenate(
        [
            owner_ref[...].astype(F32).astype(BF16),
            (local_ids % 256).astype(F32).astype(BF16),
            (local_ids // 256).astype(F32).astype(BF16),
        ],
        axis=1,
    )
    pick = jnp.where(iota((tokens, id_rows), 1).astype(F32) == high_col, 1.0, 0.0).astype(BF16)
    found = dot(pick, parts)
    in_row = iota((tokens, LANES), 1).astype(F32) == low_col

    def column(part):
        piece = found[:, part * LANES : (part + 1) * LANES]
        return jnp.sum(jnp.where(in_row, piece, 0.0), axis=1, keepdims=True)

    owner_col = column(0)
    local_col = column(1) + 256.0 * column(2)
    owner_row = to_row(owner_col)
    before = (owner_col == owner_row) & (iota((tokens, tokens), 0) < iota((tokens, tokens), 1))
    slot_row = jnp.sum(jnp.where(before, 1.0, 0.0), axis=0, keepdims=True)
    slot_col = to_col(slot_row)
    target_row = owner_row * capacity + slot_row
    sendsel_ref[...] = jnp.where(
        iota((width, tokens), 0).astype(F32) == target_row, 1.0, 0.0
    ).astype(BF16)
    lane_col = slot_col + (me * capacity).astype(F32)
    marks = jnp.where(iota((tokens, width), 1).astype(F32) == lane_col, local_col + 1.0, 0.0)

    def make_index(owner):
        line = jnp.sum(
            jnp.where(owner_col == owner.astype(F32), marks, 0.0), axis=0, keepdims=True
        )
        idx_send[owner] = jnp.broadcast_to(line, (8, width))

    each(0, owner_count, make_index)

    def idx_copy(peer):
        return to_table(
            idx_send.at[peer], idx_got.at[me], idx_ssem.at[peer], idx_rsem.at[me], peer
        )

    each(1, owner_count, lambda r: idx_copy(table_peer(r)).start())
    idx_got[me] = idx_send[me]

    for load in loads[5:6]:
        load.wait()
    x_all[pos] = x_ref[...]
    do_all[pos] = do_ref[...]
    own_ref[...] = dot(x_ref[...], proj_ref[...]).astype(BF16)
    dq_ref[...] = jnp.zeros_like(dq_ref)
    dk_ref[...] = jnp.zeros_like(dk_ref)
    dv_ref[...] = jnp.zeros_like(dv_ref)

    lane = iota((1, LANES), 1)
    group = LANES // head_size
    span = group * tokens
    head_masks = [
        jnp.where(lane // head_size == g, 1.0, 0.0).astype(BF16) for g in range(group)
    ]

    def spread(block):
        return jnp.concatenate([block * m for m in head_masks], axis=0)

    def terms(scores_dot, grad_dot, allowed):
        scores = scores_dot * temper
        gates = 0.5 * jnp.tanh(0.5 * scores) + 0.5
        scaled = gates * allowed
        weights = (scores * scaled).astype(BF16)
        slopes = scaled * (1.0 + scores * (1.0 - gates))
        score_grad = (grad_dot * slopes * temper).astype(BF16)
        return weights, score_grad

    row_ids = iota((tokens, span), 0)
    lane_ids = iota((tokens, span), 1) % tokens

    def visible(query_block, key_block):
        seen = mask_ref[query_block, key_block] == 1
        return jnp.where(seen | (query_block == key_block), history_scale, 0.0)

    def block_step(r):
        block = seq_peer(r)

        in_row, in_col = block // side == my_row, block % side == my_col

        @pl.when(jnp.logical_not(in_row | in_col))
        def _():
            x_relay(block, block).wait_recv()

        @pl.when(block <= pos)
        def _():
            @pl.when(block < pos)
            def _():
                other_ref[...] = dot(x_all[block], proj_ref[:, features:]).astype(BF16)

            @pl.when(block == pos)
            def _():
                other_ref[...] = own_ref[:, features:]

            allowed = jnp.where(
                lane_ids <= row_ids + (pos - block) * tokens, visible(pos, block), 0.0
            )
            for c in range(features // LANES):
                cols = slice(c * LANES, (c + 1) * LANES)
                keys = spread(other_ref[:, cols])
                values = spread(other_ref[:, features + c * LANES : features + (c + 1) * LANES])
                _, score_grad = terms(
                    dot_nt(own_ref[:, cols], keys), dot_nt(do_ref[:, cols], values), allowed
                )
                dq_ref[:, cols] += dot(score_grad, keys)

        @pl.when(block >= pos)
        def _():
            @pl.when(block > pos)
            def _():
                @pl.when(jnp.logical_not(in_col))
                def _():
                    do_relay(block, block).wait_recv()

                other_ref[:, :features] = dot(x_all[block], proj_ref[:, :features]).astype(BF16)

            @pl.when(block == pos)
            def _():
                other_ref[:, :features] = own_ref[:, :features]

            allowed = jnp.where(
                row_ids <= lane_ids + (block - pos) * tokens, visible(block, pos), 0.0
            )
            for c in range(features // LANES):
                cols = slice(c * LANES, (c + 1) * LANES)
                queries = spread(other_ref[:, cols])
                grads = spread(do_all[block, :, cols])
                weights, score_grad = terms(
                    dot_nt(own_ref[:, features + c * LANES : features + (c + 1) * LANES], queries),
                    dot_nt(
                        own_ref[:, 2 * features + c * LANES : 2 * features + (c + 1) * LANES], grads
                    ),
                    allowed,
                )
                dk_ref[:, cols] += dot(score_grad, queries)
                dv_ref[:, cols] += dot(weights, grads)

    block_step(0)
    each(1, side, relay_x)
    each(1, side, relay_do)
    each(1, seq_count, block_step)

    def take_index(r):
        peer = table_peer(r)
        to_table(
            idx_got.at[peer], idx_got.at[peer], idx_ssem.at[peer], idx_rsem.at[peer], peer
        ).wait_recv()

    each(1, owner_count, take_index)
    idx_all[pos] = jnp.sum(idx_got[...], axis=0)

    def idxf_copy(peer):
        return to_seq(idx_all.at[pos], idx_all.at[pos], idxf_ssem.at[peer], idxf_rsem.at[pos], peer)

    each(1, seq_count, lambda r: idxf_copy(seq_peer(r)).start())

    stacked = jnp.concatenate(
        [dq_ref[...].astype(BF16), dk_ref[...].astype(BF16), dv_ref[...].astype(BF16)], axis=1
    )
    input_grad = dot_nt(stacked, proj_ref[...]).astype(BF16)
    send_buf[...] = dot(sendsel_ref[...], input_grad).astype(BF16)

    def row_copy(peer):
        return to_table(
            send_buf.at[rows_of(peer)], got.at[pos, rows_of(me)],
            row_ssem.at[peer], row_rsem.at[me], peer,
        )

    each(1, owner_count, lambda r: row_copy(table_peer(owner_count - r)).start())
    got[pos, rows_of(me)] = send_buf[rows_of(me)]

    def chunk(block, source, ssem, peer):
        part = got.at[block, rows_of(source)]
        return to_seq(part, part, ssem, fwd_rsem.at[block, source], peer)

    def forward(source):
        def one(i):
            chunk(pos, source, fwd_ssem.at[row_peer(i)], row_peer(i)).start()
            chunk(pos, source, fwd_ssem.at[col_peer(i)], col_peer(i)).start()

        each(1, side, one)

    def pass_chunk(source):
        def along(from_peer, to_peer):
            def one(i):
                block = from_peer(i)
                chunk(block, source, rel_ssem.at[block], block).wait_recv()
                each(
                    1, side,
                    lambda k: chunk(block, source, rel_ssem.at[block], to_peer(k)).start(),
                )

            each(1, side, one)

        @pl.when(source % 2 == 0)
        def _():
            along(row_peer, col_peer)

        @pl.when(source % 2 == 1)
        def _():
            along(col_peer, row_peer)

    forward(me)

    def relay(r):
        source = table_peer(r)
        part = got.at[pos, rows_of(source)]
        to_table(part, part, row_ssem.at[source], row_rsem.at[source], source).wait_recv()
        forward(source)
        pass_chunk(table_peer(r - 1))

    each(1, owner_count, relay)
    pass_chunk(table_peer(owner_count - 1))

    slab_ids = iota((slab_rows, width), 0).astype(F32) + 1.0

    def select(block):
        return jnp.where(slab_ids == idx_all[block][0:1, :], 1.0, 0.0).astype(BF16)

    grad_ref[...] = dot(select(pos), got[pos])

    def add_block(r):
        block = seq_peer(r)
        to_seq(
            idx_all.at[block], idx_all.at[block], idxf_ssem.at[block], idxf_rsem.at[block], block
        ).wait_recv()
        in_row, in_col = block // side == my_row, block % side == my_col

        def await_pair(half):
            for odd, seen in ((0, in_row), (1, in_col)):
                @pl.when(jnp.logical_not(seen))
                def _():
                    chunk(block, 2 * half + odd, rel_ssem.at[block], block).wait_recv()

        each(0, owner_count // 2, await_pair)
        grad_ref[...] += dot(select(block), got[block])

    each(1, seq_count, add_block)

    for load in loads[6:]:
        load.wait()
    for c in range(slab_rows // LANES):
        rows = slice(c * LANES, (c + 1) * LANES)
        grad = grad_ref[rows, :]
        new_moment = first_decay * moment_ref[rows, :] + (1.0 - first_decay) * grad
        mean_square = jnp.sum(grad * grad, axis=1, keepdims=True) * (1.0 / features)
        new_second = second_decay * to_col(second_ref[c : c + 1, :]) + (
            1.0 - second_decay
        ) * mean_square
        nsec_ref[c : c + 1, :] = to_row(new_second)
        nmom_ref[rows, :] = new_moment
        factor = step_rate / (jnp.sqrt(new_second) + epsilon)
        ntab_ref[rows, :] = (table_ref[rows, :].astype(F32) - new_moment * factor).astype(BF16)

    reply_buf[...] = dot_tn(select(pos), ntab_ref[...]).astype(BF16)

    def reply_copy(peer):
        return to_table(
            reply_buf.at[rows_of(peer)], returned.at[rows_of(me)],
            rep_ssem.at[peer], rep_rsem.at[me], peer,
        )

    each(1, owner_count, lambda r: reply_copy(table_peer(r)).start())
    stores = [
        pltpu.make_async_copy(nmom_ref, nmom_hbm, store_sem.at[0]),
        pltpu.make_async_copy(ntab_ref, ntab_hbm, store_sem.at[1]),
        pltpu.make_async_copy(nsec_ref, nsec_hbm, store_sem.at[2]),
    ]
    for store in stores:
        store.start()
    returned[rows_of(me)] = reply_buf[rows_of(me)]

    each(1, seq_count, lambda r: idxf_copy(seq_peer(r)).wait_send())
    each_do(lambda copy: copy.wait_send())

    def end_seq(i):
        for peer in (row_peer(i), col_peer(i)):
            x_copy(peer).wait_send()
            to_seq(
                got.at[pos], got.at[pos], fwd_ssem.at[peer], fwd_rsem.at[pos, 0], peer
            ).wait_send()
            half = got.at[peer, pl.ds(0, width // 2)]
            for _ in range(side - 1):
                to_seq(
                    half, half, rel_ssem.at[peer], fwd_rsem.at[peer, 0], peer
                ).wait_send()

    each(1, side, end_seq)
    each(1, side, end_relays)

    def end_table(r):
        peer = table_peer(r)
        idx_copy(peer).wait_send()
        row_copy(peer).wait_send()
        part = returned.at[rows_of(peer)]
        to_table(part, part, rep_ssem.at[peer], rep_rsem.at[peer], peer).wait_recv()

    each(1, owner_count, end_table)
    event_ref[...] = dot_tn(sendsel_ref[...], returned[...]).astype(BF16)
    last = pltpu.make_async_copy(event_ref, event_hbm, store_sem.at[3])
    last.start()
    each(1, owner_count, lambda r: reply_copy(table_peer(r)).wait_send())
    for store in stores:
        store.wait()
    last.wait()


def pass_on(*refs):
    count = len(refs) // 3
    sources, targets, held = refs[:count], refs[count : 2 * count], refs[2 * count : 3 * count]
    in_sem, out_sem = refs[3 * count :]
    loads, stores = [], []
    for source, target, stage in zip(sources, targets, held):
        rows = source.shape[0]
        pieces = rows // LANES if rows > LANES else 1
        size = rows // pieces
        for piece in range(pieces):
            part = pl.ds(piece * size, size)
            number = len(loads)
            loads.append(
                pltpu.make_async_copy(source.at[part], stage.at[part], in_sem.at[number])
            )
            stores.append(
                pltpu.make_async_copy(stage.at[part], target.at[part], out_sem.at[number])
            )
    for load in loads:
        load.start()
    for load, store in zip(loads, stores):
        load.wait()
        store.start()
    for store in stores:
        store.wait()


def body(events_x, proj, out_grad, block_mask, item_ids, owner_of, local_of, table, moment, second):
    tokens, features = events_x.shape[1:]
    seq_count = lax.axis_size("seq")
    owner_count = lax.axis_size("table")
    slab_rows = table.shape[0]
    capacity = max(2 * tokens // owner_count, 16)
    width = owner_count * capacity
    smem = pl.BlockSpec(memory_space=pltpu.SMEM)
    hbm = pl.BlockSpec(memory_space=pl.ANY)
    dma = pltpu.SemaphoreType.DMA
    results = pl.pallas_call(
        functools.partial(kernel, seq_count, owner_count, capacity),
        out_shape=(
            jax.ShapeDtypeStruct((slab_rows, features), BF16),
            jax.ShapeDtypeStruct((slab_rows, features), F32),
            jax.ShapeDtypeStruct((slab_rows // LANES, LANES), F32),
            jax.ShapeDtypeStruct((tokens, features), BF16),
        ),
        in_specs=[hbm, hbm, hbm, smem] + [hbm] * 6,
        out_specs=(hbm,) * 4,
        scratch_shapes=[
            pltpu.VMEM((tokens, features), BF16),
            pltpu.VMEM((tokens, features), BF16),
            pltpu.VMEM((1, tokens), jnp.int32),
            pltpu.VMEM((owner_of.shape[0] // LANES, LANES), jnp.int32),
            pltpu.VMEM((owner_of.shape[0] // LANES, LANES), jnp.int32),
            pltpu.VMEM((slab_rows // LANES, LANES), F32),
            pltpu.VMEM((slab_rows // LANES, LANES), F32),
            pltpu.VMEM((tokens, features), BF16),
            pltpu.VMEM((seq_count, tokens, features), BF16),
            pltpu.VMEM((seq_count, tokens, features), BF16),
            pltpu.VMEM(proj.shape, BF16),
            pltpu.VMEM((slab_rows, features), BF16),
            pltpu.VMEM((slab_rows, features), F32),
            pltpu.VMEM((slab_rows, features), BF16),
            pltpu.VMEM((slab_rows, features), F32),
            pltpu.VMEM((tokens, 3 * features), BF16),
            pltpu.VMEM((tokens, 2 * features), BF16),
            pltpu.VMEM((tokens, features), F32),
            pltpu.VMEM((tokens, features), F32),
            pltpu.VMEM((tokens, features), F32),
            pltpu.VMEM((width, tokens), BF16),
            pltpu.VMEM((owner_count, 8, width), F32),
            pltpu.VMEM((owner_count, 8, width), F32),
            pltpu.VMEM((seq_count, 8, width), F32),
            pltpu.VMEM((width, features), BF16),
            pltpu.VMEM((seq_count, width, features), BF16),
            pltpu.VMEM((slab_rows, features), F32),
            pltpu.VMEM((width, features), BF16),
            pltpu.VMEM((width, features), BF16),
            dma((9,)),
            dma((4,)),
            dma((seq_count,)),
            dma((seq_count,)),
            dma((seq_count,)),
            dma((seq_count,)),
            dma((owner_count,)),
            dma((owner_count,)),
            dma((seq_count,)),
            dma((seq_count,)),
            dma((owner_count,)),
            dma((owner_count,)),
            dma((seq_count,)),
            dma((seq_count, owner_count)),
            dma((owner_count,)),
            dma((owner_count,)),
            dma((seq_count,)),
            dma((seq_count,)),
            dma((seq_count,)),
        ],
        compiler_params=pltpu.CompilerParams(
            collective_id=0, has_side_effects=True, vmem_limit_bytes=VMEM_BYTES
        ),
    )(
        events_x[0],
        proj,
        out_grad[0],
        block_mask,
        item_ids,
        owner_of.reshape(-1, LANES),
        local_of.reshape(-1, LANES),
        table,
        moment,
        second.reshape(-1, LANES),
    )
    new_table, new_moment, new_second, event_rows = pl.pallas_call(
        pass_on,
        out_shape=tuple(jax.ShapeDtypeStruct(r.shape, r.dtype) for r in results),
        in_specs=[hbm] * 4,
        out_specs=(hbm,) * 4,
        scratch_shapes=[pltpu.VMEM(r.shape, r.dtype) for r in results]
        + [dma((2 * (slab_rows // LANES) + 2,))] * 2,
        compiler_params=pltpu.CompilerParams(vmem_limit_bytes=VMEM_BYTES),
    )(*results)
    return (new_table, new_moment, new_second.reshape(-1), event_rows[None])


def solution(mesh):
    return jax.shard_map(
        body,
        mesh=mesh,
        in_specs=(
            P("table", "seq", None),
            P(),
            P("table", "seq", None),
            P(),
            P("table", "seq"),
            P(),
            P(),
            P("table", None),
            P("table", None),
            P("table"),
        ),
        out_specs=(P("table", None), P("table", None), P("table"), P("table", "seq", None)),
        check_vma=False,
    )
```

```python
import functools
import math

import jax
import jax.numpy as jnp
from jax import lax
from jax.experimental import pallas as pl
from jax.experimental.pallas import tpu as pltpu
from jax.sharding import PartitionSpec as P

HEADS = 8
LANES = 128
VMEM_BYTES = 63 * 1024 * 1024

first_decay = 0.9
second_decay = 0.99
step_rate = 0.05
epsilon = 1e-08

F32 = jnp.float32
BF16 = jnp.bfloat16
MESH = pl.DeviceIdType.MESH


def iota(shape, axis):
    return lax.broadcasted_iota(jnp.int32, shape, axis)


def dot(a, b):
    return jnp.dot(a, b, preferred_element_type=F32)


def dot_nt(a, b):
    return lax.dot_general(a, b, (((1,), (1,)), ((), ())), preferred_element_type=F32)


def kernel(
    seq_count, owner_count, capacity,
    x_hbm, proj_hbm, do_hbm, mask_ref, ids_hbm, owner_hbm, local_hbm, table_hbm, moment_hbm, second_hbm,
    ntab_hbm, nmom_hbm, nsec_hbm, recvsel_hbm, returned,
    x_ref, do_ref, ids_ref, owner_ref, local_ref, second_ref, nsec_ref, recvsel_ref, select_ref, replysel_ref,
    x_all, do_all, proj_ref, table_ref, moment_ref, ntab_ref, nmom_ref,
    own_ref, other_ref, dq_ref, dk_ref, dv_ref, sendsel_ref,
    idx_send, idx_got, idx_all, send_buf, got, grad_ref, reply_buf,
    load_sem, store_sem, x_send, x_recv, do_send, do_recv, idx_ssem, idx_rsem, idxf_ssem, idxf_rsem,
    row_ssem, row_rsem, fwd_ssem, fwd_rsem, rep_ssem, rep_rsem, rel_ssem, xr_send, dor_send,
):
    pos = lax.axis_index("seq")
    me = lax.axis_index("table")
    tokens, features = x_ref.shape
    head_size = features // HEADS
    slab_rows = table_ref.shape[0]
    width = owner_count * capacity
    history_scale = 1.0 / math.sqrt(tokens * seq_count)
    temper = 1.0 / math.sqrt(head_size)
    turn = 1 - 2 * (pos % 2)
    side = math.isqrt(seq_count)
    my_row, my_col = pos // side, pos % side

    def row_peer(i):
        return my_row * side + lax.rem(my_col + i, side)

    def col_peer(i):
        return lax.rem(my_row + i, side) * side + my_col

    def seq_peer(r):
        return lax.rem(pos + turn * r + seq_count, seq_count)

    def table_peer(r):
        peer, bit = 0, 1
        while bit < owner_count:
            mine, other = (me // bit) % 2, (r // bit) % 2
            peer = peer + bit * (mine + other - 2 * mine * other)
            bit *= 2
        return peer

    def rows_of(owner):
        return pl.ds(pl.multiple_of(owner * capacity, capacity), capacity)

    def to_seq(src, dst, ssem, rsem, peer):
        return pltpu.make_async_remote_copy(
            src_ref=src, dst_ref=dst, send_sem=ssem, recv_sem=rsem,
            device_id=(peer, me), device_id_type=MESH,
        )

    def to_table(src, dst, ssem, rsem, peer):
        return pltpu.make_async_remote_copy(
            src_ref=src, dst_ref=dst, send_sem=ssem, recv_sem=rsem,
            device_id=(pos, peer), device_id_type=MESH,
        )

    def each(first, last, step):
        lax.fori_loop(first, last, lambda r, c: (step(r), c)[1], 0)

    loads = [
        pltpu.make_async_copy(source, target, load_sem.at[number])
        for number, (source, target) in enumerate(
            [
                (ids_hbm, ids_ref),
                (owner_hbm, owner_ref),
                (local_hbm, local_ref),
                (x_hbm, x_ref),
                (do_hbm, do_ref),
                (proj_hbm, proj_ref),
                (table_hbm, table_ref),
                (moment_hbm, moment_ref),
                (second_hbm, second_ref),
            ]
        )
    ]
    for load in loads:
        load.start()

    barrier = pltpu.get_barrier_semaphore()

    def greet_seq(r):
        pl.semaphore_signal(barrier, inc=1, device_id=(seq_peer(r), me), device_id_type=MESH)

    def greet_table(r):
        pl.semaphore_signal(barrier, inc=1, device_id=(pos, table_peer(r)), device_id_type=MESH)

    each(1, seq_count, greet_seq)
    each(1, owner_count, greet_table)
    pl.semaphore_wait(barrier, seq_count + owner_count - 2)

    def x_copy(peer):
        return to_seq(x_ref, x_all.at[pos], x_send.at[peer], x_recv.at[pos], peer)

    def do_copy(peer):
        return to_seq(do_ref, do_all.at[pos], do_send.at[peer], do_recv.at[pos], peer)

    for load in loads[3:5]:
        load.wait()

    def send_x(i):
        x_copy(row_peer(i)).start()
        x_copy(col_peer(i)).start()

    def each_do(act):
        def one(i):
            for peer in (row_peer(i), col_peer(i)):
                @pl.when(peer < pos)
                def _():
                    act(do_copy(peer))

        each(1, side, one)

    each(1, side, send_x)
    each_do(lambda copy: copy.start())

    def x_relay(block, peer):
        return to_seq(
            x_all.at[block], x_all.at[block], xr_send.at[block], x_recv.at[block], peer
        )

    def do_relay(block, peer):
        return to_seq(
            do_all.at[block], do_all.at[block], dor_send.at[block], do_recv.at[block], peer
        )

    def relay_x(i):
        for block, to_peer, first in ((row_peer(i), col_peer, 0), (col_peer(i), row_peer, 1)):
            x_relay(block, block).wait_recv()

            @pl.when((block // side + block % side) % 2 == first)
            def _():
                each(1, side, lambda k: x_relay(block, to_peer(k)).start())

    def relay_do(i):
        block = col_peer(i)

        @pl.when(block > pos)
        def _():
            do_relay(block, block).wait_recv()
            each(1, side, lambda k: do_relay(block, row_peer(k)).start())

    def end_relays(i):
        for block, to_peer, first in ((row_peer(i), col_peer, 0), (col_peer(i), row_peer, 1)):
            @pl.when((block // side + block % side) % 2 == first)
            def _():
                each(1, side, lambda k: x_relay(block, to_peer(k)).wait_send())

        below = col_peer(i)

        @pl.when(below > pos)
        def _():
            each(1, side, lambda k: do_relay(below, row_peer(k)).wait_send())

    eye = iota((LANES, LANES), 0) == iota((LANES, LANES), 1)

    def to_col(row):
        return jnp.sum(jnp.where(eye, row, 0.0), axis=1, keepdims=True)

    def to_row(col):
        return jnp.sum(jnp.where(eye, col, 0.0), axis=0, keepdims=True)

    for load in loads[:3]:
        load.wait()
    ids = ids_ref[...]
    high_col = to_col((ids // LANES).astype(F32))
    low_col = to_col((ids % LANES).astype(F32))
    id_rows = owner_ref.shape[0]
    local_ids = local_ref[...]
    parts = jnp.concatenate(
        [
            owner_ref[...].astype(F32).astype(BF16),
            (local_ids % 256).astype(F32).astype(BF16),
            (local_ids // 256).astype(F32).astype(BF16),
        ],
        axis=1,
    )
    pick = jnp.where(iota((tokens, id_rows), 1).astype(F32) == high_col, 1.0, 0.0).astype(BF16)
    found = dot(pick, parts)
    in_row = iota((tokens, LANES), 1).astype(F32) == low_col

    def column(part):
        piece = found[:, part * LANES : (part + 1) * LANES]
        return jnp.sum(jnp.where(in_row, piece, 0.0), axis=1, keepdims=True)

    owner_col = column(0)
    local_col = column(1) + 256.0 * column(2)
    owner_row = to_row(owner_col)
    before = (owner_col == owner_row) & (iota((tokens, tokens), 0) < iota((tokens, tokens), 1))
    slot_row = jnp.sum(jnp.where(before, 1.0, 0.0), axis=0, keepdims=True)
    slot_col = to_col(slot_row)
    target_row = owner_row * capacity + slot_row
    sendsel_ref[...] = jnp.where(
        iota((width, tokens), 0).astype(F32) == target_row, 1.0, 0.0
    ).astype(BF16)
    target_col = owner_col * capacity + slot_col
    recvsel_ref[...] = jnp.where(
        iota((tokens, width), 1).astype(F32) == target_col, 1.0, 0.0
    ).astype(BF16)
    recvsel_store = pltpu.make_async_copy(recvsel_ref, recvsel_hbm, store_sem.at[3])
    recvsel_store.start()
    lane_col = slot_col + (me * capacity).astype(F32)
    marks = jnp.where(iota((tokens, width), 1).astype(F32) == lane_col, local_col + 1.0, 0.0)

    def make_index(owner):
        line = jnp.sum(
            jnp.where(owner_col == owner.astype(F32), marks, 0.0), axis=0, keepdims=True
        )
        idx_send[owner] = jnp.broadcast_to(line, (8, width))

    each(0, owner_count, make_index)

    def idx_copy(peer):
        return to_table(
            idx_send.at[peer], idx_got.at[me], idx_ssem.at[peer], idx_rsem.at[me], peer
        )

    each(1, owner_count, lambda r: idx_copy(table_peer(r)).start())
    idx_got[me] = idx_send[me]

    for load in loads[5:6]:
        load.wait()
    x_all[pos] = x_ref[...]
    do_all[pos] = do_ref[...]
    own_ref[...] = dot(x_ref[...], proj_ref[...]).astype(BF16)
    dq_ref[...] = jnp.zeros_like(dq_ref)
    dk_ref[...] = jnp.zeros_like(dk_ref)
    dv_ref[...] = jnp.zeros_like(dv_ref)

    lane = iota((1, LANES), 1)
    group = LANES // head_size
    span = group * tokens
    head_masks = [
        jnp.where(lane // head_size == g, 1.0, 0.0).astype(BF16) for g in range(group)
    ]

    def spread(block):
        return jnp.concatenate([block * m for m in head_masks], axis=0)

    def terms(scores_dot, grad_dot, allowed):
        scores = scores_dot * temper
        gates = 0.5 * jnp.tanh(0.5 * scores) + 0.5
        scaled = gates * allowed
        weights = (scores * scaled).astype(BF16)
        slopes = scaled * (1.0 + scores * (1.0 - gates))
        score_grad = (grad_dot * slopes * temper).astype(BF16)
        return weights, score_grad

    row_ids = iota((tokens, span), 0)
    lane_ids = iota((tokens, span), 1) % tokens

    def visible(query_block, key_block):
        seen = mask_ref[query_block, key_block] == 1
        return jnp.where(seen | (query_block == key_block), history_scale, 0.0)

    def block_step(r):
        block = seq_peer(r)

        in_row, in_col = block // side == my_row, block % side == my_col

        @pl.when(jnp.logical_not(in_row | in_col))
        def _():
            x_relay(block, block).wait_recv()

        @pl.when(block <= pos)
        def _():
            @pl.when(block < pos)
            def _():
                other_ref[...] = dot(x_all[block], proj_ref[:, features:]).astype(BF16)

            @pl.when(block == pos)
            def _():
                other_ref[...] = own_ref[:, features:]

            allowed = jnp.where(
                lane_ids <= row_ids + (pos - block) * tokens, visible(pos, block), 0.0
            )
            for c in range(features // LANES):
                cols = slice(c * LANES, (c + 1) * LANES)
                keys = spread(other_ref[:, cols])
                values = spread(other_ref[:, features + c * LANES : features + (c + 1) * LANES])
                _, score_grad = terms(
                    dot_nt(own_ref[:, cols], keys), dot_nt(do_ref[:, cols], values), allowed
                )
                dq_ref[:, cols] += dot(score_grad, keys)

        @pl.when(block >= pos)
        def _():
            @pl.when(block > pos)
            def _():
                @pl.when(jnp.logical_not(in_col))
                def _():
                    do_relay(block, block).wait_recv()

                other_ref[:, :features] = dot(x_all[block], proj_ref[:, :features]).astype(BF16)

            @pl.when(block == pos)
            def _():
                other_ref[:, :features] = own_ref[:, :features]

            allowed = jnp.where(
                row_ids <= lane_ids + (block - pos) * tokens, visible(block, pos), 0.0
            )
            for c in range(features // LANES):
                cols = slice(c * LANES, (c + 1) * LANES)
                queries = spread(other_ref[:, cols])
                grads = spread(do_all[block, :, cols])
                weights, score_grad = terms(
                    dot_nt(own_ref[:, features + c * LANES : features + (c + 1) * LANES], queries),
                    dot_nt(
                        own_ref[:, 2 * features + c * LANES : 2 * features + (c + 1) * LANES], grads
                    ),
                    allowed,
                )
                dk_ref[:, cols] += dot(score_grad, queries)
                dv_ref[:, cols] += dot(weights, grads)

    block_step(0)

    def take_index(r):
        peer = table_peer(r)
        to_table(
            idx_got.at[peer], idx_got.at[peer], idx_ssem.at[peer], idx_rsem.at[peer], peer
        ).wait_recv()

    each(1, owner_count, take_index)
    idx_all[pos] = jnp.sum(idx_got[...], axis=0)

    def idxf_copy(peer):
        return to_seq(idx_all.at[pos], idx_all.at[pos], idxf_ssem.at[peer], idxf_rsem.at[pos], peer)

    each(1, seq_count, lambda r: idxf_copy(seq_peer(r)).start())

    each(1, side, relay_x)

    slab_ids = iota((slab_rows, width), 0).astype(F32) + 1.0

    def select(block):
        select_ref[block] = jnp.where(
            slab_ids == idx_all[block][0:1, :], 1.0, 0.0
        ).astype(BF16)

    select(pos)
    slab_lanes = iota((LANES, slab_rows), 1).astype(F32) + 1.0
    for c in range(width // LANES):
        lanes = slice(c * LANES, (c + 1) * LANES)
        replysel_ref[lanes, :] = jnp.where(
            slab_lanes == to_col(idx_all[pos][0:1, lanes]), 1.0, 0.0
        ).astype(BF16)

    def select_other(r):
        block = seq_peer(r)
        to_seq(
            idx_all.at[block], idx_all.at[block], idxf_ssem.at[block], idxf_rsem.at[block], block
        ).wait_recv()
        select(block)

    each(1, seq_count, select_other)
    each(1, side, relay_do)
    each(1, seq_count, block_step)

    stacked = jnp.concatenate(
        [dq_ref[...].astype(BF16), dk_ref[...].astype(BF16), dv_ref[...].astype(BF16)], axis=1
    )
    input_grad = dot_nt(stacked, proj_ref[...]).astype(BF16)
    send_buf[...] = dot(sendsel_ref[...], input_grad).astype(BF16)

    def row_copy(peer):
        return to_table(
            send_buf.at[rows_of(peer)], got.at[pos, rows_of(me)],
            row_ssem.at[peer], row_rsem.at[me], peer,
        )

    each(1, owner_count, lambda r: row_copy(table_peer(owner_count - r)).start())
    got[pos, rows_of(me)] = send_buf[rows_of(me)]

    def chunk(block, source, ssem, peer):
        part = got.at[block, rows_of(source)]
        return to_seq(part, part, ssem, fwd_rsem.at[block, source], peer)

    def forward(source):
        def one(i):
            chunk(pos, source, fwd_ssem.at[row_peer(i)], row_peer(i)).start()
            chunk(pos, source, fwd_ssem.at[col_peer(i)], col_peer(i)).start()

        each(1, side, one)

    def pass_chunk(source):
        def along(from_peer, to_peer):
            def one(i):
                block = from_peer(i)
                chunk(block, source, rel_ssem.at[block], block).wait_recv()
                each(
                    1, side,
                    lambda k: chunk(block, source, rel_ssem.at[block], to_peer(k)).start(),
                )

            each(1, side, one)

        @pl.when(source % 2 == 0)
        def _():
            along(row_peer, col_peer)

        @pl.when(source % 2 == 1)
        def _():
            along(col_peer, row_peer)

    forward(me)

    def relay(r):
        source = table_peer(r)
        part = got.at[pos, rows_of(source)]
        to_table(part, part, row_ssem.at[source], row_rsem.at[source], source).wait_recv()
        forward(source)
        pass_chunk(table_peer(r - 1))

    each(1, owner_count, relay)
    pass_chunk(table_peer(owner_count - 1))

    grad_ref[...] = dot(select_ref[pos], got[pos])

    def add_block(r):
        block = seq_peer(r)
        in_row, in_col = block // side == my_row, block % side == my_col

        def await_pair(half):
            for odd, seen in ((0, in_row), (1, in_col)):
                @pl.when(jnp.logical_not(seen))
                def _():
                    chunk(block, 2 * half + odd, rel_ssem.at[block], block).wait_recv()

        each(0, owner_count // 2, await_pair)
        grad_ref[...] += dot(select_ref[block], got[block])

    each(1, seq_count, add_block)

    for load in loads[6:]:
        load.wait()
    for c in range(slab_rows // LANES):
        rows = slice(c * LANES, (c + 1) * LANES)
        grad = grad_ref[rows, :]
        new_moment = first_decay * moment_ref[rows, :] + (1.0 - first_decay) * grad
        mean_square = jnp.sum(grad * grad, axis=1, keepdims=True) * (1.0 / features)
        new_second = second_decay * to_col(second_ref[c : c + 1, :]) + (
            1.0 - second_decay
        ) * mean_square
        nsec_ref[c : c + 1, :] = to_row(new_second)
        nmom_ref[rows, :] = new_moment
        factor = step_rate / (jnp.sqrt(new_second) + epsilon)
        ntab_ref[rows, :] = (table_ref[rows, :].astype(F32) - new_moment * factor).astype(BF16)

    reply_buf[...] = dot(replysel_ref[...], ntab_ref[...]).astype(BF16)

    def reply_copy(peer):
        return to_table(
            reply_buf.at[rows_of(peer)], returned.at[rows_of(me)],
            rep_ssem.at[peer], rep_rsem.at[me], peer,
        )

    each(1, owner_count, lambda r: reply_copy(table_peer(r)).start())
    stores = [
        pltpu.make_async_copy(nmom_ref, nmom_hbm, store_sem.at[0]),
        pltpu.make_async_copy(ntab_ref, ntab_hbm, store_sem.at[1]),
        pltpu.make_async_copy(nsec_ref, nsec_hbm, store_sem.at[2]),
        pltpu.make_async_copy(
            reply_buf.at[rows_of(me)], returned.at[rows_of(me)], store_sem.at[4]
        ),
    ]
    for store in stores:
        store.start()

    each(1, seq_count, lambda r: idxf_copy(seq_peer(r)).wait_send())
    each_do(lambda copy: copy.wait_send())

    def end_seq(i):
        for peer in (row_peer(i), col_peer(i)):
            x_copy(peer).wait_send()
            to_seq(
                got.at[pos], got.at[pos], fwd_ssem.at[peer], fwd_rsem.at[pos, 0], peer
            ).wait_send()
            half = got.at[peer, pl.ds(0, width // 2)]
            for _ in range(side - 1):
                to_seq(
                    half, half, rel_ssem.at[peer], fwd_rsem.at[peer, 0], peer
                ).wait_send()

    each(1, side, end_seq)
    each(1, side, end_relays)

    def end_table(r):
        peer = table_peer(r)
        idx_copy(peer).wait_send()
        row_copy(peer).wait_send()
        part = returned.at[rows_of(peer)]
        to_table(part, part, rep_ssem.at[peer], rep_rsem.at[peer], peer).wait_recv()

    each(1, owner_count, end_table)
    each(1, owner_count, lambda r: reply_copy(table_peer(r)).wait_send())
    for store in stores:
        store.wait()
    recvsel_store.wait()


def finish(
    ntab_hbm, nmom_hbm, nsec_hbm, recvsel_hbm, returned_hbm,
    ntab_out, nmom_out, nsec_out, event_out,
    ntab_ref, nmom_ref, nsec_ref, recvsel_ref, returned_ref, event_ref, in_sem, out_sem, event_sem,
):
    waits = [
        pltpu.make_async_copy(returned_hbm, returned_ref, event_sem.at[0]),
        pltpu.make_async_copy(recvsel_hbm, recvsel_ref, event_sem.at[1]),
    ]
    loads, stores = [], []
    for source, target, stage in (
        (nmom_hbm, nmom_out, nmom_ref),
        (ntab_hbm, ntab_out, ntab_ref),
        (nsec_hbm, nsec_out, nsec_ref),
    ):
        rows = source.shape[0]
        pieces = rows // LANES if rows > LANES else 1
        size = rows // pieces
        for piece in range(pieces):
            part = pl.ds(piece * size, size)
            number = len(loads)
            loads.append(
                pltpu.make_async_copy(source.at[part], stage.at[part], in_sem.at[number])
            )
            stores.append(
                pltpu.make_async_copy(stage.at[part], target.at[part], out_sem.at[number])
            )
    for load in waits + loads:
        load.start()
    for load in waits:
        load.wait()
    event_ref[...] = dot(recvsel_ref[...], returned_ref[...]).astype(BF16)
    stores.append(pltpu.make_async_copy(event_ref, event_out, event_sem.at[2]))
    stores[-1].start()
    for load, store in zip(loads, stores):
        load.wait()
        store.start()
    for store in stores:
        store.wait()


def body(events_x, proj, out_grad, block_mask, item_ids, owner_of, local_of, table, moment, second):
    tokens, features = events_x.shape[1:]
    seq_count = lax.axis_size("seq")
    owner_count = lax.axis_size("table")
    slab_rows = table.shape[0]
    capacity = max(2 * tokens // owner_count, 16)
    width = owner_count * capacity
    smem = pl.BlockSpec(memory_space=pltpu.SMEM)
    hbm = pl.BlockSpec(memory_space=pl.ANY)
    dma = pltpu.SemaphoreType.DMA
    results = pl.pallas_call(
        functools.partial(kernel, seq_count, owner_count, capacity),
        out_shape=(
            jax.ShapeDtypeStruct((slab_rows, features), BF16),
            jax.ShapeDtypeStruct((slab_rows, features), F32),
            jax.ShapeDtypeStruct((slab_rows // LANES, LANES), F32),
            jax.ShapeDtypeStruct((tokens, width), BF16),
            jax.ShapeDtypeStruct((width, features), BF16),
        ),
        in_specs=[hbm, hbm, hbm, smem] + [hbm] * 6,
        out_specs=(hbm,) * 5,
        scratch_shapes=[
            pltpu.VMEM((tokens, features), BF16),
            pltpu.VMEM((tokens, features), BF16),
            pltpu.VMEM((1, tokens), jnp.int32),
            pltpu.VMEM((owner_of.shape[0] // LANES, LANES), jnp.int32),
            pltpu.VMEM((owner_of.shape[0] // LANES, LANES), jnp.int32),
            pltpu.VMEM((slab_rows // LANES, LANES), F32),
            pltpu.VMEM((slab_rows // LANES, LANES), F32),
            pltpu.VMEM((tokens, width), BF16),
            pltpu.VMEM((seq_count, slab_rows, width), BF16),
            pltpu.VMEM((width, slab_rows), BF16),
            pltpu.VMEM((seq_count, tokens, features), BF16),
            pltpu.VMEM((seq_count, tokens, features), BF16),
            pltpu.VMEM(proj.shape, BF16),
            pltpu.VMEM((slab_rows, features), BF16),
            pltpu.VMEM((slab_rows, features), F32),
            pltpu.VMEM((slab_rows, features), BF16),
            pltpu.VMEM((slab_rows, features), F32),
            pltpu.VMEM((tokens, 3 * features), BF16),
            pltpu.VMEM((tokens, 2 * features), BF16),
            pltpu.VMEM((tokens, features), F32),
            pltpu.VMEM((tokens, features), F32),
            pltpu.VMEM((tokens, features), F32),
            pltpu.VMEM((width, tokens), BF16),
            pltpu.VMEM((owner_count, 8, width), F32),
            pltpu.VMEM((owner_count, 8, width), F32),
            pltpu.VMEM((seq_count, 8, width), F32),
            pltpu.VMEM((width, features), BF16),
            pltpu.VMEM((seq_count, width, features), BF16),
            pltpu.VMEM((slab_rows, features), F32),
            pltpu.VMEM((width, features), BF16),
            dma((9,)),
            dma((5,)),
            dma((seq_count,)),
            dma((seq_count,)),
            dma((seq_count,)),
            dma((seq_count,)),
            dma((owner_count,)),
            dma((owner_count,)),
            dma((seq_count,)),
            dma((seq_count,)),
            dma((owner_count,)),
            dma((owner_count,)),
            dma((seq_count,)),
            dma((seq_count, owner_count)),
            dma((owner_count,)),
            dma((owner_count,)),
            dma((seq_count,)),
            dma((seq_count,)),
            dma((seq_count,)),
        ],
        compiler_params=pltpu.CompilerParams(
            collective_id=0, has_side_effects=True, vmem_limit_bytes=VMEM_BYTES
        ),
    )(
        events_x[0],
        proj,
        out_grad[0],
        block_mask,
        item_ids,
        owner_of.reshape(-1, LANES),
        local_of.reshape(-1, LANES),
        table,
        moment,
        second.reshape(-1, LANES),
    )
    outs = [(r.shape, r.dtype) for r in results]
    events = ((tokens, features), BF16)
    new_table, new_moment, new_second, event_rows = pl.pallas_call(
        finish,
        out_shape=tuple(jax.ShapeDtypeStruct(*o) for o in outs[:3] + [events]),
        in_specs=[hbm] * 5,
        out_specs=(hbm,) * 4,
        scratch_shapes=[pltpu.VMEM(*o) for o in outs + [events]]
        + [dma((2 * (slab_rows // LANES) + 1,))] * 2
        + [dma((3,))],
        compiler_params=pltpu.CompilerParams(vmem_limit_bytes=VMEM_BYTES),
    )(*results)
    return (new_table, new_moment, new_second.reshape(-1), event_rows[None])


def solution(mesh):
    return jax.shard_map(
        body,
        mesh=mesh,
        in_specs=(
            P("table", "seq", None),
            P(),
            P("table", "seq", None),
            P(),
            P("table", "seq"),
            P(),
            P(),
            P("table", None),
            P("table", None),
            P("table"),
        ),
        out_specs=(P("table", None), P("table", None), P("table"), P("table", "seq", None)),
        check_vma=False,
    )
```

```python
import functools
import math

import jax
import jax.numpy as jnp
from jax import lax
from jax.experimental import pallas as pl
from jax.experimental.pallas import tpu as pltpu
from jax.sharding import PartitionSpec as P

HEADS = 8
LANES = 128
VMEM_BYTES = 63 * 1024 * 1024

first_decay = 0.9
second_decay = 0.99
step_rate = 0.05
epsilon = 1e-08

F32 = jnp.float32
BF16 = jnp.bfloat16
MESH = pl.DeviceIdType.MESH


def iota(shape, axis):
    return lax.broadcasted_iota(jnp.int32, shape, axis)


def dot(a, b):
    return jnp.dot(a, b, preferred_element_type=F32)


def dot_nt(a, b):
    return lax.dot_general(a, b, (((1,), (1,)), ((), ())), preferred_element_type=F32)


def kernel(
    seq_count, owner_count, capacity,
    x_hbm, proj_hbm, do_hbm, mask_ref, ids_hbm, owner_hbm, local_hbm, table_hbm, moment_hbm, second_hbm,
    ntab_hbm, nmom_hbm, nsec_hbm, event_hbm,
    x_ref, do_ref, ids_ref, owner_ref, local_ref, second_ref, nsec_ref, event_ref, returned, recvsel_ref, select_ref, replysel_ref,
    x_all, do_all, proj_ref, table_ref, moment_ref, ntab_ref, nmom_ref,
    own_ref, other_ref, dq_ref, dk_ref, dv_ref, sendsel_ref,
    idx_send, idx_got, idx_all, send_buf, got, grad_ref, reply_buf,
    load_sem, store_sem, x_send, x_recv, do_send, do_recv, idx_ssem, idx_rsem, idxf_ssem, idxf_rsem,
    row_ssem, row_rsem, fwd_ssem, fwd_rsem, rep_ssem, rep_rsem, rel_ssem, xr_send, diag_ssem,
):
    pos = lax.axis_index("seq")
    me = lax.axis_index("table")
    tokens, features = x_ref.shape
    head_size = features // HEADS
    slab_rows = table_ref.shape[0]
    width = owner_count * capacity
    history_scale = 1.0 / math.sqrt(tokens * seq_count)
    temper = 1.0 / math.sqrt(head_size)
    turn = 1 - 2 * (pos % 2)
    side = math.isqrt(seq_count)
    my_row, my_col = pos // side, pos % side

    def row_peer(i):
        return my_row * side + lax.rem(my_col + i, side)

    def col_peer(i):
        return lax.rem(my_row + i, side) * side + my_col

    def seq_peer(r):
        return lax.rem(pos + turn * r + seq_count, seq_count)

    def table_peer(r):
        peer, bit = 0, 1
        while bit < owner_count:
            mine, other = (me // bit) % 2, (r // bit) % 2
            peer = peer + bit * (mine + other - 2 * mine * other)
            bit *= 2
        return peer

    def rows_of(owner):
        return pl.ds(pl.multiple_of(owner * capacity, capacity), capacity)

    def to_seq(src, dst, ssem, rsem, peer):
        return pltpu.make_async_remote_copy(
            src_ref=src, dst_ref=dst, send_sem=ssem, recv_sem=rsem,
            device_id=(peer, me), device_id_type=MESH,
        )

    def to_table(src, dst, ssem, rsem, peer):
        return pltpu.make_async_remote_copy(
            src_ref=src, dst_ref=dst, send_sem=ssem, recv_sem=rsem,
            device_id=(pos, peer), device_id_type=MESH,
        )

    def each(first, last, step):
        lax.fori_loop(first, last, lambda r, c: (step(r), c)[1], 0)

    loads = [
        pltpu.make_async_copy(source, target, load_sem.at[number])
        for number, (source, target) in enumerate(
            [
                (ids_hbm, ids_ref),
                (owner_hbm, owner_ref),
                (local_hbm, local_ref),
                (x_hbm, x_ref),
                (do_hbm, do_ref),
                (proj_hbm, proj_ref),
                (table_hbm, table_ref),
                (moment_hbm, moment_ref),
                (second_hbm, second_ref),
            ]
        )
    ]
    for load in loads:
        load.start()

    barrier = pltpu.get_barrier_semaphore()

    def greet_seq(r):
        pl.semaphore_signal(barrier, inc=1, device_id=(seq_peer(r), me), device_id_type=MESH)

    def greet_table(r):
        pl.semaphore_signal(barrier, inc=1, device_id=(pos, table_peer(r)), device_id_type=MESH)

    each(1, seq_count, greet_seq)
    each(1, owner_count, greet_table)
    pl.semaphore_wait(barrier, seq_count + owner_count - 2)

    def x_copy(peer):
        return to_seq(x_ref, x_all.at[pos], x_send.at[peer], x_recv.at[pos], peer)

    def do_copy(peer):
        return to_seq(do_ref, do_all.at[pos], do_send.at[peer], do_recv.at[pos], peer)

    for load in loads[3:5]:
        load.wait()

    def send_x(i):
        x_copy(row_peer(i)).start()
        x_copy(col_peer(i)).start()

    def each_do(act):
        def one(r):
            peer = seq_peer(r)

            @pl.when(peer < pos)
            def _():
                act(do_copy(peer))

        each(1, seq_count, one)

    each(1, side, send_x)
    each_do(lambda copy: copy.start())

    def x_relay(block, peer):
        return to_seq(
            x_all.at[block], x_all.at[block], xr_send.at[block], x_recv.at[block], peer
        )

    def relay_x(i):
        for block, to_peer, first in ((row_peer(i), col_peer, 0), (col_peer(i), row_peer, 1)):
            x_relay(block, block).wait_recv()

            @pl.when((block // side) % 2 == first)
            def _():
                each(1, side, lambda k: x_relay(block, to_peer(k)).start())

    def end_relays(i):
        for block, to_peer, first in ((row_peer(i), col_peer, 0), (col_peer(i), row_peer, 1)):
            @pl.when((block // side) % 2 == first)
            def _():
                each(1, side, lambda k: x_relay(block, to_peer(k)).wait_send())

    eye = iota((LANES, LANES), 0) == iota((LANES, LANES), 1)

    def to_col(row):
        return jnp.sum(jnp.where(eye, row, 0.0), axis=1, keepdims=True)

    def to_row(col):
        return jnp.sum(jnp.where(eye, col, 0.0), axis=0, keepdims=True)

    for load in loads[:3]:
        load.wait()
    ids = ids_ref[...]
    high_col = to_col((ids // LANES).astype(F32))
    low_col = to_col((ids % LANES).astype(F32))
    id_rows = owner_ref.shape[0]
    local_ids = local_ref[...]
    parts = jnp.concatenate(
        [
            owner_ref[...].astype(F32).astype(BF16),
            (local_ids % 256).astype(F32).astype(BF16),
            (local_ids // 256).astype(F32).astype(BF16),
        ],
        axis=1,
    )
    pick = jnp.where(iota((tokens, id_rows), 1).astype(F32) == high_col, 1.0, 0.0).astype(BF16)
    found = dot(pick, parts)
    in_row = iota((tokens, LANES), 1).astype(F32) == low_col

    def column(part):
        piece = found[:, part * LANES : (part + 1) * LANES]
        return jnp.sum(jnp.where(in_row, piece, 0.0), axis=1, keepdims=True)

    owner_col = column(0)
    local_col = column(1) + 256.0 * column(2)
    owner_row = to_row(owner_col)
    before = (owner_col == owner_row) & (iota((tokens, tokens), 0) < iota((tokens, tokens), 1))
    slot_row = jnp.sum(jnp.where(before, 1.0, 0.0), axis=0, keepdims=True)
    slot_col = to_col(slot_row)
    target_row = owner_row * capacity + slot_row
    sendsel_ref[...] = jnp.where(
        iota((width, tokens), 0).astype(F32) == target_row, 1.0, 0.0
    ).astype(BF16)
    target_col = owner_col * capacity + slot_col
    recvsel_ref[...] = jnp.where(
        iota((tokens, width), 1).astype(F32) == target_col, 1.0, 0.0
    ).astype(BF16)
    lane_col = slot_col + (me * capacity).astype(F32)
    marks = jnp.where(iota((tokens, width), 1).astype(F32) == lane_col, local_col + 1.0, 0.0)

    def make_index(owner):
        line = jnp.sum(
            jnp.where(owner_col == owner.astype(F32), marks, 0.0), axis=0, keepdims=True
        )
        idx_send[owner] = jnp.broadcast_to(line, (8, width))

    each(0, owner_count, make_index)

    def idx_copy(peer):
        return to_table(
            idx_send.at[peer], idx_got.at[me], idx_ssem.at[peer], idx_rsem.at[me], peer
        )

    each(1, owner_count, lambda r: idx_copy(table_peer(r)).start())
    idx_got[me] = idx_send[me]

    for load in loads[5:6]:
        load.wait()
    x_all[pos] = x_ref[...]
    do_all[pos] = do_ref[...]
    own_ref[...] = dot(x_ref[...], proj_ref[...]).astype(BF16)
    dq_ref[...] = jnp.zeros_like(dq_ref)
    dk_ref[...] = jnp.zeros_like(dk_ref)
    dv_ref[...] = jnp.zeros_like(dv_ref)

    lane = iota((1, LANES), 1)
    group = LANES // head_size
    span = group * tokens
    head_masks = [
        jnp.where(lane // head_size == g, 1.0, 0.0).astype(BF16) for g in range(group)
    ]

    def spread(block):
        return jnp.concatenate([block * m for m in head_masks], axis=0)

    def terms(scores_dot, grad_dot, allowed):
        scores = scores_dot * temper
        gates = 0.5 * jnp.tanh(0.5 * scores) + 0.5
        scaled = gates * allowed
        weights = (scores * scaled).astype(BF16)
        slopes = scaled * (1.0 + scores * (1.0 - gates))
        score_grad = (grad_dot * slopes * temper).astype(BF16)
        return weights, score_grad

    row_ids = iota((tokens, span), 0)
    lane_ids = iota((tokens, span), 1) % tokens

    def visible(query_block, key_block):
        seen = mask_ref[query_block, key_block] == 1
        return jnp.where(seen | (query_block == key_block), history_scale, 0.0)

    def block_step(r):
        block = seq_peer(r)

        in_row, in_col = block // side == my_row, block % side == my_col

        @pl.when(jnp.logical_not(in_row | in_col))
        def _():
            x_relay(block, block).wait_recv()

        @pl.when(block <= pos)
        def _():
            @pl.when(block < pos)
            def _():
                other_ref[...] = dot(x_all[block], proj_ref[:, features:]).astype(BF16)

            @pl.when(block == pos)
            def _():
                other_ref[...] = own_ref[:, features:]

            allowed = jnp.where(
                lane_ids <= row_ids + (pos - block) * tokens, visible(pos, block), 0.0
            )
            for c in range(features // LANES):
                cols = slice(c * LANES, (c + 1) * LANES)
                keys = spread(other_ref[:, cols])
                values = spread(other_ref[:, features + c * LANES : features + (c + 1) * LANES])
                _, score_grad = terms(
                    dot_nt(own_ref[:, cols], keys), dot_nt(do_ref[:, cols], values), allowed
                )
                dq_ref[:, cols] += dot(score_grad, keys)

        @pl.when(block >= pos)
        def _():
            @pl.when(block > pos)
            def _():
                other_ref[:, :features] = dot(x_all[block], proj_ref[:, :features]).astype(BF16)
                to_seq(
                    do_all.at[block], do_all.at[block], do_send.at[block], do_recv.at[block], block
                ).wait_recv()

            @pl.when(block == pos)
            def _():
                other_ref[:, :features] = own_ref[:, :features]

            allowed = jnp.where(
                row_ids <= lane_ids + (block - pos) * tokens, visible(block, pos), 0.0
            )
            for c in range(features // LANES):
                cols = slice(c * LANES, (c + 1) * LANES)
                queries = spread(other_ref[:, cols])
                grads = spread(do_all[block, :, cols])
                weights, score_grad = terms(
                    dot_nt(own_ref[:, features + c * LANES : features + (c + 1) * LANES], queries),
                    dot_nt(
                        own_ref[:, 2 * features + c * LANES : 2 * features + (c + 1) * LANES], grads
                    ),
                    allowed,
                )
                dk_ref[:, cols] += dot(score_grad, queries)
                dv_ref[:, cols] += dot(weights, grads)

    block_step(0)

    def take_index(r):
        peer = table_peer(r)
        to_table(
            idx_got.at[peer], idx_got.at[peer], idx_ssem.at[peer], idx_rsem.at[peer], peer
        ).wait_recv()

    each(1, owner_count, take_index)
    idx_all[pos] = jnp.sum(idx_got[...], axis=0)

    def idxf_copy(peer):
        return to_seq(idx_all.at[pos], idx_all.at[pos], idxf_ssem.at[peer], idxf_rsem.at[pos], peer)

    each(1, seq_count, lambda r: idxf_copy(seq_peer(r)).start())

    each(1, side, relay_x)

    slab_ids = iota((slab_rows, width), 0).astype(F32) + 1.0

    def select(block):
        select_ref[block] = jnp.where(
            slab_ids == idx_all[block][0:1, :], 1.0, 0.0
        ).astype(BF16)

    select(pos)
    slab_lanes = iota((LANES, slab_rows), 1).astype(F32) + 1.0
    for c in range(width // LANES):
        lanes = slice(c * LANES, (c + 1) * LANES)
        replysel_ref[lanes, :] = jnp.where(
            slab_lanes == to_col(idx_all[pos][0:1, lanes]), 1.0, 0.0
        ).astype(BF16)

    def select_other(r):
        block = seq_peer(r)
        to_seq(
            idx_all.at[block], idx_all.at[block], idxf_ssem.at[block], idxf_rsem.at[block], block
        ).wait_recv()
        select(block)

    each(1, seq_count, select_other)
    each(1, seq_count, block_step)

    stacked = jnp.concatenate(
        [dq_ref[...].astype(BF16), dk_ref[...].astype(BF16), dv_ref[...].astype(BF16)], axis=1
    )
    input_grad = dot_nt(stacked, proj_ref[...]).astype(BF16)
    send_buf[...] = dot(sendsel_ref[...], input_grad).astype(BF16)

    def row_copy(peer):
        return to_table(
            send_buf.at[rows_of(peer)], got.at[pos, rows_of(me)],
            row_ssem.at[peer], row_rsem.at[me], peer,
        )

    each(1, owner_count, lambda r: row_copy(table_peer(owner_count - r)).start())
    got[pos, rows_of(me)] = send_buf[rows_of(me)]

    def chunk(block, source, ssem, peer):
        part = got.at[block, rows_of(source)]
        return to_seq(part, part, ssem, fwd_rsem.at[block, source], peer)

    def forward(source):
        def one(i):
            chunk(pos, source, fwd_ssem.at[row_peer(i)], row_peer(i)).start()
            chunk(pos, source, fwd_ssem.at[col_peer(i)], col_peer(i)).start()

        each(1, side, one)

    near = owner_count // 2

    def each_diag(act):
        def one(r):
            peer = seq_peer(r)

            @pl.when(jnp.logical_not((peer // side == my_row) | (peer % side == my_col)))
            def _():
                act(peer)

        each(1, seq_count, one)

    def forward_far(source):
        forward(source)
        each_diag(lambda peer: chunk(pos, source, diag_ssem.at[peer], peer).start())

    def pass_chunk(source):
        def along(from_peer, to_peer):
            def one(i):
                block = from_peer(i)
                chunk(block, source, rel_ssem.at[block], block).wait_recv()
                each(
                    1, side,
                    lambda k: chunk(block, source, rel_ssem.at[block], to_peer(k)).start(),
                )

            each(1, side, one)

        @pl.when(source % 2 == 0)
        def _():
            along(row_peer, col_peer)

        @pl.when(source % 2 == 1)
        def _():
            along(col_peer, row_peer)

    forward(me)

    def take_chunk(r):
        source = table_peer(r)
        part = got.at[pos, rows_of(source)]
        to_table(part, part, row_ssem.at[source], row_rsem.at[source], source).wait_recv()
        return source

    def relay(r):
        forward(take_chunk(r))
        pass_chunk(table_peer(r - 1))

    each(1, near, relay)
    pass_chunk(table_peer(near - 1))
    each(near, owner_count, lambda r: forward_far(take_chunk(r)))

    grad_ref[...] = dot(select_ref[pos], got[pos])

    def add_block(r):
        block = seq_peer(r)
        in_row, in_col = block // side == my_row, block % side == my_col

        def await_chunk(r):
            source = table_peer(r)
            passed = (in_row & (source % 2 == 0)) | (in_col & (source % 2 == 1))

            @pl.when(jnp.logical_not(passed & (r < near)))
            def _():
                chunk(block, source, rel_ssem.at[block], block).wait_recv()

        each(0, owner_count, await_chunk)
        grad_ref[...] += dot(select_ref[block], got[block])

    each(1, seq_count, add_block)

    for load in loads[6:]:
        load.wait()
    for c in range(slab_rows // LANES):
        rows = slice(c * LANES, (c + 1) * LANES)
        grad = grad_ref[rows, :]
        new_moment = first_decay * moment_ref[rows, :] + (1.0 - first_decay) * grad
        mean_square = jnp.sum(grad * grad, axis=1, keepdims=True) * (1.0 / features)
        new_second = second_decay * to_col(second_ref[c : c + 1, :]) + (
            1.0 - second_decay
        ) * mean_square
        nsec_ref[c : c + 1, :] = to_row(new_second)
        nmom_ref[rows, :] = new_moment
        factor = step_rate / (jnp.sqrt(new_second) + epsilon)
        ntab_ref[rows, :] = (table_ref[rows, :].astype(F32) - new_moment * factor).astype(BF16)

    reply_buf[...] = dot(replysel_ref[...], ntab_ref[...]).astype(BF16)

    def reply_copy(peer):
        return to_table(
            reply_buf.at[rows_of(peer)], returned.at[rows_of(me)],
            rep_ssem.at[peer], rep_rsem.at[me], peer,
        )

    each(1, owner_count, lambda r: reply_copy(table_peer(r)).start())
    stores = [
        pltpu.make_async_copy(nmom_ref, nmom_hbm, store_sem.at[0]),
        pltpu.make_async_copy(ntab_ref, ntab_hbm, store_sem.at[1]),
        pltpu.make_async_copy(nsec_ref, nsec_hbm, store_sem.at[2]),
    ]
    for store in stores:
        store.start()
    returned[rows_of(me)] = reply_buf[rows_of(me)]

    each(1, seq_count, lambda r: idxf_copy(seq_peer(r)).wait_send())
    each_do(lambda copy: copy.wait_send())

    def end_seq(i):
        for peer in (row_peer(i), col_peer(i)):
            x_copy(peer).wait_send()
            to_seq(
                got.at[pos], got.at[pos], fwd_ssem.at[peer], fwd_rsem.at[pos, 0], peer
            ).wait_send()
            half = got.at[peer, pl.ds(0, width // 4)]
            for _ in range(side - 1):
                to_seq(
                    half, half, rel_ssem.at[peer], fwd_rsem.at[peer, 0], peer
                ).wait_send()

    each(1, side, end_seq)
    far = got.at[pos, pl.ds(0, width // 2)]
    each_diag(
        lambda peer: to_seq(
            far, far, diag_ssem.at[peer], fwd_rsem.at[pos, 0], peer
        ).wait_send()
    )
    each(1, side, end_relays)

    def end_table(r):
        peer = table_peer(r)
        idx_copy(peer).wait_send()
        row_copy(peer).wait_send()
        part = returned.at[rows_of(peer)]
        to_table(part, part, rep_ssem.at[peer], rep_rsem.at[peer], peer).wait_recv()

    each(1, owner_count, end_table)
    event_ref[...] = dot(recvsel_ref[...], returned[...]).astype(BF16)
    last = pltpu.make_async_copy(event_ref, event_hbm, store_sem.at[3])
    last.start()
    each(1, owner_count, lambda r: reply_copy(table_peer(r)).wait_send())
    for store in stores:
        store.wait()
    last.wait()


def pass_on(*refs):
    count = len(refs) // 3
    sources, targets, held = refs[:count], refs[count : 2 * count], refs[2 * count : 3 * count]
    in_sem, out_sem = refs[3 * count :]
    loads, stores = [], []
    for source, target, stage in zip(sources, targets, held):
        rows = source.shape[0]
        pieces = rows // LANES if rows > LANES else 1
        size = rows // pieces
        for piece in range(pieces):
            part = pl.ds(piece * size, size)
            number = len(loads)
            loads.append(
                pltpu.make_async_copy(source.at[part], stage.at[part], in_sem.at[number])
            )
            stores.append(
                pltpu.make_async_copy(stage.at[part], target.at[part], out_sem.at[number])
            )
    for load in loads:
        load.start()
    for load, store in zip(loads, stores):
        load.wait()
        store.start()
    for store in stores:
        store.wait()


def body(events_x, proj, out_grad, block_mask, item_ids, owner_of, local_of, table, moment, second):
    tokens, features = events_x.shape[1:]
    seq_count = lax.axis_size("seq")
    owner_count = lax.axis_size("table")
    slab_rows = table.shape[0]
    capacity = max(2 * tokens // owner_count, 16)
    width = owner_count * capacity
    smem = pl.BlockSpec(memory_space=pltpu.SMEM)
    hbm = pl.BlockSpec(memory_space=pl.ANY)
    dma = pltpu.SemaphoreType.DMA
    results = pl.pallas_call(
        functools.partial(kernel, seq_count, owner_count, capacity),
        out_shape=(
            jax.ShapeDtypeStruct((slab_rows, features), BF16),
            jax.ShapeDtypeStruct((slab_rows, features), F32),
            jax.ShapeDtypeStruct((slab_rows // LANES, LANES), F32),
            jax.ShapeDtypeStruct((tokens, features), BF16),
        ),
        in_specs=[hbm, hbm, hbm, smem] + [hbm] * 6,
        out_specs=(hbm,) * 4,
        scratch_shapes=[
            pltpu.VMEM((tokens, features), BF16),
            pltpu.VMEM((tokens, features), BF16),
            pltpu.VMEM((1, tokens), jnp.int32),
            pltpu.VMEM((owner_of.shape[0] // LANES, LANES), jnp.int32),
            pltpu.VMEM((owner_of.shape[0] // LANES, LANES), jnp.int32),
            pltpu.VMEM((slab_rows // LANES, LANES), F32),
            pltpu.VMEM((slab_rows // LANES, LANES), F32),
            pltpu.VMEM((tokens, features), BF16),
            pltpu.VMEM((width, features), BF16),
            pltpu.VMEM((tokens, width), BF16),
            pltpu.VMEM((seq_count, slab_rows, width), BF16),
            pltpu.VMEM((width, slab_rows), BF16),
            pltpu.VMEM((seq_count, tokens, features), BF16),
            pltpu.VMEM((seq_count, tokens, features), BF16),
            pltpu.VMEM(proj.shape, BF16),
            pltpu.VMEM((slab_rows, features), BF16),
            pltpu.VMEM((slab_rows, features), F32),
            pltpu.VMEM((slab_rows, features), BF16),
            pltpu.VMEM((slab_rows, features), F32),
            pltpu.VMEM((tokens, 3 * features), BF16),
            pltpu.VMEM((tokens, 2 * features), BF16),
            pltpu.VMEM((tokens, features), F32),
            pltpu.VMEM((tokens, features), F32),
            pltpu.VMEM((tokens, features), F32),
            pltpu.VMEM((width, tokens), BF16),
            pltpu.VMEM((owner_count, 8, width), F32),
            pltpu.VMEM((owner_count, 8, width), F32),
            pltpu.VMEM((seq_count, 8, width), F32),
            pltpu.VMEM((width, features), BF16),
            pltpu.VMEM((seq_count, width, features), BF16),
            pltpu.VMEM((slab_rows, features), F32),
            pltpu.VMEM((width, features), BF16),
            dma((9,)),
            dma((4,)),
            dma((seq_count,)),
            dma((seq_count,)),
            dma((seq_count,)),
            dma((seq_count,)),
            dma((owner_count,)),
            dma((owner_count,)),
            dma((seq_count,)),
            dma((seq_count,)),
            dma((owner_count,)),
            dma((owner_count,)),
            dma((seq_count,)),
            dma((seq_count, owner_count)),
            dma((owner_count,)),
            dma((owner_count,)),
            dma((seq_count,)),
            dma((seq_count,)),
            dma((seq_count,)),
        ],
        compiler_params=pltpu.CompilerParams(
            collective_id=0, has_side_effects=True, vmem_limit_bytes=VMEM_BYTES
        ),
    )(
        events_x[0],
        proj,
        out_grad[0],
        block_mask,
        item_ids,
        owner_of.reshape(-1, LANES),
        local_of.reshape(-1, LANES),
        table,
        moment,
        second.reshape(-1, LANES),
    )
    new_table, new_moment, new_second, event_rows = pl.pallas_call(
        pass_on,
        out_shape=tuple(jax.ShapeDtypeStruct(r.shape, r.dtype) for r in results),
        in_specs=[hbm] * 4,
        out_specs=(hbm,) * 4,
        scratch_shapes=[pltpu.VMEM(r.shape, r.dtype) for r in results]
        + [dma((2 * (slab_rows // LANES) + 2,))] * 2,
        compiler_params=pltpu.CompilerParams(vmem_limit_bytes=VMEM_BYTES),
    )(*results)
    return (new_table, new_moment, new_second.reshape(-1), event_rows[None])


def solution(mesh):
    return jax.shard_map(
        body,
        mesh=mesh,
        in_specs=(
            P("table", "seq", None),
            P(),
            P("table", "seq", None),
            P(),
            P("table", "seq"),
            P(),
            P(),
            P("table", None),
            P("table", None),
            P("table"),
        ),
        out_specs=(P("table", None), P("table", None), P("table"), P("table", "seq", None)),
        check_vma=False,
    )
```

```python
import functools
import math

import jax
import jax.numpy as jnp
from jax import lax
from jax.experimental import pallas as pl
from jax.experimental.pallas import tpu as pltpu
from jax.sharding import PartitionSpec as P

HEADS = 8
LANES = 128
VMEM_BYTES = 63 * 1024 * 1024

first_decay = 0.9
second_decay = 0.99
step_rate = 0.05
epsilon = 1e-08

F32 = jnp.float32
BF16 = jnp.bfloat16
MESH = pl.DeviceIdType.MESH


def iota(shape, axis):
    return lax.broadcasted_iota(jnp.int32, shape, axis)


def dot(a, b):
    return jnp.dot(a, b, preferred_element_type=F32)


def dot_nt(a, b):
    return lax.dot_general(a, b, (((1,), (1,)), ((), ())), preferred_element_type=F32)


def kernel(
    seq_count, owner_count, capacity,
    x_hbm, proj_hbm, do_hbm, mask_ref, ids_hbm, owner_hbm, local_hbm, table_hbm, moment_hbm, second_hbm,
    ntab_hbm, nmom_hbm, nsec_hbm, event_hbm,
    x_ref, do_ref, ids_ref, owner_ref, local_ref, second_ref, nsec_ref, event_ref, returned, recvsel_ref, select_ref, replysel_ref,
    x_all, do_all, proj_ref, table_ref, moment_ref, ntab_ref, nmom_ref,
    own_ref, scaled_ref, scaled_do_ref, other_ref, dq_ref, dk_ref, dv_ref, sendsel_ref,
    idx_send, idx_got, idx_all, send_buf, got, grad_ref, reply_buf,
    load_sem, store_sem, x_send, x_recv, do_send, do_recv, idx_ssem, idx_rsem, idxf_ssem, idxf_rsem,
    row_ssem, row_rsem, fwd_ssem, fwd_rsem, rep_ssem, rep_rsem, rel_ssem, xr_send, diag_ssem,
):
    pos = lax.axis_index("seq")
    me = lax.axis_index("table")
    tokens, features = x_ref.shape
    head_size = features // HEADS
    slab_rows = table_ref.shape[0]
    width = owner_count * capacity
    history_scale = 1.0 / math.sqrt(tokens * seq_count)
    temper = 1.0 / math.sqrt(head_size)
    turn = 1 - 2 * (pos % 2)
    side = math.isqrt(seq_count)
    my_row, my_col = pos // side, pos % side

    def row_peer(i):
        return my_row * side + lax.rem(my_col + i, side)

    def col_peer(i):
        return lax.rem(my_row + i, side) * side + my_col

    def seq_peer(r):
        return lax.rem(pos + turn * r + seq_count, seq_count)

    def table_peer(r):
        peer, bit = 0, 1
        while bit < owner_count:
            mine, other = (me // bit) % 2, (r // bit) % 2
            peer = peer + bit * (mine + other - 2 * mine * other)
            bit *= 2
        return peer

    def rows_of(owner):
        return pl.ds(pl.multiple_of(owner * capacity, capacity), capacity)

    def to_seq(src, dst, ssem, rsem, peer):
        return pltpu.make_async_remote_copy(
            src_ref=src, dst_ref=dst, send_sem=ssem, recv_sem=rsem,
            device_id=(peer, me), device_id_type=MESH,
        )

    def to_table(src, dst, ssem, rsem, peer):
        return pltpu.make_async_remote_copy(
            src_ref=src, dst_ref=dst, send_sem=ssem, recv_sem=rsem,
            device_id=(pos, peer), device_id_type=MESH,
        )

    def each(first, last, step):
        lax.fori_loop(first, last, lambda r, c: (step(r), c)[1], 0)

    loads = [
        pltpu.make_async_copy(source, target, load_sem.at[number])
        for number, (source, target) in enumerate(
            [
                (ids_hbm, ids_ref),
                (owner_hbm, owner_ref),
                (local_hbm, local_ref),
                (x_hbm, x_ref),
                (do_hbm, do_ref),
                (proj_hbm, proj_ref),
                (table_hbm, table_ref),
                (moment_hbm, moment_ref),
                (second_hbm, second_ref),
            ]
        )
    ]
    for load in loads:
        load.start()

    barrier = pltpu.get_barrier_semaphore()

    def greet_seq(r):
        pl.semaphore_signal(barrier, inc=1, device_id=(seq_peer(r), me), device_id_type=MESH)

    def greet_table(r):
        pl.semaphore_signal(barrier, inc=1, device_id=(pos, table_peer(r)), device_id_type=MESH)

    each(1, seq_count, greet_seq)
    each(1, owner_count, greet_table)
    pl.semaphore_wait(barrier, seq_count + owner_count - 2)

    def x_copy(peer):
        return to_seq(x_ref, x_all.at[pos], x_send.at[peer], x_recv.at[pos], peer)

    def do_copy(peer):
        return to_seq(do_ref, do_all.at[pos], do_send.at[peer], do_recv.at[pos], peer)

    for load in loads[3:5]:
        load.wait()

    def send_x(i):
        x_copy(row_peer(i)).start()
        x_copy(col_peer(i)).start()

    def each_do(act):
        def one(r):
            peer = seq_peer(r)

            @pl.when(peer < pos)
            def _():
                act(do_copy(peer))

        each(1, seq_count, one)

    each(1, side, send_x)
    each_do(lambda copy: copy.start())

    def x_relay(block, peer):
        return to_seq(
            x_all.at[block], x_all.at[block], xr_send.at[block], x_recv.at[block], peer
        )

    def relay_x(i):
        for block, to_peer, first in ((row_peer(i), col_peer, 0), (col_peer(i), row_peer, 1)):
            x_relay(block, block).wait_recv()

            @pl.when((block // side) % 2 == first)
            def _():
                each(1, side, lambda k: x_relay(block, to_peer(k)).start())

    def end_relays(i):
        for block, to_peer, first in ((row_peer(i), col_peer, 0), (col_peer(i), row_peer, 1)):
            @pl.when((block // side) % 2 == first)
            def _():
                each(1, side, lambda k: x_relay(block, to_peer(k)).wait_send())

    eye = iota((LANES, LANES), 0) == iota((LANES, LANES), 1)

    def to_col(row):
        return jnp.sum(jnp.where(eye, row, 0.0), axis=1, keepdims=True)

    def to_row(col):
        return jnp.sum(jnp.where(eye, col, 0.0), axis=0, keepdims=True)

    for load in loads[:3]:
        load.wait()
    ids = ids_ref[...]
    high_col = to_col((ids // LANES).astype(F32))
    low_col = to_col((ids % LANES).astype(F32))
    id_rows = owner_ref.shape[0]
    local_ids = local_ref[...]
    parts = jnp.concatenate(
        [
            owner_ref[...].astype(F32).astype(BF16),
            (local_ids % 256).astype(F32).astype(BF16),
            (local_ids // 256).astype(F32).astype(BF16),
        ],
        axis=1,
    )
    pick = jnp.where(iota((tokens, id_rows), 1).astype(F32) == high_col, 1.0, 0.0).astype(BF16)
    found = dot(pick, parts)
    in_row = iota((tokens, LANES), 1).astype(F32) == low_col

    def column(part):
        piece = found[:, part * LANES : (part + 1) * LANES]
        return jnp.sum(jnp.where(in_row, piece, 0.0), axis=1, keepdims=True)

    owner_col = column(0)
    local_col = column(1) + 256.0 * column(2)
    owner_row = to_row(owner_col)
    before = (owner_col == owner_row) & (iota((tokens, tokens), 0) < iota((tokens, tokens), 1))
    slot_row = jnp.sum(jnp.where(before, 1.0, 0.0), axis=0, keepdims=True)
    slot_col = to_col(slot_row)
    target_row = owner_row * capacity + slot_row
    sendsel_ref[...] = jnp.where(
        iota((width, tokens), 0).astype(F32) == target_row, 1.0, 0.0
    ).astype(BF16)
    target_col = owner_col * capacity + slot_col
    recvsel_ref[...] = jnp.where(
        iota((tokens, width), 1).astype(F32) == target_col, 1.0, 0.0
    ).astype(BF16)
    lane_col = slot_col + (me * capacity).astype(F32)
    marks = jnp.where(iota((tokens, width), 1).astype(F32) == lane_col, local_col + 1.0, 0.0)

    def make_index(owner):
        line = jnp.sum(
            jnp.where(owner_col == owner.astype(F32), marks, 0.0), axis=0, keepdims=True
        )
        idx_send[owner] = jnp.broadcast_to(line, (8, width))

    each(0, owner_count, make_index)

    def idx_copy(peer):
        return to_table(
            idx_send.at[peer], idx_got.at[me], idx_ssem.at[peer], idx_rsem.at[me], peer
        )

    each(1, owner_count, lambda r: idx_copy(table_peer(r)).start())
    idx_got[me] = idx_send[me]

    for load in loads[5:6]:
        load.wait()
    x_all[pos] = x_ref[...]
    do_all[pos] = do_ref[...]
    own = dot(x_ref[...], proj_ref[...]).astype(BF16)
    own_ref[...] = own
    half_temper = jnp.asarray(0.5 * temper, BF16)
    scaled_ref[...] = own * half_temper
    scaled_do_ref[...] = do_ref[...] * half_temper

    lane = iota((1, LANES), 1)
    group = LANES // head_size
    span = group * tokens
    head_masks = [
        jnp.where(lane // head_size == g, 1.0, 0.0).astype(BF16) for g in range(group)
    ]

    def spread(block):
        return jnp.concatenate([block * m for m in head_masks], axis=0)

    def terms(half_scores, grad_dot, scale):
        slant = jnp.tanh(half_scores)
        gates = (1.0 + slant) * scale
        weights = (half_scores * gates).astype(BF16)
        score_grad = (grad_dot * (gates * (1.0 + half_scores * (1.0 - slant)))).astype(BF16)
        return weights, score_grad

    def put(ref, cols, value, first):
        if first:
            ref[:, cols] = value
        else:
            ref[:, cols] += value

    def over_columns(begin, end):
        held = begin(0)
        for c in range(features // LANES):
            after = begin(c + 1) if c + 1 < features // LANES else None
            end(c, *held)
            held = after

    def lanes_at(offset, c):
        return slice(offset + c * LANES, offset + (c + 1) * LANES)

    def query_pass(source, offset, scale, first):
        def begin(c):
            keys = spread(source[:, lanes_at(offset, c)])
            values = spread(source[:, lanes_at(offset + features, c)])
            cols = lanes_at(0, c)
            return keys, dot_nt(scaled_ref[:, cols], keys), dot_nt(scaled_do_ref[:, cols], values)

        def end(c, keys, half_scores, grad_dot):
            _, score_grad = terms(half_scores, grad_dot, scale)
            put(dq_ref, lanes_at(0, c), dot(score_grad, keys), first)

        over_columns(begin, end)

    def key_pass(source, block, scale, first):
        def begin(c):
            cols = lanes_at(0, c)
            queries = spread(source[:, cols])
            grads = spread(do_all[block, :, cols])
            return (
                queries,
                grads,
                dot_nt(scaled_ref[:, lanes_at(features, c)], queries),
                dot_nt(scaled_ref[:, lanes_at(2 * features, c)], grads),
            )

        def end(c, queries, grads, half_scores, grad_dot):
            weights, score_grad = terms(half_scores, grad_dot, scale)
            put(dk_ref, lanes_at(0, c), dot(score_grad, queries), first)
            put(dv_ref, lanes_at(0, c), dot(weights, grads), first)

        over_columns(begin, end)

    def visible(query_block, key_block):
        return jnp.where(mask_ref[query_block, key_block] == 1, history_scale, 0.0)

    def own_block():
        row_ids = iota((tokens, span), 0)
        lane_ids = iota((tokens, span), 1) % tokens
        query_pass(own_ref, features, jnp.where(lane_ids <= row_ids, history_scale, 0.0), True)
        key_pass(own_ref, pos, jnp.where(row_ids <= lane_ids, history_scale, 0.0), True)

    def block_step(r):
        block = seq_peer(r)
        in_row, in_col = block // side == my_row, block % side == my_col

        @pl.when(jnp.logical_not(in_row | in_col))
        def _():
            x_relay(block, block).wait_recv()

        @pl.when(block < pos)
        def _():
            other_ref[...] = dot(x_all[block], proj_ref[:, features:]).astype(BF16)
            query_pass(other_ref, 0, visible(pos, block), False)

        @pl.when(block > pos)
        def _():
            other_ref[:, :features] = dot(x_all[block], proj_ref[:, :features]).astype(BF16)
            to_seq(
                do_all.at[block], do_all.at[block], do_send.at[block], do_recv.at[block], block
            ).wait_recv()
            key_pass(other_ref, block, visible(block, pos), False)

    own_block()

    def take_index(r):
        peer = table_peer(r)
        to_table(
            idx_got.at[peer], idx_got.at[peer], idx_ssem.at[peer], idx_rsem.at[peer], peer
        ).wait_recv()

    each(1, owner_count, take_index)
    idx_all[pos] = jnp.sum(idx_got[...], axis=0)

    def idxf_copy(peer):
        return to_seq(idx_all.at[pos], idx_all.at[pos], idxf_ssem.at[peer], idxf_rsem.at[pos], peer)

    each(1, seq_count, lambda r: idxf_copy(seq_peer(r)).start())

    each(1, side, relay_x)

    slab_ids = iota((slab_rows, width), 0).astype(F32) + 1.0

    def select(block):
        select_ref[block] = jnp.where(
            slab_ids == idx_all[block][0:1, :], 1.0, 0.0
        ).astype(BF16)

    select(pos)
    slab_lanes = iota((LANES, slab_rows), 1).astype(F32) + 1.0
    for c in range(width // LANES):
        lanes = slice(c * LANES, (c + 1) * LANES)
        replysel_ref[lanes, :] = jnp.where(
            slab_lanes == to_col(idx_all[pos][0:1, lanes]), 1.0, 0.0
        ).astype(BF16)

    def select_other(r):
        block = seq_peer(r)
        to_seq(
            idx_all.at[block], idx_all.at[block], idxf_ssem.at[block], idxf_rsem.at[block], block
        ).wait_recv()
        select(block)

    each(1, seq_count, select_other)
    each(1, seq_count, block_step)

    stacked = jnp.concatenate(
        [dq_ref[...].astype(BF16), dk_ref[...].astype(BF16), dv_ref[...].astype(BF16)], axis=1
    )
    input_grad = dot_nt(stacked, proj_ref[...]).astype(BF16)
    send_buf[...] = dot(sendsel_ref[...], input_grad).astype(BF16)

    def row_copy(peer):
        return to_table(
            send_buf.at[rows_of(peer)], got.at[pos, rows_of(me)],
            row_ssem.at[peer], row_rsem.at[me], peer,
        )

    each(1, owner_count, lambda r: row_copy(table_peer(owner_count - r)).start())
    got[pos, rows_of(me)] = send_buf[rows_of(me)]

    def chunk(block, source, ssem, peer):
        part = got.at[block, rows_of(source)]
        return to_seq(part, part, ssem, fwd_rsem.at[block, source], peer)

    def forward(source):
        def one(i):
            chunk(pos, source, fwd_ssem.at[row_peer(i)], row_peer(i)).start()
            chunk(pos, source, fwd_ssem.at[col_peer(i)], col_peer(i)).start()

        each(1, side, one)

    near = owner_count // 2

    def each_diag(act):
        def one(r):
            peer = seq_peer(r)

            @pl.when(jnp.logical_not((peer // side == my_row) | (peer % side == my_col)))
            def _():
                act(peer)

        each(1, seq_count, one)

    def forward_far(source):
        forward(source)
        each_diag(lambda peer: chunk(pos, source, diag_ssem.at[peer], peer).start())

    def pass_chunk(source):
        def along(from_peer, to_peer):
            def one(i):
                block = from_peer(i)
                chunk(block, source, rel_ssem.at[block], block).wait_recv()
                each(
                    1, side,
                    lambda k: chunk(block, source, rel_ssem.at[block], to_peer(k)).start(),
                )

            each(1, side, one)

        @pl.when(source % 2 == 0)
        def _():
            along(row_peer, col_peer)

        @pl.when(source % 2 == 1)
        def _():
            along(col_peer, row_peer)

    forward(me)

    def take_chunk(r):
        source = table_peer(r)
        part = got.at[pos, rows_of(source)]
        to_table(part, part, row_ssem.at[source], row_rsem.at[source], source).wait_recv()
        return source

    def relay(r):
        forward(take_chunk(r))
        pass_chunk(table_peer(r - 1))

    each(1, near, relay)
    pass_chunk(table_peer(near - 1))
    each(near, owner_count, lambda r: forward_far(take_chunk(r)))

    grad_ref[...] = dot(select_ref[pos], got[pos])

    def add_block(r):
        block = seq_peer(r)
        in_row, in_col = block // side == my_row, block % side == my_col

        def await_chunk(r):
            source = table_peer(r)
            passed = (in_row & (source % 2 == 0)) | (in_col & (source % 2 == 1))

            @pl.when(jnp.logical_not(passed & (r < near)))
            def _():
                chunk(block, source, rel_ssem.at[block], block).wait_recv()

        each(0, owner_count, await_chunk)
        grad_ref[...] += dot(select_ref[block], got[block])

    each(1, seq_count, add_block)

    for load in loads[6:]:
        load.wait()
    for c in range(slab_rows // LANES):
        rows = slice(c * LANES, (c + 1) * LANES)
        grad = grad_ref[rows, :]
        new_moment = first_decay * moment_ref[rows, :] + (1.0 - first_decay) * grad
        mean_square = jnp.sum(grad * grad, axis=1, keepdims=True) * (1.0 / features)
        new_second = second_decay * to_col(second_ref[c : c + 1, :]) + (
            1.0 - second_decay
        ) * mean_square
        nsec_ref[c : c + 1, :] = to_row(new_second)
        nmom_ref[rows, :] = new_moment
        factor = step_rate / (jnp.sqrt(new_second) + epsilon)
        ntab_ref[rows, :] = (table_ref[rows, :].astype(F32) - new_moment * factor).astype(BF16)

    reply_buf[...] = dot(replysel_ref[...], ntab_ref[...]).astype(BF16)

    def reply_copy(peer):
        return to_table(
            reply_buf.at[rows_of(peer)], returned.at[rows_of(me)],
            rep_ssem.at[peer], rep_rsem.at[me], peer,
        )

    each(1, owner_count, lambda r: reply_copy(table_peer(r)).start())
    stores = [
        pltpu.make_async_copy(nmom_ref, nmom_hbm, store_sem.at[0]),
        pltpu.make_async_copy(ntab_ref, ntab_hbm, store_sem.at[1]),
        pltpu.make_async_copy(nsec_ref, nsec_hbm, store_sem.at[2]),
    ]
    for store in stores:
        store.start()
    returned[rows_of(me)] = reply_buf[rows_of(me)]

    each(1, seq_count, lambda r: idxf_copy(seq_peer(r)).wait_send())
    each_do(lambda copy: copy.wait_send())

    def end_seq(i):
        for peer in (row_peer(i), col_peer(i)):
            x_copy(peer).wait_send()
            to_seq(
                got.at[pos], got.at[pos], fwd_ssem.at[peer], fwd_rsem.at[pos, 0], peer
            ).wait_send()
            half = got.at[peer, pl.ds(0, width // 4)]
            for _ in range(side - 1):
                to_seq(
                    half, half, rel_ssem.at[peer], fwd_rsem.at[peer, 0], peer
                ).wait_send()

    each(1, side, end_seq)
    far = got.at[pos, pl.ds(0, width // 2)]
    each_diag(
        lambda peer: to_seq(
            far, far, diag_ssem.at[peer], fwd_rsem.at[pos, 0], peer
        ).wait_send()
    )
    each(1, side, end_relays)

    def end_table(r):
        peer = table_peer(r)
        idx_copy(peer).wait_send()
        row_copy(peer).wait_send()
        part = returned.at[rows_of(peer)]
        to_table(part, part, rep_ssem.at[peer], rep_rsem.at[peer], peer).wait_recv()

    each(1, owner_count, end_table)
    event_ref[...] = dot(recvsel_ref[...], returned[...]).astype(BF16)
    last = pltpu.make_async_copy(event_ref, event_hbm, store_sem.at[3])
    last.start()
    each(1, owner_count, lambda r: reply_copy(table_peer(r)).wait_send())
    for store in stores:
        store.wait()
    last.wait()


def pass_on(*refs):
    count = len(refs) // 3
    sources, targets, held = refs[:count], refs[count : 2 * count], refs[2 * count : 3 * count]
    in_sem, out_sem = refs[3 * count :]
    loads, stores = [], []
    for source, target, stage in zip(sources, targets, held):
        rows = source.shape[0]
        pieces = rows // LANES if rows > LANES else 1
        size = rows // pieces
        for piece in range(pieces):
            part = pl.ds(piece * size, size)
            number = len(loads)
            loads.append(
                pltpu.make_async_copy(source.at[part], stage.at[part], in_sem.at[number])
            )
            stores.append(
                pltpu.make_async_copy(stage.at[part], target.at[part], out_sem.at[number])
            )
    for load in loads:
        load.start()
    for load, store in zip(loads, stores):
        load.wait()
        store.start()
    for store in stores:
        store.wait()


def body(events_x, proj, out_grad, block_mask, item_ids, owner_of, local_of, table, moment, second):
    tokens, features = events_x.shape[1:]
    seq_count = lax.axis_size("seq")
    owner_count = lax.axis_size("table")
    slab_rows = table.shape[0]
    capacity = max(2 * tokens // owner_count, 16)
    width = owner_count * capacity
    smem = pl.BlockSpec(memory_space=pltpu.SMEM)
    hbm = pl.BlockSpec(memory_space=pl.ANY)
    dma = pltpu.SemaphoreType.DMA
    results = pl.pallas_call(
        functools.partial(kernel, seq_count, owner_count, capacity),
        out_shape=(
            jax.ShapeDtypeStruct((slab_rows, features), BF16),
            jax.ShapeDtypeStruct((slab_rows, features), F32),
            jax.ShapeDtypeStruct((slab_rows // LANES, LANES), F32),
            jax.ShapeDtypeStruct((tokens, features), BF16),
        ),
        in_specs=[hbm, hbm, hbm, smem] + [hbm] * 6,
        out_specs=(hbm,) * 4,
        scratch_shapes=[
            pltpu.VMEM((tokens, features), BF16),
            pltpu.VMEM((tokens, features), BF16),
            pltpu.VMEM((1, tokens), jnp.int32),
            pltpu.VMEM((owner_of.shape[0] // LANES, LANES), jnp.int32),
            pltpu.VMEM((owner_of.shape[0] // LANES, LANES), jnp.int32),
            pltpu.VMEM((slab_rows // LANES, LANES), F32),
            pltpu.VMEM((slab_rows // LANES, LANES), F32),
            pltpu.VMEM((tokens, features), BF16),
            pltpu.VMEM((width, features), BF16),
            pltpu.VMEM((tokens, width), BF16),
            pltpu.VMEM((seq_count, slab_rows, width), BF16),
            pltpu.VMEM((width, slab_rows), BF16),
            pltpu.VMEM((seq_count, tokens, features), BF16),
            pltpu.VMEM((seq_count, tokens, features), BF16),
            pltpu.VMEM(proj.shape, BF16),
            pltpu.VMEM((slab_rows, features), BF16),
            pltpu.VMEM((slab_rows, features), F32),
            pltpu.VMEM((slab_rows, features), BF16),
            pltpu.VMEM((slab_rows, features), F32),
            pltpu.VMEM((tokens, 3 * features), BF16),
            pltpu.VMEM((tokens, 3 * features), BF16),
            pltpu.VMEM((tokens, features), BF16),
            pltpu.VMEM((tokens, 2 * features), BF16),
            pltpu.VMEM((tokens, features), F32),
            pltpu.VMEM((tokens, features), F32),
            pltpu.VMEM((tokens, features), F32),
            pltpu.VMEM((width, tokens), BF16),
            pltpu.VMEM((owner_count, 8, width), F32),
            pltpu.VMEM((owner_count, 8, width), F32),
            pltpu.VMEM((seq_count, 8, width), F32),
            pltpu.VMEM((width, features), BF16),
            pltpu.VMEM((seq_count, width, features), BF16),
            pltpu.VMEM((slab_rows, features), F32),
            pltpu.VMEM((width, features), BF16),
            dma((9,)),
            dma((4,)),
            dma((seq_count,)),
            dma((seq_count,)),
            dma((seq_count,)),
            dma((seq_count,)),
            dma((owner_count,)),
            dma((owner_count,)),
            dma((seq_count,)),
            dma((seq_count,)),
            dma((owner_count,)),
            dma((owner_count,)),
            dma((seq_count,)),
            dma((seq_count, owner_count)),
            dma((owner_count,)),
            dma((owner_count,)),
            dma((seq_count,)),
            dma((seq_count,)),
            dma((seq_count,)),
        ],
        compiler_params=pltpu.CompilerParams(
            collective_id=0, has_side_effects=True, vmem_limit_bytes=VMEM_BYTES
        ),
    )(
        events_x[0],
        proj,
        out_grad[0],
        block_mask,
        item_ids,
        owner_of.reshape(-1, LANES),
        local_of.reshape(-1, LANES),
        table,
        moment,
        second.reshape(-1, LANES),
    )
    new_table, new_moment, new_second, event_rows = pl.pallas_call(
        pass_on,
        out_shape=tuple(jax.ShapeDtypeStruct(r.shape, r.dtype) for r in results),
        in_specs=[hbm] * 4,
        out_specs=(hbm,) * 4,
        scratch_shapes=[pltpu.VMEM(r.shape, r.dtype) for r in results]
        + [dma((2 * (slab_rows // LANES) + 2,))] * 2,
        compiler_params=pltpu.CompilerParams(vmem_limit_bytes=VMEM_BYTES),
    )(*results)
    return (new_table, new_moment, new_second.reshape(-1), event_rows[None])


def solution(mesh):
    return jax.shard_map(
        body,
        mesh=mesh,
        in_specs=(
            P("table", "seq", None),
            P(),
            P("table", "seq", None),
            P(),
            P("table", "seq"),
            P(),
            P(),
            P("table", None),
            P("table", None),
            P("table"),
        ),
        out_specs=(P("table", None), P("table", None), P("table"), P("table", "seq", None)),
        check_vma=False,
    )
```

```python
import functools
import math

import jax
import jax.numpy as jnp
from jax import lax
from jax.experimental import pallas as pl
from jax.experimental.pallas import tpu as pltpu
from jax.sharding import PartitionSpec as P

HEADS = 8
LANES = 128
VMEM_BYTES = 63 * 1024 * 1024

first_decay = 0.9
second_decay = 0.99
step_rate = 0.05
epsilon = 1e-08

F32 = jnp.float32
BF16 = jnp.bfloat16
MESH = pl.DeviceIdType.MESH


def iota(shape, axis):
    return lax.broadcasted_iota(jnp.int32, shape, axis)


def dot(a, b):
    return jnp.dot(a, b, preferred_element_type=F32)


def dot_nt(a, b):
    return lax.dot_general(a, b, (((1,), (1,)), ((), ())), preferred_element_type=F32)


def kernel(
    seq_count, owner_count, capacity,
    x_hbm, proj_hbm, do_hbm, mask_ref, ids_hbm, owner_hbm, local_hbm, table_hbm, moment_hbm, second_hbm,
    ntab_hbm, nmom_hbm, nsec_hbm, event_hbm,
    x_ref, do_ref, ids_ref, owner_ref, local_ref, second_ref, nsec_ref, event_ref, returned, recvsel_ref, select_ref, replysel_ref,
    x_all, do_all, proj_ref, table_ref, moment_ref, ntab_ref, nmom_ref,
    own_ref, scaled_ref, scaled_do_ref, other_ref, dq_ref, dk_ref, dv_ref, sendsel_ref,
    idx_send, idx_got, idx_all, send_buf, got, grad_ref, reply_buf,
    load_sem, store_sem, x_send, x_recv, do_send, do_recv, idx_ssem, idx_rsem, idxf_ssem, idxf_rsem,
    row_ssem, row_rsem, fwd_ssem, fwd_rsem, rep_ssem, rep_rsem, rel_ssem, xr_send, diag_ssem,
):
    pos = lax.axis_index("seq")
    me = lax.axis_index("table")
    tokens, features = x_ref.shape
    head_size = features // HEADS
    slab_rows = table_ref.shape[0]
    width = owner_count * capacity
    history_scale = 1.0 / math.sqrt(tokens * seq_count)
    temper = 1.0 / math.sqrt(head_size)
    turn = 1 - 2 * (pos % 2)
    side = math.isqrt(seq_count)
    my_row, my_col = pos // side, pos % side

    def row_peer(i):
        return my_row * side + lax.rem(my_col + i, side)

    def col_peer(i):
        return lax.rem(my_row + i, side) * side + my_col

    def seq_peer(r):
        return lax.rem(pos + turn * r + seq_count, seq_count)

    def table_peer(r):
        peer, bit = 0, 1
        while bit < owner_count:
            mine, other = (me // bit) % 2, (r // bit) % 2
            peer = peer + bit * (mine + other - 2 * mine * other)
            bit *= 2
        return peer

    def rows_of(owner):
        return pl.ds(pl.multiple_of(owner * capacity, capacity), capacity)

    def to_seq(src, dst, ssem, rsem, peer):
        return pltpu.make_async_remote_copy(
            src_ref=src, dst_ref=dst, send_sem=ssem, recv_sem=rsem,
            device_id=(peer, me), device_id_type=MESH,
        )

    def to_table(src, dst, ssem, rsem, peer):
        return pltpu.make_async_remote_copy(
            src_ref=src, dst_ref=dst, send_sem=ssem, recv_sem=rsem,
            device_id=(pos, peer), device_id_type=MESH,
        )

    def each(first, last, step):
        lax.fori_loop(first, last, lambda r, c: (step(r), c)[1], 0)

    loads = [
        pltpu.make_async_copy(source, target, load_sem.at[number])
        for number, (source, target) in enumerate(
            [
                (ids_hbm, ids_ref),
                (owner_hbm, owner_ref),
                (local_hbm, local_ref),
                (x_hbm, x_ref),
                (do_hbm, do_ref),
                (proj_hbm, proj_ref),
                (table_hbm, table_ref),
                (moment_hbm, moment_ref),
                (second_hbm, second_ref),
            ]
        )
    ]
    for load in loads:
        load.start()

    barrier = pltpu.get_barrier_semaphore()

    def greet_seq(r):
        pl.semaphore_signal(barrier, inc=1, device_id=(seq_peer(r), me), device_id_type=MESH)

    def greet_table(r):
        pl.semaphore_signal(barrier, inc=1, device_id=(pos, table_peer(r)), device_id_type=MESH)

    each(1, seq_count, greet_seq)
    each(1, owner_count, greet_table)
    pl.semaphore_wait(barrier, seq_count + owner_count - 2)

    def x_copy(peer):
        return to_seq(x_ref, x_all.at[pos], x_send.at[peer], x_recv.at[pos], peer)

    def do_copy(peer):
        return to_seq(do_ref, do_all.at[pos], do_send.at[peer], do_recv.at[pos], peer)

    for load in loads[3:5]:
        load.wait()

    def send_x(i):
        x_copy(row_peer(i)).start()
        x_copy(col_peer(i)).start()

    def each_do(act):
        def one(r):
            peer = seq_peer(r)

            @pl.when(peer < pos)
            def _():
                act(do_copy(peer))

        each(1, seq_count, one)

    each(1, side, send_x)
    each_do(lambda copy: copy.start())

    def x_relay(block, peer):
        return to_seq(
            x_all.at[block], x_all.at[block], xr_send.at[block], x_recv.at[block], peer
        )

    def relay_x(i):
        for block, to_peer, first in ((row_peer(i), col_peer, 0), (col_peer(i), row_peer, 1)):
            x_relay(block, block).wait_recv()

            @pl.when((block // side) % 2 == first)
            def _():
                each(1, side, lambda k: x_relay(block, to_peer(k)).start())

    def end_relays(i):
        for block, to_peer, first in ((row_peer(i), col_peer, 0), (col_peer(i), row_peer, 1)):
            @pl.when((block // side) % 2 == first)
            def _():
                each(1, side, lambda k: x_relay(block, to_peer(k)).wait_send())

    eye = iota((LANES, LANES), 0) == iota((LANES, LANES), 1)

    def to_col(row):
        return jnp.sum(jnp.where(eye, row, 0.0), axis=1, keepdims=True)

    def to_row(col):
        return jnp.sum(jnp.where(eye, col, 0.0), axis=0, keepdims=True)

    for load in loads[:3]:
        load.wait()
    ids = ids_ref[...]
    high_col = to_col((ids // LANES).astype(F32))
    low_col = to_col((ids % LANES).astype(F32))
    id_rows = owner_ref.shape[0]
    local_ids = local_ref[...]
    parts = jnp.concatenate(
        [
            owner_ref[...].astype(F32).astype(BF16),
            (local_ids % 256).astype(F32).astype(BF16),
            (local_ids // 256).astype(F32).astype(BF16),
        ],
        axis=1,
    )
    pick = jnp.where(iota((tokens, id_rows), 1).astype(F32) == high_col, 1.0, 0.0).astype(BF16)
    found = dot(pick, parts)
    in_row = iota((tokens, LANES), 1).astype(F32) == low_col

    def column(part):
        piece = found[:, part * LANES : (part + 1) * LANES]
        return jnp.sum(jnp.where(in_row, piece, 0.0), axis=1, keepdims=True)

    owner_col = column(0)
    local_col = column(1) + 256.0 * column(2)
    owner_row = to_row(owner_col)
    before = (owner_col == owner_row) & (iota((tokens, tokens), 0) < iota((tokens, tokens), 1))
    slot_row = jnp.sum(jnp.where(before, 1.0, 0.0), axis=0, keepdims=True)
    slot_col = to_col(slot_row)
    target_row = owner_row * capacity + slot_row
    sendsel_ref[...] = jnp.where(
        iota((width, tokens), 0).astype(F32) == target_row, 1.0, 0.0
    ).astype(BF16)
    target_col = owner_col * capacity + slot_col
    recvsel_ref[...] = jnp.where(
        iota((tokens, width), 1).astype(F32) == target_col, 1.0, 0.0
    ).astype(BF16)
    lane_col = slot_col + (me * capacity).astype(F32)
    marks = jnp.where(iota((tokens, width), 1).astype(F32) == lane_col, local_col + 1.0, 0.0)

    def make_index(owner):
        line = jnp.sum(
            jnp.where(owner_col == owner.astype(F32), marks, 0.0), axis=0, keepdims=True
        )
        idx_send[owner] = jnp.broadcast_to(line, (8, width))

    each(0, owner_count, make_index)

    def idx_copy(peer):
        return to_table(
            idx_send.at[peer], idx_got.at[me], idx_ssem.at[peer], idx_rsem.at[me], peer
        )

    each(1, owner_count, lambda r: idx_copy(table_peer(r)).start())
    idx_got[me] = idx_send[me]

    for load in loads[5:6]:
        load.wait()
    x_all[pos] = x_ref[...]
    do_all[pos] = do_ref[...]
    own = dot(x_ref[...], proj_ref[...]).astype(BF16)
    own_ref[...] = own
    half_temper = jnp.asarray(0.5 * temper, BF16)
    scaled_ref[...] = own * half_temper
    scaled_do_ref[...] = do_ref[...] * half_temper

    lane = iota((1, LANES), 1)
    group = LANES // head_size
    span = group * tokens
    head_masks = [
        jnp.where(lane // head_size == g, 1.0, 0.0).astype(BF16) for g in range(group)
    ]

    def spread(block):
        return jnp.concatenate([block * m for m in head_masks], axis=0)

    def terms(half_scores, grad_dot, scale):
        slant = jnp.tanh(half_scores)
        gates = (1.0 + slant) * scale
        weights = (half_scores * gates).astype(BF16)
        score_grad = (grad_dot * (gates * (1.0 + half_scores * (1.0 - slant)))).astype(BF16)
        return weights, score_grad

    def put(ref, cols, value, first):
        if first:
            ref[:, cols] = value
        else:
            ref[:, cols] += value

    def over_columns(begin, end):
        held = begin(0)
        for c in range(features // LANES):
            after = begin(c + 1) if c + 1 < features // LANES else None
            end(c, *held)
            held = after

    def lanes_at(offset, c):
        return slice(offset + c * LANES, offset + (c + 1) * LANES)

    def query_pass(source, offset, scale, first):
        def begin(c):
            keys = spread(source[:, lanes_at(offset, c)])
            values = spread(source[:, lanes_at(offset + features, c)])
            cols = lanes_at(0, c)
            return keys, dot_nt(scaled_ref[:, cols], keys), dot_nt(scaled_do_ref[:, cols], values)

        def end(c, keys, half_scores, grad_dot):
            _, score_grad = terms(half_scores, grad_dot, scale)
            put(dq_ref, lanes_at(0, c), dot(score_grad, keys), first)

        over_columns(begin, end)

    def key_pass(source, block, scale, first):
        def begin(c):
            cols = lanes_at(0, c)
            queries = spread(source[:, cols])
            grads = spread(do_all[block, :, cols])
            return (
                queries,
                grads,
                dot_nt(scaled_ref[:, lanes_at(features, c)], queries),
                dot_nt(scaled_ref[:, lanes_at(2 * features, c)], grads),
            )

        def end(c, queries, grads, half_scores, grad_dot):
            weights, score_grad = terms(half_scores, grad_dot, scale)
            put(dk_ref, lanes_at(0, c), dot(score_grad, queries), first)
            put(dv_ref, lanes_at(0, c), dot(weights, grads), first)

        over_columns(begin, end)

    def visible(query_block, key_block):
        return jnp.where(mask_ref[query_block, key_block] == 1, history_scale, 0.0)

    def own_block():
        row_ids = iota((tokens, span), 0)
        lane_ids = iota((tokens, span), 1) % tokens
        query_pass(own_ref, features, jnp.where(lane_ids <= row_ids, history_scale, 0.0), True)
        key_pass(own_ref, pos, jnp.where(row_ids <= lane_ids, history_scale, 0.0), True)

    def block_step(r):
        block = seq_peer(r)
        in_row, in_col = block // side == my_row, block % side == my_col

        @pl.when(jnp.logical_not(in_row | in_col))
        def _():
            x_relay(block, block).wait_recv()

        @pl.when(block < pos)
        def _():
            other_ref[...] = dot(x_all[block], proj_ref[:, features:]).astype(BF16)
            query_pass(other_ref, 0, visible(pos, block), False)

        @pl.when(block > pos)
        def _():
            other_ref[:, :features] = dot(x_all[block], proj_ref[:, :features]).astype(BF16)
            to_seq(
                do_all.at[block], do_all.at[block], do_send.at[block], do_recv.at[block], block
            ).wait_recv()
            key_pass(other_ref, block, visible(block, pos), False)

    own_block()

    def take_index(r):
        peer = table_peer(r)
        to_table(
            idx_got.at[peer], idx_got.at[peer], idx_ssem.at[peer], idx_rsem.at[peer], peer
        ).wait_recv()

    each(1, owner_count, take_index)
    idx_all[pos] = jnp.sum(idx_got[...], axis=0)

    def idxf_copy(peer):
        return to_seq(idx_all.at[pos], idx_all.at[pos], idxf_ssem.at[peer], idxf_rsem.at[pos], peer)

    each(1, seq_count, lambda r: idxf_copy(seq_peer(r)).start())

    each(1, side, relay_x)
    each(1, seq_count, block_step)

    stacked = jnp.concatenate(
        [dq_ref[...].astype(BF16), dk_ref[...].astype(BF16), dv_ref[...].astype(BF16)], axis=1
    )
    input_grad = dot_nt(stacked, proj_ref[...]).astype(BF16)
    send_buf[...] = dot(sendsel_ref[...], input_grad).astype(BF16)

    def row_copy(peer):
        return to_table(
            send_buf.at[rows_of(peer)], got.at[pos, rows_of(me)],
            row_ssem.at[peer], row_rsem.at[me], peer,
        )

    each(1, owner_count, lambda r: row_copy(table_peer(owner_count - r)).start())
    got[pos, rows_of(me)] = send_buf[rows_of(me)]

    def chunk(block, source, ssem, peer):
        part = got.at[block, rows_of(source)]
        return to_seq(part, part, ssem, fwd_rsem.at[block, source], peer)

    def forward(source):
        def one(i):
            chunk(pos, source, fwd_ssem.at[row_peer(i)], row_peer(i)).start()
            chunk(pos, source, fwd_ssem.at[col_peer(i)], col_peer(i)).start()

        each(1, side, one)

    near = owner_count // 2

    def each_diag(act):
        def one(r):
            peer = seq_peer(r)

            @pl.when(jnp.logical_not((peer // side == my_row) | (peer % side == my_col)))
            def _():
                act(peer)

        each(1, seq_count, one)

    def forward_far(source):
        forward(source)
        each_diag(lambda peer: chunk(pos, source, diag_ssem.at[peer], peer).start())

    def pass_chunk(source):
        def along(from_peer, to_peer):
            def one(i):
                block = from_peer(i)
                chunk(block, source, rel_ssem.at[block], block).wait_recv()
                each(
                    1, side,
                    lambda k: chunk(block, source, rel_ssem.at[block], to_peer(k)).start(),
                )

            each(1, side, one)

        @pl.when(source % 2 == 0)
        def _():
            along(row_peer, col_peer)

        @pl.when(source % 2 == 1)
        def _():
            along(col_peer, row_peer)

    forward(me)

    def take_chunk(r):
        source = table_peer(r)
        part = got.at[pos, rows_of(source)]
        to_table(part, part, row_ssem.at[source], row_rsem.at[source], source).wait_recv()
        return source

    def relay(r):
        forward(take_chunk(r))
        pass_chunk(table_peer(r - 1))

    each(1, near, relay)
    pass_chunk(table_peer(near - 1))

    slab_ids = iota((slab_rows, width), 0).astype(F32) + 1.0

    def select(block):
        select_ref[block] = jnp.where(
            slab_ids == idx_all[block][0:1, :], 1.0, 0.0
        ).astype(BF16)

    select(pos)
    slab_lanes = iota((LANES, slab_rows), 1).astype(F32) + 1.0
    for c in range(width // LANES):
        lanes = slice(c * LANES, (c + 1) * LANES)
        replysel_ref[lanes, :] = jnp.where(
            slab_lanes == to_col(idx_all[pos][0:1, lanes]), 1.0, 0.0
        ).astype(BF16)

    def select_other(r):
        block = seq_peer(r)
        to_seq(
            idx_all.at[block], idx_all.at[block], idxf_ssem.at[block], idxf_rsem.at[block], block
        ).wait_recv()
        select(block)

    each(1, seq_count, select_other)

    each(near, owner_count, lambda r: forward_far(take_chunk(r)))

    grad_ref[...] = dot(select_ref[pos], got[pos])

    def add_block(r):
        block = seq_peer(r)
        in_row, in_col = block // side == my_row, block % side == my_col

        def await_chunk(r):
            source = table_peer(r)
            passed = (in_row & (source % 2 == 0)) | (in_col & (source % 2 == 1))

            @pl.when(jnp.logical_not(passed & (r < near)))
            def _():
                chunk(block, source, rel_ssem.at[block], block).wait_recv()

        each(0, owner_count, await_chunk)
        grad_ref[...] += dot(select_ref[block], got[block])

    each(1, seq_count, add_block)

    for load in loads[6:]:
        load.wait()
    for c in range(slab_rows // LANES):
        rows = slice(c * LANES, (c + 1) * LANES)
        grad = grad_ref[rows, :]
        new_moment = first_decay * moment_ref[rows, :] + (1.0 - first_decay) * grad
        mean_square = jnp.sum(grad * grad, axis=1, keepdims=True) * (1.0 / features)
        new_second = second_decay * to_col(second_ref[c : c + 1, :]) + (
            1.0 - second_decay
        ) * mean_square
        nsec_ref[c : c + 1, :] = to_row(new_second)
        nmom_ref[rows, :] = new_moment
        factor = step_rate / (jnp.sqrt(new_second) + epsilon)
        ntab_ref[rows, :] = (table_ref[rows, :].astype(F32) - new_moment * factor).astype(BF16)

    reply_buf[...] = dot(replysel_ref[...], ntab_ref[...]).astype(BF16)

    def reply_copy(peer):
        return to_table(
            reply_buf.at[rows_of(peer)], returned.at[rows_of(me)],
            rep_ssem.at[peer], rep_rsem.at[me], peer,
        )

    each(1, owner_count, lambda r: reply_copy(table_peer(owner_count - r)).start())
    stores = [
        pltpu.make_async_copy(nmom_ref, nmom_hbm, store_sem.at[0]),
        pltpu.make_async_copy(ntab_ref, ntab_hbm, store_sem.at[1]),
        pltpu.make_async_copy(nsec_ref, nsec_hbm, store_sem.at[2]),
    ]
    for store in stores:
        store.start()
    returned[rows_of(me)] = reply_buf[rows_of(me)]

    each(1, seq_count, lambda r: idxf_copy(seq_peer(r)).wait_send())
    each_do(lambda copy: copy.wait_send())

    def end_seq(i):
        for peer in (row_peer(i), col_peer(i)):
            x_copy(peer).wait_send()
            to_seq(
                got.at[pos], got.at[pos], fwd_ssem.at[peer], fwd_rsem.at[pos, 0], peer
            ).wait_send()
            half = got.at[peer, pl.ds(0, width // 4)]
            for _ in range(side - 1):
                to_seq(
                    half, half, rel_ssem.at[peer], fwd_rsem.at[peer, 0], peer
                ).wait_send()

    each(1, side, end_seq)
    far = got.at[pos, pl.ds(0, width // 2)]
    each_diag(
        lambda peer: to_seq(
            far, far, diag_ssem.at[peer], fwd_rsem.at[pos, 0], peer
        ).wait_send()
    )
    each(1, side, end_relays)

    def end_table(r):
        peer = table_peer(r)
        idx_copy(peer).wait_send()
        row_copy(peer).wait_send()
        part = returned.at[rows_of(peer)]
        to_table(part, part, rep_ssem.at[peer], rep_rsem.at[peer], peer).wait_recv()

    each(1, owner_count, end_table)
    event_ref[...] = dot(recvsel_ref[...], returned[...]).astype(BF16)
    last = pltpu.make_async_copy(event_ref, event_hbm, store_sem.at[3])
    last.start()
    each(1, owner_count, lambda r: reply_copy(table_peer(r)).wait_send())
    for store in stores:
        store.wait()
    last.wait()


def pass_on(*refs):
    count = len(refs) // 3
    sources, targets, held = refs[:count], refs[count : 2 * count], refs[2 * count : 3 * count]
    in_sem, out_sem = refs[3 * count :]
    loads, stores = [], []
    for source, target, stage in zip(sources, targets, held):
        rows = source.shape[0]
        pieces = rows // LANES if rows > LANES else 1
        size = rows // pieces
        for piece in range(pieces):
            part = pl.ds(piece * size, size)
            number = len(loads)
            loads.append(
                pltpu.make_async_copy(source.at[part], stage.at[part], in_sem.at[number])
            )
            stores.append(
                pltpu.make_async_copy(stage.at[part], target.at[part], out_sem.at[number])
            )
    for load in loads:
        load.start()
    for load, store in zip(loads, stores):
        load.wait()
        store.start()
    for store in stores:
        store.wait()


def body(events_x, proj, out_grad, block_mask, item_ids, owner_of, local_of, table, moment, second):
    tokens, features = events_x.shape[1:]
    seq_count = lax.axis_size("seq")
    owner_count = lax.axis_size("table")
    slab_rows = table.shape[0]
    capacity = max(2 * tokens // owner_count, 16)
    width = owner_count * capacity
    smem = pl.BlockSpec(memory_space=pltpu.SMEM)
    hbm = pl.BlockSpec(memory_space=pl.ANY)
    dma = pltpu.SemaphoreType.DMA
    results = pl.pallas_call(
        functools.partial(kernel, seq_count, owner_count, capacity),
        out_shape=(
            jax.ShapeDtypeStruct((slab_rows, features), BF16),
            jax.ShapeDtypeStruct((slab_rows, features), F32),
            jax.ShapeDtypeStruct((slab_rows // LANES, LANES), F32),
            jax.ShapeDtypeStruct((tokens, features), BF16),
        ),
        in_specs=[hbm, hbm, hbm, smem] + [hbm] * 6,
        out_specs=(hbm,) * 4,
        scratch_shapes=[
            pltpu.VMEM((tokens, features), BF16),
            pltpu.VMEM((tokens, features), BF16),
            pltpu.VMEM((1, tokens), jnp.int32),
            pltpu.VMEM((owner_of.shape[0] // LANES, LANES), jnp.int32),
            pltpu.VMEM((owner_of.shape[0] // LANES, LANES), jnp.int32),
            pltpu.VMEM((slab_rows // LANES, LANES), F32),
            pltpu.VMEM((slab_rows // LANES, LANES), F32),
            pltpu.VMEM((tokens, features), BF16),
            pltpu.VMEM((width, features), BF16),
            pltpu.VMEM((tokens, width), BF16),
            pltpu.VMEM((seq_count, slab_rows, width), BF16),
            pltpu.VMEM((width, slab_rows), BF16),
            pltpu.VMEM((seq_count, tokens, features), BF16),
            pltpu.VMEM((seq_count, tokens, features), BF16),
            pltpu.VMEM(proj.shape, BF16),
            pltpu.VMEM((slab_rows, features), BF16),
            pltpu.VMEM((slab_rows, features), F32),
            pltpu.VMEM((slab_rows, features), BF16),
            pltpu.VMEM((slab_rows, features), F32),
            pltpu.VMEM((tokens, 3 * features), BF16),
            pltpu.VMEM((tokens, 3 * features), BF16),
            pltpu.VMEM((tokens, features), BF16),
            pltpu.VMEM((tokens, 2 * features), BF16),
            pltpu.VMEM((tokens, features), F32),
            pltpu.VMEM((tokens, features), F32),
            pltpu.VMEM((tokens, features), F32),
            pltpu.VMEM((width, tokens), BF16),
            pltpu.VMEM((owner_count, 8, width), F32),
            pltpu.VMEM((owner_count, 8, width), F32),
            pltpu.VMEM((seq_count, 8, width), F32),
            pltpu.VMEM((width, features), BF16),
            pltpu.VMEM((seq_count, width, features), BF16),
            pltpu.VMEM((slab_rows, features), F32),
            pltpu.VMEM((width, features), BF16),
            dma((9,)),
            dma((4,)),
            dma((seq_count,)),
            dma((seq_count,)),
            dma((seq_count,)),
            dma((seq_count,)),
            dma((owner_count,)),
            dma((owner_count,)),
            dma((seq_count,)),
            dma((seq_count,)),
            dma((owner_count,)),
            dma((owner_count,)),
            dma((seq_count,)),
            dma((seq_count, owner_count)),
            dma((owner_count,)),
            dma((owner_count,)),
            dma((seq_count,)),
            dma((seq_count,)),
            dma((seq_count,)),
        ],
        compiler_params=pltpu.CompilerParams(
            collective_id=0, has_side_effects=True, vmem_limit_bytes=VMEM_BYTES
        ),
    )(
        events_x[0],
        proj,
        out_grad[0],
        block_mask,
        item_ids,
        owner_of.reshape(-1, LANES),
        local_of.reshape(-1, LANES),
        table,
        moment,
        second.reshape(-1, LANES),
    )
    new_table, new_moment, new_second, event_rows = pl.pallas_call(
        pass_on,
        out_shape=tuple(jax.ShapeDtypeStruct(r.shape, r.dtype) for r in results),
        in_specs=[hbm] * 4,
        out_specs=(hbm,) * 4,
        scratch_shapes=[pltpu.VMEM(r.shape, r.dtype) for r in results]
        + [dma((2 * (slab_rows // LANES) + 2,))] * 2,
        compiler_params=pltpu.CompilerParams(vmem_limit_bytes=VMEM_BYTES),
    )(*results)
    return (new_table, new_moment, new_second.reshape(-1), event_rows[None])


def solution(mesh):
    return jax.shard_map(
        body,
        mesh=mesh,
        in_specs=(
            P("table", "seq", None),
            P(),
            P("table", "seq", None),
            P(),
            P("table", "seq"),
            P(),
            P(),
            P("table", None),
            P("table", None),
            P("table"),
        ),
        out_specs=(P("table", None), P("table", None), P("table"), P("table", "seq", None)),
        check_vma=False,
    )
```

```python
import functools
import math

import jax
import jax.numpy as jnp
from jax import lax
from jax.experimental import pallas as pl
from jax.experimental.pallas import tpu as pltpu
from jax.sharding import PartitionSpec as P

HEADS = 8
LANES = 128
VMEM_BYTES = 63 * 1024 * 1024

first_decay = 0.9
second_decay = 0.99
step_rate = 0.05
epsilon = 1e-08

F32 = jnp.float32
BF16 = jnp.bfloat16
MESH = pl.DeviceIdType.MESH


def iota(shape, axis):
    return lax.broadcasted_iota(jnp.int32, shape, axis)


def dot(a, b):
    return jnp.dot(a, b, preferred_element_type=F32)


def dot_nt(a, b):
    return lax.dot_general(a, b, (((1,), (1,)), ((), ())), preferred_element_type=F32)


def kernel(
    seq_count, owner_count, capacity,
    x_hbm, proj_hbm, do_hbm, mask_ref, ids_hbm, owner_hbm, local_hbm, table_hbm, moment_hbm, second_hbm,
    ntab_hbm, nmom_hbm, nsec_hbm, event_hbm,
    x_ref, do_ref, ids_ref, owner_ref, local_ref, second_ref, nsec_ref, event_ref, returned, recvsel_ref, select_ref, replysel_ref,
    x_all, do_all, proj_ref, table_ref, moment_ref, ntab_ref, nmom_ref,
    own_ref, scaled_ref, scaled_do_ref, other_ref, dq_ref, dk_ref, dv_ref, sendsel_ref,
    idx_send, idx_got, idx_all, send_buf, got, grad_ref, reply_buf,
    load_sem, store_sem, x_send, x_recv, do_send, do_recv, idx_ssem, idx_rsem, idxf_ssem, idxf_rsem,
    row_ssem, row_rsem, fwd_ssem, fwd_rsem, rep_ssem, rep_rsem, rel_ssem, xr_send, diag_ssem,
):
    pos = lax.axis_index("seq")
    me = lax.axis_index("table")
    tokens, features = x_ref.shape
    head_size = features // HEADS
    slab_rows = table_ref.shape[0]
    width = owner_count * capacity
    history_scale = 1.0 / math.sqrt(tokens * seq_count)
    temper = 1.0 / math.sqrt(head_size)
    turn = 1 - 2 * (pos % 2)
    side = math.isqrt(seq_count)
    my_row, my_col = pos // side, pos % side

    def row_peer(i):
        return my_row * side + lax.rem(my_col + i, side)

    def col_peer(i):
        return lax.rem(my_row + i, side) * side + my_col

    def seq_peer(r):
        return lax.rem(pos + turn * r + seq_count, seq_count)

    def table_peer(r):
        peer, bit = 0, 1
        while bit < owner_count:
            mine, other = (me // bit) % 2, (r // bit) % 2
            peer = peer + bit * (mine + other - 2 * mine * other)
            bit *= 2
        return peer

    def rows_of(owner):
        return pl.ds(pl.multiple_of(owner * capacity, capacity), capacity)

    def to_seq(src, dst, ssem, rsem, peer):
        return pltpu.make_async_remote_copy(
            src_ref=src, dst_ref=dst, send_sem=ssem, recv_sem=rsem,
            device_id=(peer, me), device_id_type=MESH,
        )

    def to_table(src, dst, ssem, rsem, peer):
        return pltpu.make_async_remote_copy(
            src_ref=src, dst_ref=dst, send_sem=ssem, recv_sem=rsem,
            device_id=(pos, peer), device_id_type=MESH,
        )

    def each(first, last, step):
        lax.fori_loop(first, last, lambda r, c: (step(r), c)[1], 0)

    loads = [
        pltpu.make_async_copy(source, target, load_sem.at[number])
        for number, (source, target) in enumerate(
            [
                (ids_hbm, ids_ref),
                (owner_hbm, owner_ref),
                (local_hbm, local_ref),
                (x_hbm, x_ref),
                (do_hbm, do_ref),
                (proj_hbm, proj_ref),
                (table_hbm, table_ref),
                (moment_hbm, moment_ref),
                (second_hbm, second_ref),
            ]
        )
    ]
    for load in loads:
        load.start()

    barrier = pltpu.get_barrier_semaphore()

    def greet_seq(r):
        pl.semaphore_signal(barrier, inc=1, device_id=(seq_peer(r), me), device_id_type=MESH)

    def greet_table(r):
        pl.semaphore_signal(barrier, inc=1, device_id=(pos, table_peer(r)), device_id_type=MESH)

    each(1, seq_count, greet_seq)
    each(1, owner_count, greet_table)
    pl.semaphore_wait(barrier, seq_count + owner_count - 2)

    def x_copy(peer):
        return to_seq(x_ref, x_all.at[pos], x_send.at[peer], x_recv.at[pos], peer)

    def do_copy(peer):
        return to_seq(do_ref, do_all.at[pos], do_send.at[peer], do_recv.at[pos], peer)

    for load in loads[3:5]:
        load.wait()

    def send_x(i):
        x_copy(row_peer(i)).start()
        x_copy(col_peer(i)).start()

    def each_do(act):
        def one(r):
            peer = seq_peer(r)

            @pl.when(peer < pos)
            def _():
                act(do_copy(peer))

        each(1, seq_count, one)

    each(1, side, send_x)
    each_do(lambda copy: copy.start())

    def x_relay(block, peer):
        return to_seq(
            x_all.at[block], x_all.at[block], xr_send.at[block], x_recv.at[block], peer
        )

    def relay_x(i):
        for block, to_peer, first in ((row_peer(i), col_peer, 0), (col_peer(i), row_peer, 1)):
            x_relay(block, block).wait_recv()

            @pl.when((block // side) % 2 == first)
            def _():
                each(1, side, lambda k: x_relay(block, to_peer(k)).start())

    def end_relays(i):
        for block, to_peer, first in ((row_peer(i), col_peer, 0), (col_peer(i), row_peer, 1)):
            @pl.when((block // side) % 2 == first)
            def _():
                each(1, side, lambda k: x_relay(block, to_peer(k)).wait_send())

    eye = iota((LANES, LANES), 0) == iota((LANES, LANES), 1)

    def to_col(row):
        return jnp.sum(jnp.where(eye, row, 0.0), axis=1, keepdims=True)

    def to_row(col):
        return jnp.sum(jnp.where(eye, col, 0.0), axis=0, keepdims=True)

    for load in loads[:3]:
        load.wait()
    ids = ids_ref[...]
    high_col = to_col((ids // LANES).astype(F32))
    low_col = to_col((ids % LANES).astype(F32))
    id_rows = owner_ref.shape[0]
    local_ids = local_ref[...]
    parts = jnp.concatenate(
        [
            owner_ref[...].astype(F32).astype(BF16),
            (local_ids % 256).astype(F32).astype(BF16),
            (local_ids // 256).astype(F32).astype(BF16),
        ],
        axis=1,
    )
    pick = jnp.where(iota((tokens, id_rows), 1).astype(F32) == high_col, 1.0, 0.0).astype(BF16)
    found = dot(pick, parts)
    in_row = iota((tokens, LANES), 1).astype(F32) == low_col

    def column(part):
        piece = found[:, part * LANES : (part + 1) * LANES]
        return jnp.sum(jnp.where(in_row, piece, 0.0), axis=1, keepdims=True)

    owner_col = column(0)
    local_col = column(1) + 256.0 * column(2)
    owner_row = to_row(owner_col)
    before = (owner_col == owner_row) & (iota((tokens, tokens), 0) < iota((tokens, tokens), 1))
    slot_row = jnp.sum(jnp.where(before, 1.0, 0.0), axis=0, keepdims=True)
    slot_col = to_col(slot_row)
    target_row = owner_row * capacity + slot_row
    sendsel_ref[...] = jnp.where(
        iota((width, tokens), 0).astype(F32) == target_row, 1.0, 0.0
    ).astype(BF16)
    target_col = owner_col * capacity + slot_col
    recvsel_ref[...] = jnp.where(
        iota((tokens, width), 1).astype(F32) == target_col, 1.0, 0.0
    ).astype(BF16)
    lane_col = slot_col + (me * capacity).astype(F32)
    marks = jnp.where(iota((tokens, width), 1).astype(F32) == lane_col, local_col + 1.0, 0.0)

    def make_index(owner):
        line = jnp.sum(
            jnp.where(owner_col == owner.astype(F32), marks, 0.0), axis=0, keepdims=True
        )
        idx_send[owner] = jnp.broadcast_to(line, (8, width))

    each(0, owner_count, make_index)

    def idx_copy(peer):
        return to_table(
            idx_send.at[peer], idx_got.at[me], idx_ssem.at[peer], idx_rsem.at[me], peer
        )

    each(1, owner_count, lambda r: idx_copy(table_peer(r)).start())
    idx_got[me] = idx_send[me]

    for load in loads[5:6]:
        load.wait()
    x_all[pos] = x_ref[...]
    do_all[pos] = do_ref[...]
    own = dot(x_ref[...], proj_ref[...]).astype(BF16)
    own_ref[...] = own
    half_temper = jnp.asarray(0.5 * temper, BF16)
    scaled_ref[...] = own * half_temper
    scaled_do_ref[...] = do_ref[...] * half_temper

    lane = iota((1, LANES), 1)
    group = LANES // head_size
    span = group * tokens
    head_masks = [
        jnp.where(lane // head_size == g, 1.0, 0.0).astype(BF16) for g in range(group)
    ]

    def spread(block):
        return jnp.concatenate([block * m for m in head_masks], axis=0)

    def terms(half_scores, grad_dot, scale):
        slant = jnp.tanh(half_scores)
        gates = (1.0 + slant) * scale
        weights = (half_scores * gates).astype(BF16)
        score_grad = (grad_dot * (gates * (1.0 + half_scores * (1.0 - slant)))).astype(BF16)
        return weights, score_grad

    def put(ref, cols, value, first):
        if first:
            ref[:, cols] = value
        else:
            ref[:, cols] += value

    def over_columns(begin, end):
        held = begin(0)
        for c in range(features // LANES):
            after = begin(c + 1) if c + 1 < features // LANES else None
            end(c, *held)
            held = after

    def lanes_at(offset, c):
        return slice(offset + c * LANES, offset + (c + 1) * LANES)

    def query_pass(source, offset, scale, first):
        def begin(c):
            keys = spread(source[:, lanes_at(offset, c)])
            values = spread(source[:, lanes_at(offset + features, c)])
            cols = lanes_at(0, c)
            return keys, dot_nt(scaled_ref[:, cols], keys), dot_nt(scaled_do_ref[:, cols], values)

        def end(c, keys, half_scores, grad_dot):
            _, score_grad = terms(half_scores, grad_dot, scale)
            put(dq_ref, lanes_at(0, c), dot(score_grad, keys), first)

        over_columns(begin, end)

    def key_pass(source, block, scale, first):
        def begin(c):
            cols = lanes_at(0, c)
            queries = spread(source[:, cols])
            grads = spread(do_all[block, :, cols])
            return (
                queries,
                grads,
                dot_nt(scaled_ref[:, lanes_at(features, c)], queries),
                dot_nt(scaled_ref[:, lanes_at(2 * features, c)], grads),
            )

        def end(c, queries, grads, half_scores, grad_dot):
            weights, score_grad = terms(half_scores, grad_dot, scale)
            put(dk_ref, lanes_at(0, c), dot(score_grad, queries), first)
            put(dv_ref, lanes_at(0, c), dot(weights, grads), first)

        over_columns(begin, end)

    def visible(query_block, key_block):
        return jnp.where(mask_ref[query_block, key_block] == 1, history_scale, 0.0)

    def own_block(keys_too):
        row_ids = iota((tokens, span), 0)
        lane_ids = iota((tokens, span), 1) % tokens
        if not keys_too:
            query_pass(
                own_ref, features, jnp.where(lane_ids <= row_ids, history_scale, 0.0), True
            )
            return
        key_pass(own_ref, pos, jnp.where(row_ids <= lane_ids, history_scale, 0.0), True)

    def block_step(r):
        block = seq_peer(r)
        in_row, in_col = block // side == my_row, block % side == my_col

        @pl.when(jnp.logical_not(in_row | in_col))
        def _():
            x_relay(block, block).wait_recv()

        @pl.when(block < pos)
        def _():
            other_ref[...] = dot(x_all[block], proj_ref[:, features:]).astype(BF16)
            query_pass(other_ref, 0, visible(pos, block), False)

        @pl.when(block > pos)
        def _():
            other_ref[:, :features] = dot(x_all[block], proj_ref[:, :features]).astype(BF16)
            to_seq(
                do_all.at[block], do_all.at[block], do_send.at[block], do_recv.at[block], block
            ).wait_recv()
            key_pass(other_ref, block, visible(block, pos), False)

    own_block(False)

    def take_index(r):
        peer = table_peer(r)
        to_table(
            idx_got.at[peer], idx_got.at[peer], idx_ssem.at[peer], idx_rsem.at[peer], peer
        ).wait_recv()

    each(1, owner_count, take_index)
    idx_all[pos] = jnp.sum(idx_got[...], axis=0)

    def idxf_copy(peer):
        return to_seq(idx_all.at[pos], idx_all.at[pos], idxf_ssem.at[peer], idxf_rsem.at[pos], peer)

    each(1, seq_count, lambda r: idxf_copy(seq_peer(r)).start())

    each(1, side, relay_x)
    own_block(True)
    each(1, seq_count, block_step)

    stacked = jnp.concatenate(
        [dq_ref[...].astype(BF16), dk_ref[...].astype(BF16), dv_ref[...].astype(BF16)], axis=1
    )
    input_grad = dot_nt(stacked, proj_ref[...]).astype(BF16)
    send_buf[...] = dot(sendsel_ref[...], input_grad).astype(BF16)

    def row_copy(peer):
        return to_table(
            send_buf.at[rows_of(peer)], got.at[pos, rows_of(me)],
            row_ssem.at[peer], row_rsem.at[me], peer,
        )

    each(1, owner_count, lambda r: row_copy(table_peer(owner_count - r)).start())
    got[pos, rows_of(me)] = send_buf[rows_of(me)]

    def chunk(block, source, ssem, peer):
        part = got.at[block, rows_of(source)]
        return to_seq(part, part, ssem, fwd_rsem.at[block, source], peer)

    def forward(source):
        def one(i):
            chunk(pos, source, fwd_ssem.at[row_peer(i)], row_peer(i)).start()
            chunk(pos, source, fwd_ssem.at[col_peer(i)], col_peer(i)).start()

        each(1, side, one)

    near = owner_count // 2

    def each_diag(act):
        def one(r):
            peer = seq_peer(r)

            @pl.when(jnp.logical_not((peer // side == my_row) | (peer % side == my_col)))
            def _():
                act(peer)

        each(1, seq_count, one)

    def forward_far(source):
        forward(source)
        each_diag(lambda peer: chunk(pos, source, diag_ssem.at[peer], peer).start())

    def pass_chunk(source):
        def along(from_peer, to_peer):
            def one(i):
                block = from_peer(i)
                chunk(block, source, rel_ssem.at[block], block).wait_recv()
                each(
                    1, side,
                    lambda k: chunk(block, source, rel_ssem.at[block], to_peer(k)).start(),
                )

            each(1, side, one)

        @pl.when(source % 2 == 0)
        def _():
            along(row_peer, col_peer)

        @pl.when(source % 2 == 1)
        def _():
            along(col_peer, row_peer)

    forward(me)

    def take_chunk(r):
        source = table_peer(r)
        part = got.at[pos, rows_of(source)]
        to_table(part, part, row_ssem.at[source], row_rsem.at[source], source).wait_recv()
        return source

    def relay(r):
        forward(take_chunk(r))
        pass_chunk(table_peer(r - 1))

    each(1, near, relay)
    pass_chunk(table_peer(near - 1))

    slab_ids = iota((slab_rows, width), 0).astype(F32) + 1.0

    def select(block):
        select_ref[block] = jnp.where(
            slab_ids == idx_all[block][0:1, :], 1.0, 0.0
        ).astype(BF16)

    select(pos)
    slab_lanes = iota((LANES, slab_rows), 1).astype(F32) + 1.0
    for c in range(width // LANES):
        lanes = slice(c * LANES, (c + 1) * LANES)
        replysel_ref[lanes, :] = jnp.where(
            slab_lanes == to_col(idx_all[pos][0:1, lanes]), 1.0, 0.0
        ).astype(BF16)

    def select_other(r):
        block = seq_peer(r)
        to_seq(
            idx_all.at[block], idx_all.at[block], idxf_ssem.at[block], idxf_rsem.at[block], block
        ).wait_recv()
        select(block)

    each(1, seq_count, select_other)

    each(near, owner_count, lambda r: forward_far(take_chunk(r)))

    grad_ref[...] = dot(select_ref[pos], got[pos])

    def add_block(r):
        block = seq_peer(r)
        in_row, in_col = block // side == my_row, block % side == my_col

        def await_chunk(r):
            source = table_peer(r)
            passed = (in_row & (source % 2 == 0)) | (in_col & (source % 2 == 1))

            @pl.when(jnp.logical_not(passed & (r < near)))
            def _():
                chunk(block, source, rel_ssem.at[block], block).wait_recv()

        each(0, owner_count, await_chunk)
        grad_ref[...] += dot(select_ref[block], got[block])

    each(1, seq_count, add_block)

    for load in loads[6:]:
        load.wait()
    for c in range(slab_rows // LANES):
        rows = slice(c * LANES, (c + 1) * LANES)
        grad = grad_ref[rows, :]
        new_moment = first_decay * moment_ref[rows, :] + (1.0 - first_decay) * grad
        mean_square = jnp.sum(grad * grad, axis=1, keepdims=True) * (1.0 / features)
        new_second = second_decay * to_col(second_ref[c : c + 1, :]) + (
            1.0 - second_decay
        ) * mean_square
        nsec_ref[c : c + 1, :] = to_row(new_second)
        nmom_ref[rows, :] = new_moment
        factor = step_rate / (jnp.sqrt(new_second) + epsilon)
        ntab_ref[rows, :] = (table_ref[rows, :].astype(F32) - new_moment * factor).astype(BF16)

    reply_buf[...] = dot(replysel_ref[...], ntab_ref[...]).astype(BF16)

    def reply_copy(peer):
        return to_table(
            reply_buf.at[rows_of(peer)], returned.at[rows_of(me)],
            rep_ssem.at[peer], rep_rsem.at[me], peer,
        )

    each(1, owner_count, lambda r: reply_copy(table_peer(owner_count - r)).start())
    stores = [
        pltpu.make_async_copy(nmom_ref, nmom_hbm, store_sem.at[0]),
        pltpu.make_async_copy(ntab_ref, ntab_hbm, store_sem.at[1]),
        pltpu.make_async_copy(nsec_ref, nsec_hbm, store_sem.at[2]),
    ]
    for store in stores:
        store.start()
    returned[rows_of(me)] = reply_buf[rows_of(me)]

    each(1, seq_count, lambda r: idxf_copy(seq_peer(r)).wait_send())
    each_do(lambda copy: copy.wait_send())

    def end_seq(i):
        for peer in (row_peer(i), col_peer(i)):
            x_copy(peer).wait_send()
            to_seq(
                got.at[pos], got.at[pos], fwd_ssem.at[peer], fwd_rsem.at[pos, 0], peer
            ).wait_send()
            half = got.at[peer, pl.ds(0, width // 4)]
            for _ in range(side - 1):
                to_seq(
                    half, half, rel_ssem.at[peer], fwd_rsem.at[peer, 0], peer
                ).wait_send()

    each(1, side, end_seq)
    far = got.at[pos, pl.ds(0, width // 2)]
    each_diag(
        lambda peer: to_seq(
            far, far, diag_ssem.at[peer], fwd_rsem.at[pos, 0], peer
        ).wait_send()
    )
    each(1, side, end_relays)

    def end_table(r):
        peer = table_peer(r)
        idx_copy(peer).wait_send()
        row_copy(peer).wait_send()
        part = returned.at[rows_of(peer)]
        to_table(part, part, rep_ssem.at[peer], rep_rsem.at[peer], peer).wait_recv()

    each(1, owner_count, end_table)
    event_ref[...] = dot(recvsel_ref[...], returned[...]).astype(BF16)
    last = pltpu.make_async_copy(event_ref, event_hbm, store_sem.at[3])
    last.start()
    each(1, owner_count, lambda r: reply_copy(table_peer(r)).wait_send())
    for store in stores:
        store.wait()
    last.wait()


def pass_on(*refs):
    count = len(refs) // 3
    sources, targets, held = refs[:count], refs[count : 2 * count], refs[2 * count : 3 * count]
    in_sem, out_sem = refs[3 * count :]
    loads, stores = [], []
    for source, target, stage in zip(sources, targets, held):
        rows = source.shape[0]
        pieces = rows // LANES if rows > LANES else 1
        size = rows // pieces
        for piece in range(pieces):
            part = pl.ds(piece * size, size)
            number = len(loads)
            loads.append(
                pltpu.make_async_copy(source.at[part], stage.at[part], in_sem.at[number])
            )
            stores.append(
                pltpu.make_async_copy(stage.at[part], target.at[part], out_sem.at[number])
            )
    for load in loads:
        load.start()
    for load, store in zip(loads, stores):
        load.wait()
        store.start()
    for store in stores:
        store.wait()


def body(events_x, proj, out_grad, block_mask, item_ids, owner_of, local_of, table, moment, second):
    tokens, features = events_x.shape[1:]
    seq_count = lax.axis_size("seq")
    owner_count = lax.axis_size("table")
    slab_rows = table.shape[0]
    capacity = max(2 * tokens // owner_count, 16)
    width = owner_count * capacity
    smem = pl.BlockSpec(memory_space=pltpu.SMEM)
    hbm = pl.BlockSpec(memory_space=pl.ANY)
    dma = pltpu.SemaphoreType.DMA
    results = pl.pallas_call(
        functools.partial(kernel, seq_count, owner_count, capacity),
        out_shape=(
            jax.ShapeDtypeStruct((slab_rows, features), BF16),
            jax.ShapeDtypeStruct((slab_rows, features), F32),
            jax.ShapeDtypeStruct((slab_rows // LANES, LANES), F32),
            jax.ShapeDtypeStruct((tokens, features), BF16),
        ),
        in_specs=[hbm, hbm, hbm, smem] + [hbm] * 6,
        out_specs=(hbm,) * 4,
        scratch_shapes=[
            pltpu.VMEM((tokens, features), BF16),
            pltpu.VMEM((tokens, features), BF16),
            pltpu.VMEM((1, tokens), jnp.int32),
            pltpu.VMEM((owner_of.shape[0] // LANES, LANES), jnp.int32),
            pltpu.VMEM((owner_of.shape[0] // LANES, LANES), jnp.int32),
            pltpu.VMEM((slab_rows // LANES, LANES), F32),
            pltpu.VMEM((slab_rows // LANES, LANES), F32),
            pltpu.VMEM((tokens, features), BF16),
            pltpu.VMEM((width, features), BF16),
            pltpu.VMEM((tokens, width), BF16),
            pltpu.VMEM((seq_count, slab_rows, width), BF16),
            pltpu.VMEM((width, slab_rows), BF16),
            pltpu.VMEM((seq_count, tokens, features), BF16),
            pltpu.VMEM((seq_count, tokens, features), BF16),
            pltpu.VMEM(proj.shape, BF16),
            pltpu.VMEM((slab_rows, features), BF16),
            pltpu.VMEM((slab_rows, features), F32),
            pltpu.VMEM((slab_rows, features), BF16),
            pltpu.VMEM((slab_rows, features), F32),
            pltpu.VMEM((tokens, 3 * features), BF16),
            pltpu.VMEM((tokens, 3 * features), BF16),
            pltpu.VMEM((tokens, features), BF16),
            pltpu.VMEM((tokens, 2 * features), BF16),
            pltpu.VMEM((tokens, features), F32),
            pltpu.VMEM((tokens, features), F32),
            pltpu.VMEM((tokens, features), F32),
            pltpu.VMEM((width, tokens), BF16),
            pltpu.VMEM((owner_count, 8, width), F32),
            pltpu.VMEM((owner_count, 8, width), F32),
            pltpu.VMEM((seq_count, 8, width), F32),
            pltpu.VMEM((width, features), BF16),
            pltpu.VMEM((seq_count, width, features), BF16),
            pltpu.VMEM((slab_rows, features), F32),
            pltpu.VMEM((width, features), BF16),
            dma((9,)),
            dma((4,)),
            dma((seq_count,)),
            dma((seq_count,)),
            dma((seq_count,)),
            dma((seq_count,)),
            dma((owner_count,)),
            dma((owner_count,)),
            dma((seq_count,)),
            dma((seq_count,)),
            dma((owner_count,)),
            dma((owner_count,)),
            dma((seq_count,)),
            dma((seq_count, owner_count)),
            dma((owner_count,)),
            dma((owner_count,)),
            dma((seq_count,)),
            dma((seq_count,)),
            dma((seq_count,)),
        ],
        compiler_params=pltpu.CompilerParams(
            collective_id=0, has_side_effects=True, vmem_limit_bytes=VMEM_BYTES
        ),
    )(
        events_x[0],
        proj,
        out_grad[0],
        block_mask,
        item_ids,
        owner_of.reshape(-1, LANES),
        local_of.reshape(-1, LANES),
        table,
        moment,
        second.reshape(-1, LANES),
    )
    new_table, new_moment, new_second, event_rows = pl.pallas_call(
        pass_on,
        out_shape=tuple(jax.ShapeDtypeStruct(r.shape, r.dtype) for r in results),
        in_specs=[hbm] * 4,
        out_specs=(hbm,) * 4,
        scratch_shapes=[pltpu.VMEM(r.shape, r.dtype) for r in results]
        + [dma((2 * (slab_rows // LANES) + 2,))] * 2,
        compiler_params=pltpu.CompilerParams(vmem_limit_bytes=VMEM_BYTES),
    )(*results)
    return (new_table, new_moment, new_second.reshape(-1), event_rows[None])


def solution(mesh):
    return jax.shard_map(
        body,
        mesh=mesh,
        in_specs=(
            P("table", "seq", None),
            P(),
            P("table", "seq", None),
            P(),
            P("table", "seq"),
            P(),
            P(),
            P("table", None),
            P("table", None),
            P("table"),
        ),
        out_specs=(P("table", None), P("table", None), P("table"), P("table", "seq", None)),
        check_vma=False,
    )
```
